512 devices in a mesh: pipe: 8 (over y, core), tp: 64 (over x, z).
Axes of the slice: x: 4, y: 4, z: 16, core: 2. Of those that a mesh axis runs over, the one named last changes fastest.
Arguments:
- in_flight: bfloat16 [8, 128, 3072], P('pipe', 'tp'), may hold values from -6 to 6
- w_qkv: bfloat16 [8, 3, 3072, 3072], P('pipe', None, 'tp'), may hold values from -0.109375 to 0.109375
- w_mlp: bfloat16 [8, 12288, 3072], P('pipe', 'tp'), may hold values from -0.109375 to 0.109375
- w_attn_out: bfloat16 [8, 3072, 3072], P('pipe', 'tp'), may hold values from -0.109375 to 0.109375
- w_mlp_out: bfloat16 [8, 12288, 3072], P('pipe', 'tp'), may hold values from -0.0546875 to 0.0546875
- modulation: float32 [8, 3, 3072], P('pipe'), may hold values from -3 to 3
- qk_gain: float32 [8, 2, 128], P('pipe'), may hold values from 0.25 to 1.75
- context_kv: bfloat16 [8, 2, 1536, 3072], P('pipe', None, 'tp'), may hold values from -8 to 8
- text_len: int32 [1], replicated, may hold values from 1 to 512
Outputs:
- leaving: bfloat16 [8, 128, 3072], P('pipe', 'tp')
The draws below stay inside these ranges and needn't reach their ends.
All inputs are finite; a program needn't handle non-finite values.
Results may differ from the reference program's by a relative error of at most 0.017.
Values may be sent and summed in bfloat16 or wider, within the bound.
No kernel may reach another device: no remote copies, remote signals or barrier semaphores. Data moves between devices by JAX's collectives and lax.ppermute only.
A program may use at most 64 MiB of HBM per device.

```python
import jax
import jax.numpy as jnp
from jax import lax

D = 3072
HEADS = 24
HEAD_DIM = 128
FF = 12288
PATCH = 128
TICKS = 2
SEGMENTS = 8
CTX = 1536
TXT = 512


def level_of(rng, extent, pieces, low, top_value):
    def one(dim, shards_of):
        heights = jax.random.uniform(jax.random.fold_in(jax.random.fold_in(rng, 6), dim), (shards_of,), jnp.float32, low / len(pieces), top_value / len(pieces))
        return jnp.repeat(jnp.exp(heights), extent[dim] // shards_of).reshape((-1,) + (1,) * (len(extent) - dim - 1))

    gain = one(*pieces[0])
    for cut in pieces[1:]:
        gain = gain * one(*cut)
    return gain


def scatter_about(key, shape, spread, reach, split=(), kind=jnp.bfloat16):
    level = level_of(key, shape, split, -0.22, 0.18) if split else 1.0
    result = jax.random.normal(key, shape, jnp.float32) * spread * level
    return jnp.minimum(jnp.maximum(result, -reach), reach).astype(kind)


def setup_inputs(seed: int = 0) -> dict:
    seeds = jax.random.split(jax.random.key(seed), 10)
    in_flight = scatter_about(seeds[0], (SEGMENTS, PATCH, D), 1.0, 6.0, ((0, 8), (1, 64)))
    w_qkv = scatter_about(seeds[1], (SEGMENTS, 3, D, D), D ** -0.5, 0.109375, ((0, 8), (2, 64)))
    w_mlp = scatter_about(seeds[2], (SEGMENTS, FF, D), D ** -0.5, 0.109375, ((0, 8), (1, 64)))
    w_attn_out = scatter_about(seeds[3], (SEGMENTS, D, D), D ** -0.5, 0.109375, ((0, 8), (1, 64)))
    w_mlp_out = scatter_about(seeds[4], (SEGMENTS, FF, D), FF ** -0.5, 0.0546875, ((0, 8), (1, 64)))
    modulation = scatter_about(seeds[5], (SEGMENTS, 3, D), 0.5, 3.0, ((0, 8),), jnp.float32)
    qk_gain = jnp.clip(1.0 + 0.15 * jax.random.normal(seeds[6], (SEGMENTS, 2, HEAD_DIM), jnp.float32), 0.25, 1.75)
    context_kv = scatter_about(seeds[7], (SEGMENTS, 2, CTX, D), 2.0, 8.0, ((0, 8), (2, 64)))
    text_len = jax.random.randint(seeds[8], (1,), 1, TXT + 1).astype(jnp.int32)
    return {"in_flight": in_flight, "w_qkv": w_qkv, "w_mlp": w_mlp, "w_attn_out": w_attn_out, "w_mlp_out": w_mlp_out, "modulation": modulation, "qk_gain": qk_gain, "context_kv": context_kv, "text_len": text_len}


eps_norm = 1e-06

def modulated(hidden_state, shift_scale):
    x_float = hidden_state.astype(jnp.float32)
    row_mean = lax.optimization_barrier(jnp.mean(x_float, axis=-1, keepdims=True))
    row_var = lax.optimization_barrier(jnp.mean(jnp.square(x_float - row_mean), axis=-1, keepdims=True))
    normed = (x_float - row_mean) * lax.rsqrt(row_var + eps_norm)
    return (normed * (1.0 + shift_scale[1]) + shift_scale[0]).astype(jnp.bfloat16)

def head_norm(values_in, gain_vector):
    mean_square = lax.optimization_barrier(jnp.mean(values_in * values_in, axis=-1, keepdims=True))
    return values_in * lax.rsqrt(mean_square + eps_norm) * gain_vector

def block(hidden_state, weight_qkv, weight_mlp, weight_attn, weight_down, shift_scale, gains, cached_keys, cached_values, key_mask):
    patch_len = hidden_state.shape[0]
    normed = modulated(hidden_state, shift_scale)
    projected = jnp.dot(normed, weight_qkv.reshape(3 * D, D).T, preferred_element_type=jnp.float32)
    projected = projected.astype(jnp.bfloat16).reshape(patch_len, 3, HEADS, HEAD_DIM)
    queries = (head_norm(projected[:, 0].astype(jnp.float32), gains[0]) * HEAD_DIM ** (-0.5)).astype(jnp.bfloat16)
    fresh_keys = head_norm(projected[:, 1].astype(jnp.float32), gains[1]).astype(jnp.bfloat16)
    all_keys = jnp.concatenate([cached_keys.reshape(-1, HEADS, HEAD_DIM), fresh_keys], axis=0)
    all_values = jnp.concatenate([cached_values.reshape(-1, HEADS, HEAD_DIM), projected[:, 2]], axis=0)
    full_mask = jnp.concatenate([key_mask, jnp.ones((patch_len,), dtype=bool)])
    scores = jnp.einsum('qhd,khd->qhk', queries.astype(jnp.float32), all_keys.astype(jnp.float32), precision=lax.Precision.HIGHEST)
    scores = jnp.where(full_mask[None, None, :], scores, -1e+30)
    probs = jnp.exp(scores)
    totals = lax.optimization_barrier(jnp.sum(probs, axis=-1))
    probs_low = lax.optimization_barrier(probs.astype(jnp.bfloat16)).astype(jnp.float32)
    weighted = jnp.einsum('qhk,khd->qhd', probs_low, all_values.astype(jnp.float32), precision=lax.Precision.HIGHEST)
    attention = (weighted / totals[..., None]).reshape(patch_len, D).astype(jnp.bfloat16)
    hidden = jax.nn.gelu(jnp.dot(normed, weight_mlp.T, preferred_element_type=jnp.float32), approximate=True).astype(jnp.bfloat16)
    branch = jnp.dot(attention, weight_attn, preferred_element_type=jnp.float32) + jnp.dot(hidden, weight_down, preferred_element_type=jnp.float32)
    return (hidden_state.astype(jnp.float32) + shift_scale[2] * branch).astype(jnp.bfloat16)

def reference(in_flight, w_qkv, w_mlp, w_attn_out, w_mlp_out, modulation, qk_gain, context_kv, text_len):
    positions = jnp.arange(CTX, dtype=jnp.int32)
    key_mask = (positions >= TXT) | (positions < text_len[0])
    results = [None] * SEGMENTS
    for anchor in range(SEGMENTS):
        hidden_state = in_flight[anchor]
        for tick_number in range(TICKS):
            segment = (anchor + tick_number) % SEGMENTS
            hidden_state = block(hidden_state, w_qkv[segment], w_mlp[segment], w_attn_out[segment], w_mlp_out[segment], modulation[segment], qk_gain[segment], context_kv[segment, 0], context_kv[segment, 1], key_mask)
        results[(anchor + TICKS) % SEGMENTS] = hidden_state
    return jnp.stack(results)
```

```python
import jax
import jax.numpy as jnp
from jax import lax
from jax.sharding import PartitionSpec as P

HEADS = 24
HEAD_DIM = 128
TICKS = 2
TXT = 512
TEAM = 8
TEAM_HEADS = 3

eps_norm = 1e-06
f32 = jnp.float32
bf16 = jnp.bfloat16


def shifted(block, axis, distance):
    size = lax.axis_size(axis)
    return lax.ppermute(block, axis, [((i - distance) % size, i) for i in range(size)])


def modulated(hidden_state, shift_scale):
    x_float = hidden_state.astype(f32)
    row_mean = jnp.mean(x_float, axis=-1, keepdims=True)
    row_var = jnp.mean(jnp.square(x_float - row_mean), axis=-1, keepdims=True)
    normed = (x_float - row_mean) * lax.rsqrt(row_var + eps_norm)
    return (normed * (1.0 + shift_scale[1]) + shift_scale[0]).astype(bf16)


def head_norm(values_in, gain_vector):
    mean_square = jnp.mean(values_in * values_in, axis=-2, keepdims=True)
    return values_in * lax.rsqrt(mean_square + eps_norm) * gain_vector[:, None]


def local(
    in_flight, w_qkv, w_mlp, w_attn_out, w_mlp_out, modulation, qk_gain, context_kv, text_len
):
    tp_count = lax.axis_size("tp")
    tp_index = lax.axis_index("tp")
    rows = in_flight.shape[1]
    tokens = rows * tp_count
    width = w_attn_out.shape[2]
    shard = w_attn_out.shape[1]
    ctx_local = context_kv.shape[2]
    teams = tp_count // TEAM
    team_width = TEAM * shard
    member = tp_index % TEAM
    inside = [[TEAM * t + m for m in range(TEAM)] for t in range(teams)]
    across = [[TEAM * t + m for t in range(teams)] for m in range(TEAM)]
    shift_scale = modulation[0]
    gains = qk_gain[0]
    weight_qkv = w_qkv[0].reshape(3 * shard, width)
    weight_mlp = w_mlp[0]
    weight_attn = w_attn_out[0]
    weight_down = w_mlp_out[0]

    cached = context_kv[0].reshape(2, ctx_local, teams, team_width).transpose(2, 0, 1, 3)
    cached = lax.all_to_all(cached, "tp", 0, 0, axis_index_groups=across)
    cached = cached.transpose(1, 0, 2, 3).reshape(2, teams * ctx_local, TEAM_HEADS, HEAD_DIM)
    cached_keys, cached_values = cached[0], cached[1]
    slot = jnp.arange(teams * ctx_local, dtype=jnp.int32)
    position = ctx_local * (TEAM * (slot // ctx_local) + member) + slot % ctx_local
    cached_mask = (position >= TXT) | (position < text_len[0])
    token = jnp.arange(tokens, dtype=jnp.int32)
    fresh_mask = token // (tokens // TEAM) == member

    current = in_flight[0]
    for tick_number in range(TICKS):
        normed_rows = modulated(current, shift_scale)
        spread = jnp.broadcast_to(normed_rows[None], (tp_count, rows, width))
        normed = lax.all_to_all(spread, "tp", 0, 0).reshape(tokens, width)
        own = lax.dot_general(
            weight_qkv, normed, (((1,), (1,)), ((), ())), preferred_element_type=f32
        ).astype(bf16)
        team = lax.all_gather(own.reshape(3, shard, tokens), "tp", axis=1, tiled=True, axis_index_groups=inside)
        team = team.reshape(3, TEAM_HEADS, HEAD_DIM, tokens)
        queries = (head_norm(team[0].astype(f32), gains[0]) * HEAD_DIM ** (-0.5)).astype(bf16)
        fresh_keys = head_norm(team[1].astype(f32), gains[1]).astype(bf16)
        fresh_values = team[2]
        cached_scores = jnp.einsum("khd,hdq->hkq", cached_keys, queries, preferred_element_type=f32)
        fresh_scores = jnp.einsum("hdk,hdq->hkq", fresh_keys, queries, preferred_element_type=f32)
        cached_probs = jnp.exp(jnp.where(cached_mask[None, :, None], cached_scores, -1e30))
        fresh_probs = jnp.exp(jnp.where(fresh_mask[None, :, None], fresh_scores, -1e30))
        totals = jnp.sum(cached_probs, axis=1) + jnp.sum(fresh_probs, axis=1)
        weighted = jnp.einsum(
            "khd,hkq->hdq", cached_values, cached_probs.astype(bf16), preferred_element_type=f32
        ) + jnp.einsum(
            "hdk,hkq->hdq", fresh_values, fresh_probs.astype(bf16), preferred_element_type=f32
        )
        parts = weighted.astype(bf16).reshape(TEAM, shard, tokens)
        spread_totals = jnp.broadcast_to(totals.astype(bf16)[None], (TEAM, TEAM_HEADS, tokens))
        parts = jnp.concatenate(
            [parts, spread_totals, jnp.zeros((TEAM, 16 - TEAM_HEADS, tokens), bf16)], axis=1
        )
        parts = lax.all_to_all(parts, "tp", 0, 0, axis_index_groups=inside)
        summed = jnp.sum(parts.astype(f32), axis=0)
        feature_head = (member * shard + jnp.arange(shard, dtype=jnp.int32)) // HEAD_DIM
        total_rows = summed[shard + TEAM_HEADS - 1][None]
        for h in range(TEAM_HEADS - 1):
            total_rows = jnp.where(feature_head[:, None] == h, summed[shard + h][None], total_rows)
        attention = (summed[:shard] / total_rows).astype(bf16)
        hidden = jax.nn.gelu(
            lax.dot_general(
                normed, weight_mlp, (((1,), (1,)), ((), ())), preferred_element_type=f32
            ),
            approximate=True,
        ).astype(bf16)
        branch = lax.dot_general(
            attention, weight_attn, (((0,), (0,)), ((), ())), preferred_element_type=f32
        ) + jnp.dot(hidden, weight_down, preferred_element_type=f32)
        branch = (branch * shift_scale[2]).astype(bf16).reshape(tp_count, rows, width)
        branch = lax.all_to_all(branch, "tp", 0, 0)
        finished = (current.astype(f32) + jnp.sum(branch.astype(f32), axis=0)).astype(bf16)
        current = shifted(finished, "pipe", 1)
    return current[None]


def solution(mesh):
    placed = (
        P("pipe", "tp", None),
        P("pipe", None, "tp", None),
        P("pipe", "tp", None),
        P("pipe", "tp", None),
        P("pipe", "tp", None),
        P("pipe", None, None),
        P("pipe", None, None),
        P("pipe", None, "tp", None),
        P(),
    )
    return jax.shard_map(
        local, mesh=mesh, in_specs=placed, out_specs=P("pipe", "tp", None), check_vma=False
    )
```

```python
import jax
import jax.numpy as jnp
from jax import lax
from jax.sharding import PartitionSpec as P

HEADS = 24
HEAD_DIM = 128
TICKS = 2
TXT = 512
TEAM = 8
TEAM_HEADS = 3

eps_norm = 1e-06
f32 = jnp.float32
bf16 = jnp.bfloat16


def shifted(block, axis, distance):
    size = lax.axis_size(axis)
    return lax.ppermute(block, axis, [((i - distance) % size, i) for i in range(size)])


def modulated(hidden_state, shift_scale):
    x_float = hidden_state.astype(f32)
    row_mean = jnp.mean(x_float, axis=-1, keepdims=True)
    row_var = jnp.mean(jnp.square(x_float - row_mean), axis=-1, keepdims=True)
    normed = (x_float - row_mean) * lax.rsqrt(row_var + eps_norm)
    return (normed * (1.0 + shift_scale[1]) + shift_scale[0]).astype(bf16)


def head_norm(values_in, gain_vector):
    mean_square = jnp.mean(values_in * values_in, axis=-2, keepdims=True)
    return values_in * lax.rsqrt(mean_square + eps_norm) * gain_vector[:, None]


def gathered(block, groups):
    size = len(groups[0])
    spread = jnp.broadcast_to(block[None], (size,) + block.shape)
    spread = lax.all_to_all(spread, "tp", 0, 0, axis_index_groups=groups)
    return spread.reshape((size * block.shape[0],) + block.shape[1:])


def summed_over(block, groups):
    size = len(groups[0])
    parts = block.astype(bf16).reshape((size, block.shape[0] // size) + block.shape[1:])
    parts = lax.all_to_all(parts, "tp", 0, 0, axis_index_groups=groups)
    return jnp.sum(parts.astype(f32), axis=0)


def local(
    in_flight, w_qkv, w_mlp, w_attn_out, w_mlp_out, modulation, qk_gain, context_kv, text_len
):
    tp_count = lax.axis_size("tp")
    tp_index = lax.axis_index("tp")
    rows = in_flight.shape[1]
    tokens = rows * tp_count
    width = w_attn_out.shape[2]
    shard = w_attn_out.shape[1]
    ctx_local = context_kv.shape[2]
    teams = tp_count // TEAM
    team_width = TEAM * shard
    member = tp_index % TEAM
    z_count, x_count = 2 * TEAM, tp_count // (2 * TEAM)
    along_z = [[z_count * x + z for z in range(z_count)] for x in range(x_count)]
    along_x = [[z_count * x + z for x in range(x_count)] for z in range(z_count)]
    inside = [[TEAM * t + m for m in range(TEAM)] for t in range(teams)]
    offset = [TEAM + TEAM // 2 if m < TEAM // 2 else TEAM // 2 for m in range(TEAM)]
    across = [
        [z_count * x + m + half * offset[m] for x in range(x_count) for half in range(2)]
        for m in range(TEAM)
    ]
    shift_scale = modulation[0]
    gains = qk_gain[0]
    weight_qkv = w_qkv[0].reshape(3 * shard, width)
    weight_mlp = w_mlp[0]
    weight_attn = w_attn_out[0]
    weight_down = w_mlp_out[0]

    cached = context_kv[0].reshape(2, ctx_local, teams, team_width).transpose(2, 0, 1, 3)
    cached = lax.all_to_all(cached, "tp", 0, 0, axis_index_groups=across)
    cached = cached.transpose(1, 0, 2, 3).reshape(2, teams * ctx_local, TEAM_HEADS, HEAD_DIM)
    cached_keys, cached_values = cached[0], cached[1]
    z_here = tp_index % z_count
    low = jnp.where(
        z_here < TEAM, z_here, (z_here - TEAM + TEAM // 2) % TEAM
    )
    high = low + jnp.where(low < TEAM // 2, TEAM + TEAM // 2, TEAM // 2)
    slot = jnp.arange(teams * ctx_local, dtype=jnp.int32)
    source = slot // ctx_local
    source = z_count * (source // 2) + jnp.where(source % 2 == 0, low, high)
    position = ctx_local * source + slot % ctx_local
    cached_mask = (position >= TXT) | (position < text_len[0])
    token = jnp.arange(tokens, dtype=jnp.int32)
    fresh_mask = token // (tokens // TEAM) == member

    current = in_flight[0]
    for tick_number in range(TICKS):
        normed_rows = modulated(current, shift_scale)
        normed = gathered(gathered(normed_rows, along_z), along_x)
        own = lax.dot_general(
            weight_qkv, normed, (((1,), (1,)), ((), ())), preferred_element_type=f32
        ).astype(bf16)
        team = gathered(own, inside).reshape(TEAM, 3, shard, tokens).transpose(1, 0, 2, 3)
        team = team.reshape(3, TEAM_HEADS, HEAD_DIM, tokens)
        queries = (head_norm(team[0].astype(f32), gains[0]) * HEAD_DIM ** (-0.5)).astype(bf16)
        fresh_keys = head_norm(team[1].astype(f32), gains[1]).astype(bf16)
        fresh_values = team[2]
        cached_scores = jnp.einsum("khd,hdq->hkq", cached_keys, queries, preferred_element_type=f32)
        fresh_scores = jnp.einsum("hdk,hdq->hkq", fresh_keys, queries, preferred_element_type=f32)
        cached_probs = jnp.exp(jnp.where(cached_mask[None, :, None], cached_scores, -1e30))
        fresh_probs = jnp.exp(jnp.where(fresh_mask[None, :, None], fresh_scores, -1e30))
        totals = jnp.sum(cached_probs, axis=1) + jnp.sum(fresh_probs, axis=1)
        weighted = jnp.einsum(
            "khd,hkq->hdq", cached_values, cached_probs.astype(bf16), preferred_element_type=f32
        ) + jnp.einsum(
            "hdk,hkq->hdq", fresh_values, fresh_probs.astype(bf16), preferred_element_type=f32
        )
        parts = weighted.astype(bf16).reshape(TEAM, shard, tokens)
        spread_totals = jnp.broadcast_to(totals.astype(bf16)[None], (TEAM, TEAM_HEADS, tokens))
        parts = jnp.concatenate(
            [parts, spread_totals, jnp.zeros((TEAM, 16 - TEAM_HEADS, tokens), bf16)], axis=1
        )
        parts = lax.all_to_all(parts, "tp", 0, 0, axis_index_groups=inside)
        summed = jnp.sum(parts.astype(f32), axis=0)
        feature_head = (member * shard + jnp.arange(shard, dtype=jnp.int32)) // HEAD_DIM
        total_rows = summed[shard + TEAM_HEADS - 1][None]
        for h in range(TEAM_HEADS - 1):
            total_rows = jnp.where(feature_head[:, None] == h, summed[shard + h][None], total_rows)
        attention = (summed[:shard] / total_rows).astype(bf16)
        hidden = jax.nn.gelu(
            lax.dot_general(
                normed, weight_mlp, (((1,), (1,)), ((), ())), preferred_element_type=f32
            ),
            approximate=True,
        ).astype(bf16)
        branch = lax.dot_general(
            attention, weight_attn, (((0,), (0,)), ((), ())), preferred_element_type=f32
        ) + jnp.dot(hidden, weight_down, preferred_element_type=f32)
        branch = summed_over(branch * shift_scale[2], along_x)
        branch = summed_over(branch, along_z)
        finished = (current.astype(f32) + branch).astype(bf16)
        current = shifted(finished, "pipe", 1)
    return current[None]


def solution(mesh):
    placed = (
        P("pipe", "tp", None),
        P("pipe", None, "tp", None),
        P("pipe", "tp", None),
        P("pipe", "tp", None),
        P("pipe", "tp", None),
        P("pipe", None, None),
        P("pipe", None, None),
        P("pipe", None, "tp", None),
        P(),
    )
    return jax.shard_map(
        local, mesh=mesh, in_specs=placed, out_specs=P("pipe", "tp", None), check_vma=False
    )
```

```python
import jax
import jax.numpy as jnp
from jax import lax
from jax.sharding import PartitionSpec as P

HEADS = 24
HEAD_DIM = 128
TICKS = 2
TXT = 512
TEAM = 8
TEAM_HEADS = 3
LANES = 128

eps_norm = 1e-06
f32 = jnp.float32
bf16 = jnp.bfloat16


def shifted(block, axis, distance):
    size = lax.axis_size(axis)
    return lax.ppermute(block, axis, [((i - distance) % size, i) for i in range(size)])


def modulated(hidden_state, shift_scale):
    x_float = hidden_state.astype(f32)
    row_mean = jnp.mean(x_float, axis=-1, keepdims=True)
    row_var = jnp.mean(jnp.square(x_float - row_mean), axis=-1, keepdims=True)
    normed = (x_float - row_mean) * lax.rsqrt(row_var + eps_norm)
    return (normed * (1.0 + shift_scale[1]) + shift_scale[0]).astype(bf16)


def head_norm(values_in, gain_vector):
    mean_square = jnp.mean(values_in * values_in, axis=-2, keepdims=True)
    return values_in * lax.rsqrt(mean_square + eps_norm) * gain_vector[:, None]


def gathered(block, groups):
    size = len(groups[0])
    spread = jnp.broadcast_to(block[None], (size,) + block.shape)
    spread = lax.all_to_all(spread, "tp", 0, 0, axis_index_groups=groups)
    return spread.reshape((size * block.shape[0],) + block.shape[1:])


def summed_over(block, groups):
    size = len(groups[0])
    parts = block.astype(bf16).reshape((size, block.shape[0] // size) + block.shape[1:])
    parts = lax.all_to_all(parts, "tp", 0, 0, axis_index_groups=groups)
    return jnp.sum(parts.astype(f32), axis=0)


def local(
    in_flight, w_qkv, w_mlp, w_attn_out, w_mlp_out, modulation, qk_gain, context_kv, text_len
):
    tp_count = lax.axis_size("tp")
    tp_index = lax.axis_index("tp")
    rows = in_flight.shape[1]
    tokens = rows * tp_count
    width = w_attn_out.shape[2]
    shard = w_attn_out.shape[1]
    ctx_local = context_kv.shape[2]
    teams = tp_count // TEAM
    team_width = TEAM * shard
    member = tp_index % TEAM
    z_count, x_count = 2 * TEAM, tp_count // (2 * TEAM)
    along_z = [[z_count * x + z for z in range(z_count)] for x in range(x_count)]
    along_x = [[z_count * x + z for x in range(x_count)] for z in range(z_count)]
    inside = [[TEAM * t + m for m in range(TEAM)] for t in range(teams)]
    shift_scale = modulation[0]
    gains = qk_gain[0]
    weight_qkv = w_qkv[0].reshape(3 * shard, width)
    weight_mlp = w_mlp[0]
    weight_attn = w_attn_out[0]
    weight_down = w_mlp_out[0]

    half_team = TEAM // 2
    partner = [
        z + TEAM + half_team if z < half_team else z + half_team if z < TEAM
        else z - half_team if z < TEAM + half_team else z - TEAM - half_team
        for z in range(z_count)
    ]
    z_here = tp_index % z_count
    z_partner = jnp.where(
        z_here < TEAM,
        z_here + jnp.where(z_here < half_team, TEAM + half_team, half_team),
        z_here - jnp.where(z_here < TEAM + half_team, half_team, TEAM + half_team),
    )
    by_half = context_kv[0].reshape(2, ctx_local, x_count, 2, team_width)
    upper = z_here >= TEAM
    keep = jnp.where(upper, by_half[:, :, :, 1], by_half[:, :, :, 0])
    give = jnp.where(upper, by_half[:, :, :, 0], by_half[:, :, :, 1])
    got = lax.ppermute(
        give, "tp", [(z_count * x + z, z_count * x + partner[z]) for x in range(x_count) for z in range(z_count)]
    )
    cached = jnp.concatenate([keep, got], axis=1).transpose(2, 1, 0, 3)
    cached = cached.reshape(x_count, 2 * ctx_local, 2 * team_width)
    slot = jnp.arange(teams * ctx_local, dtype=jnp.int32)
    within = slot % (2 * ctx_local)
    source = z_count * (slot // (2 * ctx_local)) + jnp.where(within < ctx_local, z_here, z_partner)
    position = ctx_local * source + within % ctx_local
    cached_mask = (position >= TXT) | (position < text_len[0])
    token = jnp.arange(tokens, dtype=jnp.int32)
    fresh_mask = token // (tokens // TEAM) == member

    current = in_flight[0]
    for tick_number in range(TICKS):
        normed_rows = modulated(current, shift_scale)
        normed = gathered(normed_rows.reshape(rows * width // LANES, LANES), along_z)
        normed = normed.reshape(rows * z_count, width)
        if tick_number == 0:
            wide = 2 * team_width
            split = width // wide
            normed = normed.reshape(-1, split, wide).transpose(1, 0, 2).reshape(-1, wide)
            both = jnp.concatenate(
                [jnp.broadcast_to(normed[None], (x_count,) + normed.shape), cached], axis=1
            )
            both = lax.all_to_all(both, "tp", 0, 0, axis_index_groups=along_x)
            normed = both[:, : normed.shape[0]].reshape(x_count, split, -1, wide)
            normed = normed.transpose(0, 2, 1, 3).reshape(tokens, width)
            cached = both[:, split * rows * z_count :].reshape(-1, 2, TEAM_HEADS, HEAD_DIM)
            cached_keys, cached_values = cached[:, 0], cached[:, 1]
        else:
            normed = gathered(normed, along_x)
        own = lax.dot_general(
            weight_qkv, normed, (((1,), (1,)), ((), ())), preferred_element_type=f32
        ).astype(bf16)
        team = gathered(own, inside).reshape(TEAM, 3, shard, tokens).transpose(1, 0, 2, 3)
        team = team.reshape(3, TEAM_HEADS, HEAD_DIM, tokens)
        queries = (head_norm(team[0].astype(f32), gains[0]) * HEAD_DIM ** (-0.5)).astype(bf16)
        fresh_keys = head_norm(team[1].astype(f32), gains[1]).astype(bf16)
        fresh_values = team[2]
        cached_scores = jnp.einsum("khd,hdq->hkq", cached_keys, queries, preferred_element_type=f32)
        fresh_scores = jnp.einsum("hdk,hdq->hkq", fresh_keys, queries, preferred_element_type=f32)
        cached_probs = jnp.exp(jnp.where(cached_mask[None, :, None], cached_scores, -1e30))
        fresh_probs = jnp.exp(jnp.where(fresh_mask[None, :, None], fresh_scores, -1e30))
        totals = jnp.sum(cached_probs, axis=1) + jnp.sum(fresh_probs, axis=1)
        weighted = jnp.einsum(
            "khd,hkq->hdq", cached_values, cached_probs.astype(bf16), preferred_element_type=f32
        ) + jnp.einsum(
            "hdk,hkq->hdq", fresh_values, fresh_probs.astype(bf16), preferred_element_type=f32
        )
        parts = weighted.astype(bf16).reshape(TEAM, shard, tokens)
        spread_totals = jnp.broadcast_to(totals.astype(bf16)[None], (TEAM, TEAM_HEADS, tokens))
        parts = jnp.concatenate(
            [parts, spread_totals, jnp.zeros((TEAM, 16 - TEAM_HEADS, tokens), bf16)], axis=1
        )
        parts = lax.all_to_all(parts, "tp", 0, 0, axis_index_groups=inside)
        summed = jnp.sum(parts.astype(f32), axis=0)
        feature_head = (member * shard + jnp.arange(shard, dtype=jnp.int32)) // HEAD_DIM
        total_rows = summed[shard + TEAM_HEADS - 1][None]
        for h in range(TEAM_HEADS - 1):
            total_rows = jnp.where(feature_head[:, None] == h, summed[shard + h][None], total_rows)
        attention = (summed[:shard] / total_rows).astype(bf16)
        hidden = jax.nn.gelu(
            lax.dot_general(
                normed, weight_mlp, (((1,), (1,)), ((), ())), preferred_element_type=f32
            ),
            approximate=True,
        ).astype(bf16)
        hidden = lax.optimization_barrier(hidden)
        branch = lax.dot_general(
            attention, weight_attn, (((0,), (0,)), ((), ())), preferred_element_type=f32
        ) + jnp.dot(hidden, weight_down, preferred_element_type=f32)
        branch = summed_over(branch * shift_scale[2], along_x)
        branch = summed_over(branch.reshape(-1, LANES), along_z).reshape(rows, width)
        finished = (current.astype(f32) + branch).astype(bf16)
        current = shifted(finished, "pipe", 1)
    return current[None]


def solution(mesh):
    placed = (
        P("pipe", "tp", None),
        P("pipe", None, "tp", None),
        P("pipe", "tp", None),
        P("pipe", "tp", None),
        P("pipe", "tp", None),
        P("pipe", None, None),
        P("pipe", None, None),
        P("pipe", None, "tp", None),
        P(),
    )
    return jax.shard_map(
        local, mesh=mesh, in_specs=placed, out_specs=P("pipe", "tp", None), check_vma=False
    )
```

```python
import jax
import jax.numpy as jnp
from jax import lax
from jax.experimental import pallas as pl
from jax.experimental.pallas import tpu as pltpu
from jax.sharding import PartitionSpec as P

HEADS = 24
HEAD_DIM = 128
TICKS = 2
TXT = 512
TEAM = 8
TEAM_HEADS = 3
LANES = 128

eps_norm = 1e-06
f32 = jnp.float32
bf16 = jnp.bfloat16


def shifted(block, axis, distance):
    size = lax.axis_size(axis)
    return lax.ppermute(block, axis, [((i - distance) % size, i) for i in range(size)])


def modulated(hidden_state, shift_scale):
    x_float = hidden_state.astype(f32)
    row_mean = jnp.mean(x_float, axis=-1, keepdims=True)
    row_var = jnp.mean(jnp.square(x_float - row_mean), axis=-1, keepdims=True)
    normed = (x_float - row_mean) * lax.rsqrt(row_var + eps_norm)
    return (normed * (1.0 + shift_scale[1]) + shift_scale[0]).astype(bf16)


def attend_kernel(team_ref, cached_ref, mask_ref, gain_q_ref, gain_k_ref, out_ref, packed_ref):
    shard = team_ref.shape[1] - 16
    members = team_ref.shape[0]
    lane = lax.broadcasted_iota(jnp.int32, (16, LANES), 1)
    row = lax.broadcasted_iota(jnp.int32, (16, LANES), 0)
    fresh = [team_ref[c, shard:, :].astype(f32) for c in range(members)]
    features = jnp.concatenate([team_ref[c, :shard, :] for c in range(members)], axis=0)
    open_key = mask_ref[...] > 0.0
    sums = jnp.zeros((16, LANES), f32)
    for h in range(TEAM_HEADS):
        query = features[h * HEAD_DIM : (h + 1) * HEAD_DIM].astype(f32)
        scale = lax.rsqrt(jnp.mean(query * query, axis=0, keepdims=True) + eps_norm)
        query = (query * scale * gain_q_ref[...] * HEAD_DIM ** (-0.5)).astype(bf16)
        key = jnp.zeros((16, LANES), f32)
        value = jnp.zeros((16, LANES), f32)
        for c in range(members):
            start = c * shard - h * HEAD_DIM
            if start <= -shard or start >= HEAD_DIM:
                continue
            here = (lane >= start) & (lane < start + shard)
            key = jnp.where(here, pltpu.roll(fresh[c], start % LANES, 1), key)
            value = jnp.where(here, pltpu.roll(fresh[c], (start - shard) % LANES, 1), value)
        scale = lax.rsqrt(jnp.mean(key * key, axis=1, keepdims=True) + eps_norm)
        key = (key * scale * gain_k_ref[...]).astype(bf16)
        cached_key = cached_ref[:, h * HEAD_DIM : (h + 1) * HEAD_DIM]
        at = (TEAM_HEADS + h) * HEAD_DIM
        cached_value = cached_ref[:, at : at + HEAD_DIM]
        scores = jnp.dot(cached_key, query, preferred_element_type=f32)
        probs = jnp.exp(jnp.where(open_key, scores, -1e30))
        fresh_probs = jnp.exp(jnp.dot(key, query, preferred_element_type=f32))
        total = jnp.sum(probs, axis=0, keepdims=True) + jnp.sum(fresh_probs, axis=0, keepdims=True)
        sums = jnp.where(row == h, total, sums)
        contract = (((0,), (0,)), ((), ()))
        weighted = lax.dot_general(
            cached_value, probs.astype(bf16), contract, preferred_element_type=f32
        ) + lax.dot_general(
            value.astype(bf16), fresh_probs.astype(bf16), contract, preferred_element_type=f32
        )
        packed_ref[h * HEAD_DIM : (h + 1) * HEAD_DIM, :] = weighted.astype(bf16)
    for c in range(members):
        out_ref[c, :shard, :] = packed_ref[c * shard : (c + 1) * shard, :]
        out_ref[c, shard:, :] = sums.astype(bf16)


def attend(team, cached, mask, gains, interpret=False):
    whole = pl.BlockSpec(memory_space=pltpu.VMEM)
    return pl.pallas_call(
        attend_kernel,
        out_shape=jax.ShapeDtypeStruct(team.shape, bf16),
        in_specs=[whole] * 5,
        out_specs=whole,
        scratch_shapes=[pltpu.VMEM((TEAM_HEADS * HEAD_DIM, LANES), bf16)],
        compiler_params=pltpu.CompilerParams(vmem_limit_bytes=16 * 1024 * 1024),
        interpret=interpret,
    )(team, cached, mask, gains[0][:, None], gains[1][None, :])


def gathered(block, groups):
    size = len(groups[0])
    spread = jnp.broadcast_to(block[None], (size,) + block.shape)
    spread = lax.all_to_all(spread, "tp", 0, 0, axis_index_groups=groups)
    return spread.reshape((size * block.shape[0],) + block.shape[1:])


def summed_over(block, groups):
    size = len(groups[0])
    parts = block.astype(bf16).reshape((size, block.shape[0] // size) + block.shape[1:])
    parts = lax.all_to_all(parts, "tp", 0, 0, axis_index_groups=groups)
    return jnp.sum(parts.astype(f32), axis=0)


def local(
    in_flight, w_qkv, w_mlp, w_attn_out, w_mlp_out, modulation, qk_gain, context_kv, text_len
):
    tp_count = lax.axis_size("tp")
    tp_index = lax.axis_index("tp")
    rows = in_flight.shape[1]
    tokens = rows * tp_count
    width = w_attn_out.shape[2]
    shard = w_attn_out.shape[1]
    ctx_local = context_kv.shape[2]
    teams = tp_count // TEAM
    team_width = TEAM * shard
    member = tp_index % TEAM
    z_count, x_count = 2 * TEAM, tp_count // (2 * TEAM)
    along_z = [[z_count * x + z for z in range(z_count)] for x in range(x_count)]
    along_x = [[z_count * x + z for x in range(x_count)] for z in range(z_count)]
    inside = [[TEAM * t + m for m in range(TEAM)] for t in range(teams)]
    shift_scale = modulation[0]
    gains = qk_gain[0]
    weight_q = w_qkv[0, 0]
    weight_kv = w_qkv[0, 1:].reshape(2 * shard, width)
    weight_mlp = w_mlp[0]
    weight_attn = w_attn_out[0]
    weight_down = w_mlp_out[0]

    half_team = TEAM // 2
    partner = [
        z + TEAM + half_team if z < half_team else z + half_team if z < TEAM
        else z - half_team if z < TEAM + half_team else z - TEAM - half_team
        for z in range(z_count)
    ]
    z_here = tp_index % z_count
    z_partner = jnp.where(
        z_here < TEAM,
        z_here + jnp.where(z_here < half_team, TEAM + half_team, half_team),
        z_here - jnp.where(z_here < TEAM + half_team, half_team, TEAM + half_team),
    )
    by_half = context_kv[0].reshape(2, ctx_local, x_count, 2, team_width)
    upper = z_here >= TEAM
    keep = jnp.where(upper, by_half[:, :, :, 1], by_half[:, :, :, 0])
    give = jnp.where(upper, by_half[:, :, :, 0], by_half[:, :, :, 1])
    got = lax.ppermute(
        give, "tp", [(z_count * x + z, z_count * x + partner[z]) for x in range(x_count) for z in range(z_count)]
    )
    cached = jnp.concatenate([keep, got], axis=1).transpose(2, 1, 0, 3)
    cached = cached.reshape(x_count, 2 * ctx_local, 2 * team_width)
    slot = jnp.arange(teams * ctx_local, dtype=jnp.int32)
    within = slot % (2 * ctx_local)
    source = z_count * (slot // (2 * ctx_local)) + jnp.where(within < ctx_local, z_here, z_partner)
    position = ctx_local * source + within % ctx_local
    cached_mask = ((position >= TXT) | (position < text_len[0])).astype(f32)
    cached_mask = jnp.broadcast_to(cached_mask[:, None], (teams * ctx_local, LANES))
    current = in_flight[0]
    for tick_number in range(TICKS):
        normed_rows = modulated(current, shift_scale)
        normed = gathered(normed_rows.reshape(rows * width // LANES, LANES), along_z)
        normed = normed.reshape(rows * z_count, width)
        if tick_number == 0:
            wide = 2 * team_width
            split = width // wide
            normed = normed.reshape(-1, split, wide).transpose(1, 0, 2).reshape(-1, wide)
            both = jnp.concatenate(
                [jnp.broadcast_to(normed[None], (x_count,) + normed.shape), cached], axis=1
            )
            both = lax.all_to_all(both, "tp", 0, 0, axis_index_groups=along_x)
            normed = both[:, : normed.shape[0]].reshape(x_count, split, -1, wide)
            normed = normed.transpose(0, 2, 1, 3).reshape(tokens, width)
            cached = both[:, split * rows * z_count :].reshape(-1, wide)
        else:
            normed = gathered(normed, along_x)
        own_q = lax.dot_general(
            weight_q, normed, (((1,), (1,)), ((), ())), preferred_element_type=f32
        ).astype(bf16)
        own_kv = lax.dot_general(
            normed, weight_kv, (((1,), (1,)), ((), ())), preferred_element_type=f32
        ).astype(bf16)
        own_kv = jnp.pad(own_kv, ((0, 0), (0, LANES - 2 * shard))).reshape(TEAM, -1, LANES)
        team = jnp.concatenate(
            [jnp.broadcast_to(own_q[None], (TEAM,) + own_q.shape), own_kv], axis=1
        )
        team = lax.all_to_all(team, "tp", 0, 0, axis_index_groups=inside)
        parts = attend(team, cached, cached_mask, gains)
        parts = lax.all_to_all(parts, "tp", 0, 0, axis_index_groups=inside)
        summed = jnp.sum(parts.astype(f32), axis=0)
        feature_head = (member * shard + jnp.arange(shard, dtype=jnp.int32)) // HEAD_DIM
        total_rows = summed[shard + TEAM_HEADS - 1][None]
        for h in range(TEAM_HEADS - 1):
            total_rows = jnp.where(feature_head[:, None] == h, summed[shard + h][None], total_rows)
        attention = (summed[:shard] / total_rows).astype(bf16)
        hidden = jax.nn.gelu(
            lax.dot_general(
                normed, weight_mlp, (((1,), (1,)), ((), ())), preferred_element_type=f32
            ),
            approximate=True,
        ).astype(bf16)
        hidden = lax.optimization_barrier(hidden)
        forward = jnp.dot(hidden, weight_down, preferred_element_type=f32) * shift_scale[2]
        forward = lax.optimization_barrier(forward)
        branch = lax.dot_general(
            attention, weight_attn, (((0,), (0,)), ((), ())), preferred_element_type=f32
        )
        branch = branch * shift_scale[2] + forward
        branch = summed_over(branch, along_x)
        branch = summed_over(branch.reshape(-1, LANES), along_z).reshape(rows, width)
        finished = (current.astype(f32) + branch).astype(bf16)
        current = shifted(finished, "pipe", 1)
    return current[None]


def solution(mesh):
    placed = (
        P("pipe", "tp", None),
        P("pipe", None, "tp", None),
        P("pipe", "tp", None),
        P("pipe", "tp", None),
        P("pipe", "tp", None),
        P("pipe", None, None),
        P("pipe", None, None),
        P("pipe", None, "tp", None),
        P(),
    )
    return jax.shard_map(
        local, mesh=mesh, in_specs=placed, out_specs=P("pipe", "tp", None), check_vma=False
    )
```

```python
import jax
import jax.numpy as jnp
from jax import lax
from jax.experimental import pallas as pl
from jax.experimental.pallas import tpu as pltpu
from jax.sharding import PartitionSpec as P

HEADS = 24
HEAD_DIM = 128
TICKS = 2
TXT = 512
TEAM = 8
TEAM_HEADS = 3
LANES = 128

eps_norm = 1e-06
f32 = jnp.float32
bf16 = jnp.bfloat16


def shifted(block, axis, distance):
    size = lax.axis_size(axis)
    return lax.ppermute(block, axis, [((i - distance) % size, i) for i in range(size)])


def modulated(hidden_state, shift_scale):
    x_float = hidden_state.astype(f32)
    row_mean = jnp.mean(x_float, axis=-1, keepdims=True)
    row_var = jnp.mean(jnp.square(x_float - row_mean), axis=-1, keepdims=True)
    normed = (x_float - row_mean) * lax.rsqrt(row_var + eps_norm)
    return (normed * (1.0 + shift_scale[1]) + shift_scale[0]).astype(bf16)


def project_kernel(normed_ref, weight_ref, out_ref):
    members = out_ref.shape[0]
    shard = weight_ref.shape[0] // 3
    contract = (((1,), (1,)), ((), ()))
    query = lax.dot_general(
        weight_ref[:shard], normed_ref[...], contract, preferred_element_type=f32
    ).astype(bf16)
    others = lax.dot_general(
        normed_ref[...], weight_ref[shard:], contract, preferred_element_type=f32
    ).astype(bf16)
    for c in range(members):
        out_ref[c, :shard, :] = query
        out_ref[c, shard:, : 2 * shard] = others[16 * c : 16 * c + 16]
        out_ref[c, shard:, 2 * shard :] = jnp.zeros((16, LANES - 2 * shard), bf16)


def project(normed, weights):
    whole = pl.BlockSpec(memory_space=pltpu.VMEM)
    return pl.pallas_call(
        project_kernel,
        out_shape=jax.ShapeDtypeStruct((TEAM, weights.shape[0] // 3 + 16, LANES), bf16),
        in_specs=[whole] * 2,
        out_specs=whole,
        compiler_params=pltpu.CompilerParams(vmem_limit_bytes=16 * 1024 * 1024),
    )(normed, weights)


def attend_kernel(team_ref, cached_ref, mask_ref, gain_q_ref, gain_k_ref, out_ref, packed_ref):
    shard = team_ref.shape[1] - 16
    members = team_ref.shape[0]
    lane = lax.broadcasted_iota(jnp.int32, (16, LANES), 1)
    row = lax.broadcasted_iota(jnp.int32, (16, LANES), 0)
    fresh = [team_ref[c, shard:, :].astype(f32) for c in range(members)]
    features = jnp.concatenate([team_ref[c, :shard, :] for c in range(members)], axis=0)
    open_key = mask_ref[...] > 0.0
    sums = jnp.zeros((16, LANES), f32)
    for h in range(TEAM_HEADS):
        query = features[h * HEAD_DIM : (h + 1) * HEAD_DIM].astype(f32)
        scale = lax.rsqrt(jnp.mean(query * query, axis=0, keepdims=True) + eps_norm)
        query = (query * scale * gain_q_ref[...] * HEAD_DIM ** (-0.5)).astype(bf16)
        key = jnp.zeros((16, LANES), f32)
        value = jnp.zeros((16, LANES), f32)
        for c in range(members):
            start = c * shard - h * HEAD_DIM
            if start <= -shard or start >= HEAD_DIM:
                continue
            here = (lane >= start) & (lane < start + shard)
            key = jnp.where(here, pltpu.roll(fresh[c], start % LANES, 1), key)
            value = jnp.where(here, pltpu.roll(fresh[c], (start - shard) % LANES, 1), value)
        scale = lax.rsqrt(jnp.mean(key * key, axis=1, keepdims=True) + eps_norm)
        key = (key * scale * gain_k_ref[...]).astype(bf16)
        cached_key = cached_ref[:, h * HEAD_DIM : (h + 1) * HEAD_DIM]
        at = (TEAM_HEADS + h) * HEAD_DIM
        cached_value = cached_ref[:, at : at + HEAD_DIM]
        scores = jnp.dot(cached_key, query, preferred_element_type=f32)
        probs = jnp.exp(jnp.where(open_key, scores, -1e30))
        fresh_probs = jnp.exp(jnp.dot(key, query, preferred_element_type=f32))
        total = jnp.sum(probs, axis=0, keepdims=True) + jnp.sum(fresh_probs, axis=0, keepdims=True)
        sums = jnp.where(row == h, total, sums)
        contract = (((0,), (0,)), ((), ()))
        weighted = lax.dot_general(
            cached_value, probs.astype(bf16), contract, preferred_element_type=f32
        ) + lax.dot_general(
            value.astype(bf16), fresh_probs.astype(bf16), contract, preferred_element_type=f32
        )
        packed_ref[h * HEAD_DIM : (h + 1) * HEAD_DIM, :] = weighted.astype(bf16)
    for c in range(members):
        out_ref[c, :shard, :] = packed_ref[c * shard : (c + 1) * shard, :]
        out_ref[c, shard:, :] = sums.astype(bf16)


def attend(team, cached, mask, gains, interpret=False):
    whole = pl.BlockSpec(memory_space=pltpu.VMEM)
    return pl.pallas_call(
        attend_kernel,
        out_shape=jax.ShapeDtypeStruct(team.shape, bf16),
        in_specs=[whole] * 5,
        out_specs=whole,
        scratch_shapes=[pltpu.VMEM((TEAM_HEADS * HEAD_DIM, LANES), bf16)],
        compiler_params=pltpu.CompilerParams(vmem_limit_bytes=16 * 1024 * 1024),
        interpret=interpret,
    )(team, cached, mask, gains[0][:, None], gains[1][None, :])


def gathered(block, groups):
    size = len(groups[0])
    spread = jnp.broadcast_to(block[None], (size,) + block.shape)
    spread = lax.all_to_all(spread, "tp", 0, 0, axis_index_groups=groups)
    return spread.reshape((size * block.shape[0],) + block.shape[1:])


def summed_over(block, groups):
    size = len(groups[0])
    parts = block.astype(bf16).reshape((size, block.shape[0] // size) + block.shape[1:])
    parts = lax.all_to_all(parts, "tp", 0, 0, axis_index_groups=groups)
    return jnp.sum(parts.astype(f32), axis=0)


def local(
    in_flight, w_qkv, w_mlp, w_attn_out, w_mlp_out, modulation, qk_gain, context_kv, text_len
):
    tp_count = lax.axis_size("tp")
    tp_index = lax.axis_index("tp")
    rows = in_flight.shape[1]
    tokens = rows * tp_count
    width = w_attn_out.shape[2]
    shard = w_attn_out.shape[1]
    ctx_local = context_kv.shape[2]
    teams = tp_count // TEAM
    team_width = TEAM * shard
    member = tp_index % TEAM
    z_count, x_count = 2 * TEAM, tp_count // (2 * TEAM)
    along_z = [[z_count * x + z for z in range(z_count)] for x in range(x_count)]
    along_x = [[z_count * x + z for x in range(x_count)] for z in range(z_count)]
    inside = [[TEAM * t + m for m in range(TEAM)] for t in range(teams)]
    shift_scale = modulation[0]
    gains = qk_gain[0]
    weight_qkv = w_qkv[0].reshape(3 * shard, width)
    weight_mlp = w_mlp[0]
    weight_attn = w_attn_out[0]
    weight_down = w_mlp_out[0]

    half_team = TEAM // 2
    partner = [
        z + TEAM + half_team if z < half_team else z + half_team if z < TEAM
        else z - half_team if z < TEAM + half_team else z - TEAM - half_team
        for z in range(z_count)
    ]
    x_here, z_here = tp_index // z_count, tp_index % z_count
    z_partner = jnp.where(
        z_here < TEAM,
        z_here + jnp.where(z_here < half_team, TEAM + half_team, half_team),
        z_here - jnp.where(z_here < TEAM + half_team, half_team, TEAM + half_team),
    )
    upper = z_here >= TEAM
    slot = jnp.arange(teams * ctx_local, dtype=jnp.int32)
    within = slot % (2 * ctx_local)
    source = z_count * ((x_here - slot // (2 * ctx_local)) % x_count)
    source = source + jnp.where(within < ctx_local, z_here, z_partner)
    position = ctx_local * source + within % ctx_local
    cached_mask = ((position >= TXT) | (position < text_len[0])).astype(f32)
    cached_mask = jnp.broadcast_to(cached_mask[:, None], (teams * ctx_local, LANES))

    current = in_flight[0]
    first_rows = modulated(current, shift_scale)
    first_rows, flat = lax.optimization_barrier((first_rows, context_kv[0]))
    flat = flat.reshape(2 * ctx_local, width)
    by_x = []
    for step in range(x_count):
        block = lax.dynamic_slice_in_dim(
            flat, (x_here + step) % x_count * 2 * team_width, 2 * team_width, 1
        )
        if step:
            route = [
                (z_count * x + z, z_count * ((x + step) % x_count) + z)
                for x in range(x_count) for z in range(z_count)
            ]
            block = lax.ppermute(block, "tp", route)
        by_x.append(block)
    by_x = jnp.stack(by_x)
    keep = jnp.where(upper, by_x[:, :, team_width:], by_x[:, :, :team_width])
    give = jnp.where(upper, by_x[:, :, :team_width], by_x[:, :, team_width:])

    for tick_number in range(TICKS):
        normed_rows = modulated(current, shift_scale) if tick_number else first_rows
        normed = gathered(normed_rows.reshape(rows * width // LANES, LANES), along_z)
        normed = normed.reshape(rows * z_count, width)
        if tick_number == 0:
            normed, give = lax.optimization_barrier((normed, give))
            got = lax.ppermute(
                give,
                "tp",
                [(z_count * x + z, z_count * x + partner[z]) for x in range(x_count) for z in range(z_count)],
            )
            cached = jnp.stack([keep, got], axis=1)
            cached = cached.reshape(x_count, 2, 2, ctx_local, team_width).transpose(0, 1, 3, 2, 4)
            cached = cached.reshape(teams * ctx_local, 2 * team_width)
        normed = gathered(normed, along_x)
        team = project(normed, weight_qkv)
        team = lax.all_to_all(team, "tp", 0, 0, axis_index_groups=inside)
        parts = attend(team, cached, cached_mask, gains)
        parts = lax.all_to_all(parts, "tp", 0, 0, axis_index_groups=inside)
        summed = jnp.sum(parts.astype(f32), axis=0)
        feature_head = (member * shard + jnp.arange(shard, dtype=jnp.int32)) // HEAD_DIM
        total_rows = summed[shard + TEAM_HEADS - 1][None]
        for h in range(TEAM_HEADS - 1):
            total_rows = jnp.where(feature_head[:, None] == h, summed[shard + h][None], total_rows)
        attention = (summed[:shard] / total_rows).astype(bf16)
        hidden = jax.nn.gelu(
            lax.dot_general(
                normed, weight_mlp, (((1,), (1,)), ((), ())), preferred_element_type=f32
            ),
            approximate=True,
        ).astype(bf16)
        hidden = lax.optimization_barrier(hidden)
        forward = jnp.dot(hidden, weight_down, preferred_element_type=f32) * shift_scale[2]
        forward = lax.optimization_barrier(forward)
        branch = lax.dot_general(
            attention, weight_attn, (((0,), (0,)), ((), ())), preferred_element_type=f32
        )
        branch = branch * shift_scale[2] + forward
        branch = summed_over(branch, along_x)
        branch = summed_over(branch.reshape(-1, LANES), along_z).reshape(rows, width)
        finished = (current.astype(f32) + branch).astype(bf16)
        current = shifted(finished, "pipe", 1)
    return current[None]


def solution(mesh):
    placed = (
        P("pipe", "tp", None),
        P("pipe", None, "tp", None),
        P("pipe", "tp", None),
        P("pipe", "tp", None),
        P("pipe", "tp", None),
        P("pipe", None, None),
        P("pipe", None, None),
        P("pipe", None, "tp", None),
        P(),
    )
    return jax.shard_map(
        local, mesh=mesh, in_specs=placed, out_specs=P("pipe", "tp", None), check_vma=False
    )
```

```python
import jax
import jax.numpy as jnp
from jax import lax
from jax.experimental import pallas as pl
from jax.experimental.pallas import tpu as pltpu
from jax.sharding import PartitionSpec as P

HEADS = 24
HEAD_DIM = 128
TICKS = 2
TXT = 512
TEAM = 8
TEAM_HEADS = 3
LANES = 128

eps_norm = 1e-06
f32 = jnp.float32
bf16 = jnp.bfloat16


def shifted(block, axis, distance):
    size = lax.axis_size(axis)
    return lax.ppermute(block, axis, [((i - distance) % size, i) for i in range(size)])


def spread_kernel(rows_ref, modulation_ref, out_ref, block_ref):
    x = rows_ref[...].astype(f32)
    centred = x - jnp.mean(x, axis=1, keepdims=True)
    variance = jnp.mean(centred * centred, axis=1, keepdims=True)
    normed = centred * lax.rsqrt(variance + eps_norm)
    normed = normed * (1.0 + modulation_ref[1:2, :]) + modulation_ref[0:1, :]
    rows, width = x.shape
    pieces = width // LANES
    for r in range(rows):
        for p in range(pieces):
            at = r * pieces + p
            block_ref[at : at + 1, :] = normed[r : r + 1, p * LANES : (p + 1) * LANES]
    block = block_ref[...].astype(bf16)
    for j in range(out_ref.shape[0]):
        out_ref[j] = block


def spread(rows, modulation, receivers):
    whole = pl.BlockSpec(memory_space=pltpu.VMEM)
    lines = rows.shape[0] * rows.shape[1] // LANES
    return pl.pallas_call(
        spread_kernel,
        out_shape=jax.ShapeDtypeStruct((receivers, lines, LANES), bf16),
        in_specs=[whole] * 2,
        out_specs=whole,
        scratch_shapes=[pltpu.VMEM((lines, LANES), f32)],
        compiler_params=pltpu.CompilerParams(vmem_limit_bytes=16 * 1024 * 1024),
    )(rows, modulation)


def finish_kernel(member_ref, parts_ref, weight_ref, forward_ref, modulation_ref, out_ref):
    shard, width = weight_ref.shape
    summed = parts_ref[0].astype(f32)
    for c in range(1, parts_ref.shape[0]):
        summed = summed + parts_ref[c].astype(f32)
    feature = member_ref[0] * shard + lax.broadcasted_iota(jnp.int32, (shard, LANES), 0)
    total = jnp.broadcast_to(summed[shard + TEAM_HEADS - 1][None], (shard, LANES))
    for h in range(TEAM_HEADS - 2, -1, -1):
        total = jnp.where(feature < (h + 1) * HEAD_DIM, summed[shard + h][None], total)
    attention = (summed[:shard] / total).astype(bf16)
    branch = lax.dot_general(
        attention, weight_ref[...], (((0,), (0,)), ((), ())), preferred_element_type=f32
    )
    out_ref[...] = ((branch + forward_ref[...]) * modulation_ref[2:3, :]).astype(bf16)


def finish(member, parts, weights, forward, modulation):
    whole = pl.BlockSpec(memory_space=pltpu.VMEM)
    return pl.pallas_call(
        finish_kernel,
        out_shape=jax.ShapeDtypeStruct(forward.shape, bf16),
        in_specs=[pl.BlockSpec(memory_space=pltpu.SMEM)] + [whole] * 4,
        out_specs=whole,
        compiler_params=pltpu.CompilerParams(vmem_limit_bytes=16 * 1024 * 1024),
    )(member, parts, weights, forward, modulation)


def project_kernel(normed_ref, weight_ref, out_ref):
    members = out_ref.shape[0]
    shard = weight_ref.shape[0] // 3
    contract = (((1,), (1,)), ((), ()))
    query = lax.dot_general(
        weight_ref[:shard], normed_ref[...], contract, preferred_element_type=f32
    ).astype(bf16)
    others = lax.dot_general(
        normed_ref[...], weight_ref[shard:], contract, preferred_element_type=f32
    ).astype(bf16)
    for c in range(members):
        out_ref[c, :shard, :] = query
        out_ref[c, shard:, : 2 * shard] = others[16 * c : 16 * c + 16]
        out_ref[c, shard:, 2 * shard :] = jnp.zeros((16, LANES - 2 * shard), bf16)


def project(normed, weights):
    whole = pl.BlockSpec(memory_space=pltpu.VMEM)
    return pl.pallas_call(
        project_kernel,
        out_shape=jax.ShapeDtypeStruct((TEAM, weights.shape[0] // 3 + 16, LANES), bf16),
        in_specs=[whole] * 2,
        out_specs=whole,
        compiler_params=pltpu.CompilerParams(vmem_limit_bytes=16 * 1024 * 1024),
    )(normed, weights)


def attend_kernel(
    team_ref, keep_ref, got_ref, mask_ref, gain_q_ref, gain_k_ref, out_ref, packed_ref
):
    shard = team_ref.shape[1] - 16
    members = team_ref.shape[0]
    lane = lax.broadcasted_iota(jnp.int32, (16, LANES), 1)
    row = lax.broadcasted_iota(jnp.int32, (16, LANES), 0)
    fresh = [team_ref[c, shard:, :].astype(f32) for c in range(members)]
    features = jnp.concatenate([team_ref[c, :shard, :] for c in range(members)], axis=0)
    open_key = mask_ref[...] > 0.0
    blocks = [r[i].astype(f32) for i in range(keep_ref.shape[0]) for r in (keep_ref, got_ref)]
    half = keep_ref.shape[1] // 2
    cached_keys = jnp.concatenate([b[:half] for b in blocks], axis=0).astype(bf16)
    cached_values = jnp.concatenate([b[half:] for b in blocks], axis=0).astype(bf16)
    sums = jnp.zeros((16, LANES), f32)
    for h in range(TEAM_HEADS):
        query = features[h * HEAD_DIM : (h + 1) * HEAD_DIM].astype(f32)
        scale = lax.rsqrt(jnp.mean(query * query, axis=0, keepdims=True) + eps_norm)
        query = (query * scale * gain_q_ref[...] * HEAD_DIM ** (-0.5)).astype(bf16)
        key = jnp.zeros((16, LANES), f32)
        value = jnp.zeros((16, LANES), f32)
        for c in range(members):
            start = c * shard - h * HEAD_DIM
            if start <= -shard or start >= HEAD_DIM:
                continue
            here = (lane >= start) & (lane < start + shard)
            key = jnp.where(here, pltpu.roll(fresh[c], start % LANES, 1), key)
            value = jnp.where(here, pltpu.roll(fresh[c], (start - shard) % LANES, 1), value)
        scale = lax.rsqrt(jnp.mean(key * key, axis=1, keepdims=True) + eps_norm)
        key = (key * scale * gain_k_ref[...]).astype(bf16)
        cached_key = cached_keys[:, h * HEAD_DIM : (h + 1) * HEAD_DIM]
        cached_value = cached_values[:, h * HEAD_DIM : (h + 1) * HEAD_DIM]
        scores = jnp.dot(cached_key, query, preferred_element_type=f32)
        probs = jnp.exp(jnp.where(open_key, scores, -1e30))
        fresh_probs = jnp.exp(jnp.dot(key, query, preferred_element_type=f32))
        total = jnp.sum(probs, axis=0, keepdims=True) + jnp.sum(fresh_probs, axis=0, keepdims=True)
        sums = jnp.where(row == h, total, sums)
        contract = (((0,), (0,)), ((), ()))
        weighted = lax.dot_general(
            cached_value, probs.astype(bf16), contract, preferred_element_type=f32
        ) + lax.dot_general(
            value.astype(bf16), fresh_probs.astype(bf16), contract, preferred_element_type=f32
        )
        packed_ref[h * HEAD_DIM : (h + 1) * HEAD_DIM, :] = weighted.astype(bf16)
    for c in range(members):
        out_ref[c, :shard, :] = packed_ref[c * shard : (c + 1) * shard, :]
        out_ref[c, shard:, :] = sums.astype(bf16)


def attend(team, keep, got, mask, gains):
    whole = pl.BlockSpec(memory_space=pltpu.VMEM)
    return pl.pallas_call(
        attend_kernel,
        out_shape=jax.ShapeDtypeStruct(team.shape, bf16),
        in_specs=[whole] * 6,
        out_specs=whole,
        scratch_shapes=[pltpu.VMEM((TEAM_HEADS * HEAD_DIM, LANES), bf16)],
        compiler_params=pltpu.CompilerParams(vmem_limit_bytes=16 * 1024 * 1024),
    )(team, keep, got, mask, gains[0][:, None], gains[1][None, :])


def gathered(block, groups):
    size = len(groups[0])
    spread = jnp.broadcast_to(block[None], (size,) + block.shape)
    spread = lax.all_to_all(spread, "tp", 0, 0, axis_index_groups=groups)
    return spread.reshape((size * block.shape[0],) + block.shape[1:])


def summed_over(block, groups):
    size = len(groups[0])
    parts = block.astype(bf16).reshape((size, block.shape[0] // size) + block.shape[1:])
    parts = lax.all_to_all(parts, "tp", 0, 0, axis_index_groups=groups)
    return jnp.sum(parts.astype(f32), axis=0)


def local(
    in_flight, w_qkv, w_mlp, w_attn_out, w_mlp_out, modulation, qk_gain, context_kv, text_len
):
    tp_count = lax.axis_size("tp")
    tp_index = lax.axis_index("tp")
    rows = in_flight.shape[1]
    tokens = rows * tp_count
    width = w_attn_out.shape[2]
    shard = w_attn_out.shape[1]
    ctx_local = context_kv.shape[2]
    teams = tp_count // TEAM
    team_width = TEAM * shard
    member = tp_index % TEAM
    z_count, x_count = 2 * TEAM, tp_count // (2 * TEAM)
    along_z = [[z_count * x + z for z in range(z_count)] for x in range(x_count)]
    along_x = [[z_count * x + z for x in range(x_count)] for z in range(z_count)]
    inside = [[TEAM * t + m for m in range(TEAM)] for t in range(teams)]
    shift_scale = modulation[0]
    gains = qk_gain[0]
    weight_qkv = w_qkv[0].reshape(3 * shard, width)
    weight_mlp = w_mlp[0]
    weight_attn = w_attn_out[0]
    weight_down = w_mlp_out[0]

    half_team = TEAM // 2
    partner = [
        z + TEAM + half_team if z < half_team else z + half_team if z < TEAM
        else z - half_team if z < TEAM + half_team else z - TEAM - half_team
        for z in range(z_count)
    ]
    x_here, z_here = tp_index // z_count, tp_index % z_count
    z_partner = jnp.where(
        z_here < TEAM,
        z_here + jnp.where(z_here < half_team, TEAM + half_team, half_team),
        z_here - jnp.where(z_here < TEAM + half_team, half_team, TEAM + half_team),
    )
    upper = z_here >= TEAM
    slot = jnp.arange(teams * ctx_local, dtype=jnp.int32)
    within = slot % (2 * ctx_local)
    source = z_count * ((x_here - slot // (2 * ctx_local)) % x_count)
    source = source + jnp.where(within < ctx_local, z_here, z_partner)
    position = ctx_local * source + within % ctx_local
    cached_mask = ((position >= TXT) | (position < text_len[0])).astype(f32)
    cached_mask = jnp.broadcast_to(cached_mask[:, None], (teams * ctx_local, LANES))

    current = in_flight[0]
    block = spread(current, shift_scale, z_count)
    block, flat = lax.optimization_barrier((block, context_kv[0]))
    flat = flat.reshape(2 * ctx_local, width)
    by_x = []
    for step in range(x_count):
        part = lax.dynamic_slice_in_dim(
            flat, (x_here + step) % x_count * 2 * team_width, 2 * team_width, 1
        )
        if step:
            route = [
                (z_count * x + z, z_count * ((x + step) % x_count) + z)
                for x in range(x_count) for z in range(z_count)
            ]
            part = lax.ppermute(part, "tp", route)
        by_x.append(part)
    by_x = jnp.stack(by_x)
    keep = jnp.where(upper, by_x[:, :, team_width:], by_x[:, :, :team_width])
    give = jnp.where(upper, by_x[:, :, :team_width], by_x[:, :, team_width:])

    for tick_number in range(TICKS):
        if tick_number:
            block = spread(current, shift_scale, z_count)
        normed = lax.all_to_all(block, "tp", 0, 0, axis_index_groups=along_z)
        normed = normed.reshape(rows * z_count, width)
        if tick_number == 0:
            normed, give = lax.optimization_barrier((normed, give))
            got = lax.ppermute(
                give,
                "tp",
                [(z_count * x + z, z_count * x + partner[z]) for x in range(x_count) for z in range(z_count)],
            )
        normed = gathered(normed, along_x)
        if tick_number == 0:
            normed, got = lax.optimization_barrier((normed, got))
        team = project(normed, weight_qkv)
        team = lax.all_to_all(team, "tp", 0, 0, axis_index_groups=inside)
        parts = attend(team, keep, got, cached_mask, gains)
        parts = lax.all_to_all(parts, "tp", 0, 0, axis_index_groups=inside)
        hidden = jax.nn.gelu(
            lax.dot_general(
                normed, weight_mlp, (((1,), (1,)), ((), ())), preferred_element_type=f32
            ),
            approximate=True,
        ).astype(bf16)
        hidden = lax.optimization_barrier(hidden)
        forward = jnp.dot(hidden, weight_down, preferred_element_type=f32)
        forward = lax.optimization_barrier(forward)
        branch = finish(member[None], parts, weight_attn, forward, shift_scale)
        branch = summed_over(branch, along_x)
        branch = summed_over(branch.reshape(-1, LANES), along_z).reshape(rows, width)
        finished = (current.astype(f32) + branch).astype(bf16)
        current = shifted(finished, "pipe", 1)
    return current[None]


def solution(mesh):
    placed = (
        P("pipe", "tp", None),
        P("pipe", None, "tp", None),
        P("pipe", "tp", None),
        P("pipe", "tp", None),
        P("pipe", "tp", None),
        P("pipe", None, None),
        P("pipe", None, None),
        P("pipe", None, "tp", None),
        P(),
    )
    return jax.shard_map(
        local, mesh=mesh, in_specs=placed, out_specs=P("pipe", "tp", None), check_vma=False
    )
```

```python
import jax
import jax.numpy as jnp
from jax import lax
from jax.experimental import pallas as pl
from jax.experimental.pallas import tpu as pltpu
from jax.sharding import PartitionSpec as P

HEADS = 24
HEAD_DIM = 128
TICKS = 2
TXT = 512
TEAM = 8
TEAM_HEADS = 3
LANES = 128

eps_norm = 1e-06
f32 = jnp.float32
bf16 = jnp.bfloat16


def shifted(block, axis, distance):
    size = lax.axis_size(axis)
    return lax.ppermute(block, axis, [((i - distance) % size, i) for i in range(size)])


def spread_kernel(rows_ref, modulation_ref, out_ref, block_ref):
    x = rows_ref[...].astype(f32)
    centred = x - jnp.mean(x, axis=1, keepdims=True)
    variance = jnp.mean(centred * centred, axis=1, keepdims=True)
    normed = centred * lax.rsqrt(variance + eps_norm)
    normed = normed * (1.0 + modulation_ref[1]) + modulation_ref[0]
    rows, width = x.shape
    pieces = width // LANES
    for r in range(rows):
        for p in range(pieces):
            at = r * pieces + p
            block_ref[at : at + 1, :] = normed[r : r + 1, p * LANES : (p + 1) * LANES]
    block = block_ref[...].astype(bf16)
    for j in range(out_ref.shape[0]):
        out_ref[j] = block


def spread(rows, modulation, receivers):
    whole = pl.BlockSpec(memory_space=pltpu.VMEM)
    lines = rows.shape[0] * rows.shape[1] // LANES
    return pl.pallas_call(
        spread_kernel,
        out_shape=jax.ShapeDtypeStruct((receivers, lines, LANES), bf16),
        in_specs=[whole] * 2,
        out_specs=whole,
        scratch_shapes=[pltpu.VMEM((lines, LANES), f32)],
        compiler_params=pltpu.CompilerParams(vmem_limit_bytes=16 * 1024 * 1024),
    )(rows, modulation)


def finish_kernel(member_ref, parts_ref, weight_ref, forward_ref, modulation_ref, out_ref):
    shard, width = weight_ref.shape
    summed = parts_ref[0].astype(f32)
    for c in range(1, parts_ref.shape[0]):
        summed = summed + parts_ref[c].astype(f32)
    feature = member_ref[0] * shard + lax.broadcasted_iota(jnp.int32, (shard, LANES), 0)
    total = jnp.broadcast_to(summed[shard + TEAM_HEADS - 1][None], (shard, LANES))
    for h in range(TEAM_HEADS - 2, -1, -1):
        total = jnp.where(feature < (h + 1) * HEAD_DIM, summed[shard + h][None], total)
    attention = (summed[:shard] / total).astype(bf16)
    branch = lax.dot_general(
        attention, weight_ref[...], (((0,), (0,)), ((), ())), preferred_element_type=f32
    )
    out_ref[...] = ((branch + forward_ref[...]) * modulation_ref[2]).astype(bf16)


def finish(member, parts, weights, forward, modulation):
    whole = pl.BlockSpec(memory_space=pltpu.VMEM)
    return pl.pallas_call(
        finish_kernel,
        out_shape=jax.ShapeDtypeStruct(forward.shape, bf16),
        in_specs=[pl.BlockSpec(memory_space=pltpu.SMEM)] + [whole] * 4,
        out_specs=whole,
        compiler_params=pltpu.CompilerParams(vmem_limit_bytes=16 * 1024 * 1024),
    )(member, parts, weights, forward, modulation)


def project_kernel(normed_ref, weight_ref, out_ref):
    members = out_ref.shape[0]
    shard = weight_ref.shape[0] // 3
    contract = (((1,), (1,)), ((), ()))
    query = lax.dot_general(
        weight_ref[:shard], normed_ref[...], contract, preferred_element_type=f32
    ).astype(bf16)
    others = lax.dot_general(
        normed_ref[...], weight_ref[shard:], contract, preferred_element_type=f32
    ).astype(bf16)
    for c in range(members):
        out_ref[c, :shard, :] = query
        out_ref[c, shard:, : 2 * shard] = others[16 * c : 16 * c + 16]
        out_ref[c, shard:, 2 * shard :] = jnp.zeros((16, LANES - 2 * shard), bf16)


def project(normed, weights):
    whole = pl.BlockSpec(memory_space=pltpu.VMEM)
    return pl.pallas_call(
        project_kernel,
        out_shape=jax.ShapeDtypeStruct((TEAM, weights.shape[0] // 3 + 16, LANES), bf16),
        in_specs=[whole] * 2,
        out_specs=whole,
        compiler_params=pltpu.CompilerParams(vmem_limit_bytes=16 * 1024 * 1024),
    )(normed, weights)


def attend_kernel(team_ref, mask_ref, gain_q_ref, gain_k_ref, *refs):
    *cached_refs, out_ref, packed_ref = refs
    shard = team_ref.shape[1] - 16
    members = team_ref.shape[0]
    lane = lax.broadcasted_iota(jnp.int32, (16, LANES), 1)
    row = lax.broadcasted_iota(jnp.int32, (16, LANES), 0)
    fresh = [team_ref[c, shard:, :].astype(f32) for c in range(members)]
    features = jnp.concatenate([team_ref[c, :shard, :] for c in range(members)], axis=0)
    open_key = mask_ref[...] > 0.0
    blocks = [r[i].astype(f32) for r in cached_refs for i in range(r.shape[0])]
    half = blocks[0].shape[0] // 2
    cached_keys = jnp.concatenate([b[:half] for b in blocks], axis=0).astype(bf16)
    cached_values = jnp.concatenate([b[half:] for b in blocks], axis=0).astype(bf16)
    sums = jnp.zeros((16, LANES), f32)
    for h in range(TEAM_HEADS):
        query = features[h * HEAD_DIM : (h + 1) * HEAD_DIM].astype(f32)
        scale = lax.rsqrt(jnp.mean(query * query, axis=0, keepdims=True) + eps_norm)
        query = (query * scale * gain_q_ref[...] * HEAD_DIM ** (-0.5)).astype(bf16)
        key = jnp.zeros((16, LANES), f32)
        value = jnp.zeros((16, LANES), f32)
        for c in range(members):
            start = c * shard - h * HEAD_DIM
            if start <= -shard or start >= HEAD_DIM:
                continue
            here = (lane >= start) & (lane < start + shard)
            key = jnp.where(here, pltpu.roll(fresh[c], start % LANES, 1), key)
            value = jnp.where(here, pltpu.roll(fresh[c], (start - shard) % LANES, 1), value)
        scale = lax.rsqrt(jnp.mean(key * key, axis=1, keepdims=True) + eps_norm)
        key = (key * scale * gain_k_ref[...]).astype(bf16)
        cached_key = cached_keys[:, h * HEAD_DIM : (h + 1) * HEAD_DIM]
        cached_value = cached_values[:, h * HEAD_DIM : (h + 1) * HEAD_DIM]
        scores = jnp.dot(cached_key, query, preferred_element_type=f32)
        probs = jnp.exp(jnp.where(open_key, scores, -1e30))
        fresh_probs = jnp.exp(jnp.dot(key, query, preferred_element_type=f32))
        total = jnp.sum(probs, axis=0, keepdims=True) + jnp.sum(fresh_probs, axis=0, keepdims=True)
        sums = jnp.where(row == h, total, sums)
        contract = (((0,), (0,)), ((), ()))
        weighted = lax.dot_general(
            cached_value, probs.astype(bf16), contract, preferred_element_type=f32
        ) + lax.dot_general(
            value.astype(bf16), fresh_probs.astype(bf16), contract, preferred_element_type=f32
        )
        packed_ref[h * HEAD_DIM : (h + 1) * HEAD_DIM, :] = weighted.astype(bf16)
    for c in range(members):
        out_ref[c, :shard, :] = packed_ref[c * shard : (c + 1) * shard, :]
        out_ref[c, shard:, :] = sums.astype(bf16)


def attend(team, cached, mask, gains):
    whole = pl.BlockSpec(memory_space=pltpu.VMEM)
    return pl.pallas_call(
        attend_kernel,
        out_shape=jax.ShapeDtypeStruct(team.shape, bf16),
        in_specs=[whole] * (4 + len(cached)),
        out_specs=whole,
        scratch_shapes=[pltpu.VMEM((TEAM_HEADS * HEAD_DIM, LANES), bf16)],
        compiler_params=pltpu.CompilerParams(vmem_limit_bytes=16 * 1024 * 1024),
    )(team, mask, gains[0][:, None], gains[1][None, :], *cached)


def gathered(block, groups):
    size = len(groups[0])
    spread = jnp.broadcast_to(block[None], (size,) + block.shape)
    spread = lax.all_to_all(spread, "tp", 0, 0, axis_index_groups=groups)
    return spread.reshape((size * block.shape[0],) + block.shape[1:])


def summed_over(block, groups):
    size = len(groups[0])
    parts = block.astype(bf16).reshape((size, block.shape[0] // size) + block.shape[1:])
    parts = lax.all_to_all(parts, "tp", 0, 0, axis_index_groups=groups)
    return jnp.sum(parts.astype(f32), axis=0)


def local(
    in_flight, w_qkv, w_mlp, w_attn_out, w_mlp_out, modulation, qk_gain, context_kv, text_len
):
    tp_count = lax.axis_size("tp")
    tp_index = lax.axis_index("tp")
    rows = in_flight.shape[1]
    tokens = rows * tp_count
    width = w_attn_out.shape[2]
    shard = w_attn_out.shape[1]
    ctx_local = context_kv.shape[2]
    teams = tp_count // TEAM
    team_width = TEAM * shard
    member = tp_index % TEAM
    z_count, x_count = 2 * TEAM, tp_count // (2 * TEAM)
    along_z = [[z_count * x + z for z in range(z_count)] for x in range(x_count)]
    along_x = [[z_count * x + z for x in range(x_count)] for z in range(z_count)]
    inside = [[TEAM * t + m for m in range(TEAM)] for t in range(teams)]
    shift_scale = modulation.reshape(3, 1, width)
    gains = qk_gain[0]
    weight_qkv = w_qkv[0].reshape(3 * shard, width)
    weight_mlp = w_mlp[0]
    weight_attn = w_attn_out[0]
    weight_down = w_mlp_out[0]

    half_team = TEAM // 2
    partner = [
        z + TEAM + half_team if z < half_team else z + half_team if z < TEAM
        else z - half_team if z < TEAM + half_team else z - TEAM - half_team
        for z in range(z_count)
    ]
    x_here, z_here = tp_index // z_count, tp_index % z_count
    z_partner = jnp.where(
        z_here < TEAM,
        z_here + jnp.where(z_here < half_team, TEAM + half_team, half_team),
        z_here - jnp.where(z_here < TEAM + half_team, half_team, TEAM + half_team),
    )
    upper = z_here >= TEAM
    slot = jnp.arange(teams * ctx_local, dtype=jnp.int32)
    within = slot % (2 * ctx_local)
    source = z_count * ((x_here - slot // (2 * ctx_local)) % x_count)
    source = source + jnp.where(within < ctx_local, z_here, z_partner)
    position = ctx_local * source + within % ctx_local
    cached_mask = ((position >= TXT) | (position < text_len[0])).astype(f32)
    cached_mask = jnp.broadcast_to(cached_mask[:, None], (teams * ctx_local, LANES))

    current = in_flight[0]
    block = spread(current, shift_scale, z_count)
    block, flat = lax.optimization_barrier((block, context_kv[0]))
    by_team = flat.reshape(2 * ctx_local, x_count, 2, team_width).transpose(2, 1, 0, 3)
    keep = jnp.where(upper, by_team[1], by_team[0])
    give = jnp.where(upper, by_team[0], by_team[1])
    got = lax.ppermute(
        give,
        "tp",
        [(z_count * x + z, z_count * x + partner[z]) for x in range(x_count) for z in range(z_count)],
    )

    for tick_number in range(TICKS):
        if tick_number:
            block = spread(current, shift_scale, z_count)
        normed = lax.all_to_all(block, "tp", 0, 0, axis_index_groups=along_z)
        normed = normed.reshape(rows * z_count, width)
        if tick_number == 0:
            normed, keep, got = lax.optimization_barrier((normed, keep, got))
            cached = []
            for step in range(x_count):
                target = (x_here + step) % x_count
                part = jnp.stack(
                    [lax.dynamic_index_in_dim(p, target, 0, keepdims=False) for p in (keep, got)]
                )
                if step:
                    route = [
                        (z_count * x + z, z_count * ((x + step) % x_count) + z)
                        for x in range(x_count) for z in range(z_count)
                    ]
                    part = lax.ppermute(part, "tp", route)
                cached.append(part)
        normed = gathered(normed, along_x)
        if tick_number == 0:
            normed, cached = lax.optimization_barrier((normed, cached))
        team = project(normed, weight_qkv)
        team = lax.all_to_all(team, "tp", 0, 0, axis_index_groups=inside)
        parts = attend(team, cached, cached_mask, gains)
        parts = lax.all_to_all(parts, "tp", 0, 0, axis_index_groups=inside)
        hidden = jax.nn.gelu(
            lax.dot_general(
                normed, weight_mlp, (((1,), (1,)), ((), ())), preferred_element_type=f32
            ),
            approximate=True,
        ).astype(bf16)
        hidden = lax.optimization_barrier(hidden)
        forward = jnp.dot(hidden, weight_down, preferred_element_type=f32)
        forward = lax.optimization_barrier(forward)
        branch = finish(member[None], parts, weight_attn, forward, shift_scale)
        branch = summed_over(branch, along_x)
        branch = summed_over(branch.reshape(-1, LANES), along_z).reshape(rows, width)
        finished = (current.astype(f32) + branch).astype(bf16)
        current = shifted(finished, "pipe", 1)
    return current[None]


def solution(mesh):
    placed = (
        P("pipe", "tp", None),
        P("pipe", None, "tp", None),
        P("pipe", "tp", None),
        P("pipe", "tp", None),
        P("pipe", "tp", None),
        P("pipe", None, None),
        P("pipe", None, None),
        P("pipe", None, "tp", None),
        P(),
    )
    return jax.shard_map(
        local, mesh=mesh, in_specs=placed, out_specs=P("pipe", "tp", None), check_vma=False
    )
```

```python
import jax
import jax.numpy as jnp
from jax import lax
from jax.experimental import pallas as pl
from jax.experimental.pallas import tpu as pltpu
from jax.sharding import PartitionSpec as P

HEADS = 24
HEAD_DIM = 128
TICKS = 2
TXT = 512
TEAM = 8
TEAM_HEADS = 3
LANES = 128

eps_norm = 1e-06
f32 = jnp.float32
bf16 = jnp.bfloat16


def shifted(block, axis, distance):
    size = lax.axis_size(axis)
    return lax.ppermute(block, axis, [((i - distance) % size, i) for i in range(size)])


def finish_kernel(member_ref, parts_ref, weight_ref, forward_ref, modulation_ref, out_ref):
    shard, width = weight_ref.shape
    summed = parts_ref[0].astype(f32)
    for c in range(1, parts_ref.shape[0]):
        summed = summed + parts_ref[c].astype(f32)
    feature = member_ref[0] * shard + lax.broadcasted_iota(jnp.int32, (shard, LANES), 0)
    total = jnp.broadcast_to(summed[shard + TEAM_HEADS - 1][None], (shard, LANES))
    for h in range(TEAM_HEADS - 2, -1, -1):
        total = jnp.where(feature < (h + 1) * HEAD_DIM, summed[shard + h][None], total)
    attention = (summed[:shard] / total).astype(bf16)
    branch = lax.dot_general(
        attention, weight_ref[...], (((0,), (0,)), ((), ())), preferred_element_type=f32
    )
    out_ref[...] = ((branch + forward_ref[...]) * modulation_ref[2]).astype(bf16)


def finish(member, parts, weights, forward, modulation):
    whole = pl.BlockSpec(memory_space=pltpu.VMEM)
    return pl.pallas_call(
        finish_kernel,
        out_shape=jax.ShapeDtypeStruct(forward.shape, bf16),
        in_specs=[pl.BlockSpec(memory_space=pltpu.SMEM)] + [whole] * 4,
        out_specs=whole,
        compiler_params=pltpu.CompilerParams(vmem_limit_bytes=16 * 1024 * 1024),
    )(member, parts, weights, forward, modulation)


def project_kernel(rows_ref, weight_ref, modulation_ref, out_ref, normed_ref):
    members = out_ref.shape[0]
    shard = weight_ref.shape[0] // 3
    for j in range(rows_ref.shape[0] // 16):
        x = rows_ref[16 * j : 16 * j + 16, :].astype(f32)
        centred = x - jnp.mean(x, axis=1, keepdims=True)
        variance = jnp.mean(centred * centred, axis=1, keepdims=True)
        normed = centred * lax.rsqrt(variance + eps_norm)
        normed = normed * (1.0 + modulation_ref[1]) + modulation_ref[0]
        normed_ref[16 * j : 16 * j + 16, :] = normed.astype(bf16)
    contract = (((1,), (1,)), ((), ()))
    query = lax.dot_general(
        weight_ref[:shard], normed_ref[...], contract, preferred_element_type=f32
    ).astype(bf16)
    others = lax.dot_general(
        normed_ref[...], weight_ref[shard:], contract, preferred_element_type=f32
    ).astype(bf16)
    for c in range(members):
        out_ref[c, :shard, :] = query
        out_ref[c, shard:, : 2 * shard] = others[16 * c : 16 * c + 16]
        out_ref[c, shard:, 2 * shard :] = jnp.zeros((16, LANES - 2 * shard), bf16)


def project(rows, weights, modulation):
    whole = pl.BlockSpec(memory_space=pltpu.VMEM)
    message = jax.ShapeDtypeStruct((TEAM, weights.shape[0] // 3 + 16, LANES), bf16)
    return pl.pallas_call(
        project_kernel,
        out_shape=(message, jax.ShapeDtypeStruct(rows.shape, bf16)),
        in_specs=[whole] * 3,
        out_specs=(whole, whole),
        compiler_params=pltpu.CompilerParams(vmem_limit_bytes=24 * 1024 * 1024),
    )(rows, weights, modulation)


def attend_kernel(
    team_ref, keep_ref, got_ref, mask_ref, gain_q_ref, gain_k_ref, out_ref, packed_ref
):
    shard = team_ref.shape[1] - 16
    members = team_ref.shape[0]
    lane = lax.broadcasted_iota(jnp.int32, (16, LANES), 1)
    row = lax.broadcasted_iota(jnp.int32, (16, LANES), 0)
    fresh = [team_ref[c, shard:, :].astype(f32) for c in range(members)]
    features = jnp.concatenate([team_ref[c, :shard, :] for c in range(members)], axis=0)
    open_key = mask_ref[...] > 0.0
    blocks = [r[i].astype(f32) for i in range(keep_ref.shape[0]) for r in (keep_ref, got_ref)]
    half = keep_ref.shape[1] // 2
    cached_keys = jnp.concatenate([b[:half] for b in blocks], axis=0).astype(bf16)
    cached_values = jnp.concatenate([b[half:] for b in blocks], axis=0).astype(bf16)
    sums = jnp.zeros((16, LANES), f32)
    for h in range(TEAM_HEADS):
        query = features[h * HEAD_DIM : (h + 1) * HEAD_DIM].astype(f32)
        scale = lax.rsqrt(jnp.mean(query * query, axis=0, keepdims=True) + eps_norm)
        query = (query * scale * gain_q_ref[...] * HEAD_DIM ** (-0.5)).astype(bf16)
        key = jnp.zeros((16, LANES), f32)
        value = jnp.zeros((16, LANES), f32)
        for c in range(members):
            start = c * shard - h * HEAD_DIM
            if start <= -shard or start >= HEAD_DIM:
                continue
            here = (lane >= start) & (lane < start + shard)
            key = jnp.where(here, pltpu.roll(fresh[c], start % LANES, 1), key)
            value = jnp.where(here, pltpu.roll(fresh[c], (start - shard) % LANES, 1), value)
        scale = lax.rsqrt(jnp.mean(key * key, axis=1, keepdims=True) + eps_norm)
        key = (key * scale * gain_k_ref[...]).astype(bf16)
        cached_key = cached_keys[:, h * HEAD_DIM : (h + 1) * HEAD_DIM]
        cached_value = cached_values[:, h * HEAD_DIM : (h + 1) * HEAD_DIM]
        scores = jnp.dot(cached_key, query, preferred_element_type=f32)
        probs = jnp.exp(jnp.where(open_key, scores, -1e30))
        fresh_probs = jnp.exp(jnp.dot(key, query, preferred_element_type=f32))
        total = jnp.sum(probs, axis=0, keepdims=True) + jnp.sum(fresh_probs, axis=0, keepdims=True)
        sums = jnp.where(row == h, total, sums)
        contract = (((0,), (0,)), ((), ()))
        weighted = lax.dot_general(
            cached_value, probs.astype(bf16), contract, preferred_element_type=f32
        ) + lax.dot_general(
            value.astype(bf16), fresh_probs.astype(bf16), contract, preferred_element_type=f32
        )
        packed_ref[h * HEAD_DIM : (h + 1) * HEAD_DIM, :] = weighted.astype(bf16)
    for c in range(members):
        out_ref[c, :shard, :] = packed_ref[c * shard : (c + 1) * shard, :]
        out_ref[c, shard:, :] = sums.astype(bf16)


def attend(team, keep, got, mask, gains):
    whole = pl.BlockSpec(memory_space=pltpu.VMEM)
    return pl.pallas_call(
        attend_kernel,
        out_shape=jax.ShapeDtypeStruct(team.shape, bf16),
        in_specs=[whole] * 6,
        out_specs=whole,
        scratch_shapes=[pltpu.VMEM((TEAM_HEADS * HEAD_DIM, LANES), bf16)],
        compiler_params=pltpu.CompilerParams(vmem_limit_bytes=16 * 1024 * 1024),
    )(team, keep, got, mask, gains[0][:, None], gains[1][None, :])


def gathered(block, groups):
    size = len(groups[0])
    spread = jnp.broadcast_to(block[None], (size,) + block.shape)
    spread = lax.all_to_all(spread, "tp", 0, 0, axis_index_groups=groups)
    return spread.reshape((size * block.shape[0],) + block.shape[1:])


def summed_over(block, groups):
    size = len(groups[0])
    parts = block.astype(bf16).reshape((size, block.shape[0] // size) + block.shape[1:])
    parts = lax.all_to_all(parts, "tp", 0, 0, axis_index_groups=groups)
    return jnp.sum(parts.astype(f32), axis=0)


def local(
    in_flight, w_qkv, w_mlp, w_attn_out, w_mlp_out, modulation, qk_gain, context_kv, text_len
):
    tp_count = lax.axis_size("tp")
    tp_index = lax.axis_index("tp")
    rows = in_flight.shape[1]
    tokens = rows * tp_count
    width = w_attn_out.shape[2]
    shard = w_attn_out.shape[1]
    ctx_local = context_kv.shape[2]
    teams = tp_count // TEAM
    team_width = TEAM * shard
    member = tp_index % TEAM
    z_count, x_count = 2 * TEAM, tp_count // (2 * TEAM)
    quads = z_count // 4

    def device(x, a, c, l):
        return z_count * x + 4 * a + 2 * c + l

    xs, quarters, two = range(x_count), range(quads), range(2)
    far = [[device(x, a, c, l) for c in two for a in quarters] for x in xs for l in two]
    blocks = [[device(x, a, c, l) for x in xs for l in two] for a in quarters for c in two]
    pairs = [[device(x, a, c, l) for c in two] for x in xs for l in two for a in quarters]
    quad = [[device(x, a, c, l) for a in quarters] for x in xs for l in two for c in two]
    inside = [[TEAM * t + m for m in range(TEAM)] for t in range(teams)]
    shift_scale = modulation.reshape(3, 1, width)
    gains = qk_gain[0]
    weight_qkv = w_qkv[0].reshape(3 * shard, width)
    weight_mlp = w_mlp[0]
    weight_attn = w_attn_out[0]
    weight_down = w_mlp_out[0]

    half_team = TEAM // 2
    partner = [
        z + TEAM + half_team if z < half_team else z + half_team if z < TEAM
        else z - half_team if z < TEAM + half_team else z - TEAM - half_team
        for z in range(z_count)
    ]
    x_here, z_here = tp_index // z_count, tp_index % z_count
    z_partner = jnp.where(
        z_here < TEAM,
        z_here + jnp.where(z_here < half_team, TEAM + half_team, half_team),
        z_here - jnp.where(z_here < TEAM + half_team, half_team, TEAM + half_team),
    )
    upper = z_here >= TEAM
    slot = jnp.arange(teams * ctx_local, dtype=jnp.int32)
    within = slot % (2 * ctx_local)
    source = z_count * ((x_here - slot // (2 * ctx_local)) % x_count)
    source = source + jnp.where(within < ctx_local, z_here, z_partner)
    position = ctx_local * source + within % ctx_local
    cached_mask = ((position >= TXT) | (position < text_len[0])).astype(f32)
    cached_mask = jnp.broadcast_to(cached_mask[:, None], (teams * ctx_local, LANES))

    current = in_flight[0]
    block = jnp.broadcast_to(
        current.reshape(1, rows * width // LANES, LANES), (2 * quads, rows * width // LANES, LANES)
    )
    block, flat = lax.optimization_barrier((block, context_kv[0]))
    flat = flat.reshape(2 * ctx_local, width)
    by_x = []
    for step in range(x_count):
        part = lax.dynamic_slice_in_dim(
            flat, (x_here + step) % x_count * 2 * team_width, 2 * team_width, 1
        )
        if step:
            route = [
                (z_count * x + z, z_count * ((x + step) % x_count) + z)
                for x in range(x_count) for z in range(z_count)
            ]
            part = lax.ppermute(part, "tp", route)
        by_x.append(part)
    by_x = jnp.stack(by_x)
    keep = jnp.where(upper, by_x[:, :, team_width:], by_x[:, :, :team_width])
    give = jnp.where(upper, by_x[:, :, :team_width], by_x[:, :, team_width:])

    first = 2 * quads * rows * (2 * x_here + z_here % 2) + quads * rows * (z_here // 2 % 2)
    eighth = lax.all_to_all(block, "tp", 0, 0, axis_index_groups=far).reshape(-1, width)
    for tick_number in range(TICKS):
        if tick_number == 0:
            eighth, give = lax.optimization_barrier((eighth, give))
            got = lax.ppermute(
                give,
                "tp",
                [(z_count * x + z, z_count * x + partner[z]) for x in range(x_count) for z in range(z_count)],
            )
        else:
            eighth = gathered(current, pairs)
        patch = gathered(eighth, blocks)
        if tick_number == 0:
            patch, got = lax.optimization_barrier((patch, got))
        team, normed = project(patch, weight_qkv, shift_scale)
        team = lax.all_to_all(team, "tp", 0, 0, axis_index_groups=inside)
        parts = attend(team, keep, got, cached_mask, gains)
        parts = lax.all_to_all(parts, "tp", 0, 0, axis_index_groups=inside)
        hidden = jax.nn.gelu(
            lax.dot_general(
                normed, weight_mlp, (((1,), (1,)), ((), ())), preferred_element_type=f32
            ),
            approximate=True,
        ).astype(bf16)
        hidden = lax.optimization_barrier(hidden)
        forward = jnp.dot(hidden, weight_down, preferred_element_type=f32)
        forward = lax.optimization_barrier(forward)
        branch = finish(member[None], parts, weight_attn, forward, shift_scale)
        branch = summed_over(branch, blocks).astype(bf16)
        if tick_number < TICKS - 1:
            branch = summed_over(branch, pairs).astype(bf16)
            branch = lax.all_to_all(
                jnp.broadcast_to(branch[None], (quads,) + branch.shape),
                "tp", 0, 0, axis_index_groups=quad,
            )
            branch = jnp.sum(branch.astype(f32), axis=0)
            residual = lax.dynamic_slice_in_dim(patch, first, quads * rows, 0)
        else:
            branch = summed_over(branch.reshape(-1, LANES), far).reshape(rows, width)
            residual = lax.dynamic_slice_in_dim(patch, first + rows * (z_here // 4), rows, 0)
        finished = (residual.astype(f32) + branch).astype(bf16)
        current = shifted(finished, "pipe", 1)
    return current[None]


def solution(mesh):
    placed = (
        P("pipe", "tp", None),
        P("pipe", None, "tp", None),
        P("pipe", "tp", None),
        P("pipe", "tp", None),
        P("pipe", "tp", None),
        P("pipe", None, None),
        P("pipe", None, None),
        P("pipe", None, "tp", None),
        P(),
    )
    return jax.shard_map(
        local, mesh=mesh, in_specs=placed, out_specs=P("pipe", "tp", None), check_vma=False
    )
```

```python
import jax
import jax.numpy as jnp
from jax import lax
from jax.experimental import pallas as pl
from jax.experimental.pallas import tpu as pltpu
from jax.sharding import PartitionSpec as P

HEADS = 24
HEAD_DIM = 128
TICKS = 2
TXT = 512
TEAM = 8
TEAM_HEADS = 3
LANES = 128

eps_norm = 1e-06
f32 = jnp.float32
bf16 = jnp.bfloat16


def shifted(block, axis, distance):
    size = lax.axis_size(axis)
    return lax.ppermute(block, axis, [((i - distance) % size, i) for i in range(size)])


def spread_kernel(rows_ref, modulation_ref, out_ref, block_ref):
    x = rows_ref[...].astype(f32)
    centred = x - jnp.mean(x, axis=1, keepdims=True)
    variance = jnp.mean(centred * centred, axis=1, keepdims=True)
    normed = centred * lax.rsqrt(variance + eps_norm)
    normed = normed * (1.0 + modulation_ref[1]) + modulation_ref[0]
    rows, width = x.shape
    pieces = width // LANES
    for r in range(rows):
        for p in range(pieces):
            at = r * pieces + p
            block_ref[at : at + 1, :] = normed[r : r + 1, p * LANES : (p + 1) * LANES]
    block = block_ref[...].astype(bf16)
    for j in range(out_ref.shape[0]):
        out_ref[j] = block


def spread(rows, modulation, receivers):
    whole = pl.BlockSpec(memory_space=pltpu.VMEM)
    lines = rows.shape[0] * rows.shape[1] // LANES
    return pl.pallas_call(
        spread_kernel,
        out_shape=jax.ShapeDtypeStruct((receivers, lines, LANES), bf16),
        in_specs=[whole] * 2,
        out_specs=whole,
        scratch_shapes=[pltpu.VMEM((lines, LANES), f32)],
        compiler_params=pltpu.CompilerParams(vmem_limit_bytes=8 * 1024 * 1024),
    )(rows, modulation)


def finish_kernel(member_ref, parts_ref, weight_ref, forward_ref, modulation_ref, out_ref):
    shard, width = weight_ref.shape
    summed = parts_ref[0].astype(f32)
    for c in range(1, parts_ref.shape[0]):
        summed = summed + parts_ref[c].astype(f32)
    feature = member_ref[0] * shard + lax.broadcasted_iota(jnp.int32, (shard, LANES), 0)
    total = jnp.broadcast_to(summed[shard + TEAM_HEADS - 1][None], (shard, LANES))
    for h in range(TEAM_HEADS - 2, -1, -1):
        total = jnp.where(feature < (h + 1) * HEAD_DIM, summed[shard + h][None], total)
    attention = (summed[:shard] / total).astype(bf16)
    branch = lax.dot_general(
        attention, weight_ref[...], (((0,), (0,)), ((), ())), preferred_element_type=f32
    )
    out_ref[...] = ((branch + forward_ref[...]) * modulation_ref[2]).astype(bf16)


def finish(member, parts, weights, forward, modulation):
    whole = pl.BlockSpec(memory_space=pltpu.VMEM)
    return pl.pallas_call(
        finish_kernel,
        out_shape=jax.ShapeDtypeStruct(forward.shape, bf16),
        in_specs=[pl.BlockSpec(memory_space=pltpu.SMEM)] + [whole] * 4,
        out_specs=whole,
        compiler_params=pltpu.CompilerParams(vmem_limit_bytes=8 * 1024 * 1024),
    )(member, parts, weights, forward, modulation)


def project_kernel(normed_ref, weight_ref, out_ref):
    members = out_ref.shape[0]
    shard = weight_ref.shape[0] // 3
    contract = (((1,), (1,)), ((), ()))
    query = lax.dot_general(
        weight_ref[:shard], normed_ref[...], contract, preferred_element_type=f32
    ).astype(bf16)
    others = lax.dot_general(
        normed_ref[...], weight_ref[shard:], contract, preferred_element_type=f32
    ).astype(bf16)
    for c in range(members):
        out_ref[c, :shard, :] = query
        out_ref[c, shard:, : 2 * shard] = others[16 * c : 16 * c + 16]
        out_ref[c, shard:, 2 * shard :] = jnp.zeros((16, LANES - 2 * shard), bf16)


def project(normed, weights):
    whole = pl.BlockSpec(memory_space=pltpu.VMEM)
    return pl.pallas_call(
        project_kernel,
        out_shape=jax.ShapeDtypeStruct((TEAM, weights.shape[0] // 3 + 16, LANES), bf16),
        in_specs=[whole] * 2,
        out_specs=whole,
        compiler_params=pltpu.CompilerParams(vmem_limit_bytes=8 * 1024 * 1024),
    )(normed, weights)


def attend_kernel(
    team_ref, keep_ref, got_ref, mask_ref, gain_q_ref, gain_k_ref, out_ref, packed_ref
):
    shard = team_ref.shape[1] - 16
    members = team_ref.shape[0]
    lane = lax.broadcasted_iota(jnp.int32, (16, LANES), 1)
    row = lax.broadcasted_iota(jnp.int32, (16, LANES), 0)
    fresh = [team_ref[c, shard:, :].astype(f32) for c in range(members)]
    features = jnp.concatenate([team_ref[c, :shard, :] for c in range(members)], axis=0)
    open_key = mask_ref[...] > 0.0
    blocks = [r[i].astype(f32) for i in range(keep_ref.shape[0]) for r in (keep_ref, got_ref)]
    half = keep_ref.shape[1] // 2
    cached_keys = jnp.concatenate([b[:half] for b in blocks], axis=0).astype(bf16)
    cached_values = jnp.concatenate([b[half:] for b in blocks], axis=0).astype(bf16)
    sums = jnp.zeros((16, LANES), f32)
    for h in range(TEAM_HEADS):
        query = features[h * HEAD_DIM : (h + 1) * HEAD_DIM].astype(f32)
        scale = lax.rsqrt(jnp.mean(query * query, axis=0, keepdims=True) + eps_norm)
        query = (query * scale * gain_q_ref[...] * HEAD_DIM ** (-0.5)).astype(bf16)
        key = jnp.zeros((16, LANES), f32)
        value = jnp.zeros((16, LANES), f32)
        for c in range(members):
            start = c * shard - h * HEAD_DIM
            if start <= -shard or start >= HEAD_DIM:
                continue
            here = (lane >= start) & (lane < start + shard)
            key = jnp.where(here, pltpu.roll(fresh[c], start % LANES, 1), key)
            value = jnp.where(here, pltpu.roll(fresh[c], (start - shard) % LANES, 1), value)
        scale = lax.rsqrt(jnp.mean(key * key, axis=1, keepdims=True) + eps_norm)
        key = (key * scale * gain_k_ref[...]).astype(bf16)
        cached_key = cached_keys[:, h * HEAD_DIM : (h + 1) * HEAD_DIM]
        cached_value = cached_values[:, h * HEAD_DIM : (h + 1) * HEAD_DIM]
        scores = jnp.dot(cached_key, query, preferred_element_type=f32)
        probs = jnp.exp(jnp.where(open_key, scores, -1e30))
        fresh_probs = jnp.exp(jnp.dot(key, query, preferred_element_type=f32))
        total = jnp.sum(probs, axis=0, keepdims=True) + jnp.sum(fresh_probs, axis=0, keepdims=True)
        sums = jnp.where(row == h, total, sums)
        contract = (((0,), (0,)), ((), ()))
        weighted = lax.dot_general(
            cached_value, probs.astype(bf16), contract, preferred_element_type=f32
        ) + lax.dot_general(
            value.astype(bf16), fresh_probs.astype(bf16), contract, preferred_element_type=f32
        )
        packed_ref[h * HEAD_DIM : (h + 1) * HEAD_DIM, :] = weighted.astype(bf16)
    for c in range(members):
        out_ref[c, :shard, :] = packed_ref[c * shard : (c + 1) * shard, :]
        out_ref[c, shard:, :] = sums.astype(bf16)


def attend(team, keep, got, mask, gains):
    whole = pl.BlockSpec(memory_space=pltpu.VMEM)
    return pl.pallas_call(
        attend_kernel,
        out_shape=jax.ShapeDtypeStruct(team.shape, bf16),
        in_specs=[whole] * 6,
        out_specs=whole,
        scratch_shapes=[pltpu.VMEM((TEAM_HEADS * HEAD_DIM, LANES), bf16)],
        compiler_params=pltpu.CompilerParams(vmem_limit_bytes=8 * 1024 * 1024),
    )(team, keep, got, mask, gains[0][:, None], gains[1][None, :])


def gathered(block, groups):
    size = len(groups[0])
    spread = jnp.broadcast_to(block[None], (size,) + block.shape)
    spread = lax.all_to_all(spread, "tp", 0, 0, axis_index_groups=groups)
    return spread.reshape((size * block.shape[0],) + block.shape[1:])


def summed_over(block, groups):
    size = len(groups[0])
    parts = block.astype(bf16).reshape((size, block.shape[0] // size) + block.shape[1:])
    parts = lax.all_to_all(parts, "tp", 0, 0, axis_index_groups=groups)
    return jnp.sum(parts.astype(f32), axis=0)


def local(
    in_flight, w_qkv, w_mlp, w_attn_out, w_mlp_out, modulation, qk_gain, context_kv, text_len
):
    tp_count = lax.axis_size("tp")
    tp_index = lax.axis_index("tp")
    rows = in_flight.shape[1]
    tokens = rows * tp_count
    width = w_attn_out.shape[2]
    shard = w_attn_out.shape[1]
    ctx_local = context_kv.shape[2]
    teams = tp_count // TEAM
    team_width = TEAM * shard
    member = tp_index % TEAM
    z_count, x_count = 2 * TEAM, tp_count // (2 * TEAM)
    xs, hs, two = range(x_count), range(z_count // 2), range(2)
    along_z = [[z_count * x + 2 * h + l for l in two for h in hs] for x in xs]
    along_x = [[z_count * x + z for x in xs] for z in range(z_count)]
    far = [[z_count * x + 2 * h + l for h in hs] for x in xs for l in two]
    blocks = [[z_count * x + 2 * h + l for x in xs for l in two] for h in hs]
    inside = [[TEAM * t + m for m in range(TEAM)] for t in range(teams)]
    shift_scale = modulation.reshape(3, 1, width)
    gains = qk_gain[0]
    weight_qkv = w_qkv[0].reshape(3 * shard, width)
    weight_mlp = w_mlp[0]
    weight_attn = w_attn_out[0]
    weight_down = w_mlp_out[0]

    half_team = TEAM // 2
    partner = [
        z + TEAM + half_team if z < half_team else z + half_team if z < TEAM
        else z - half_team if z < TEAM + half_team else z - TEAM - half_team
        for z in range(z_count)
    ]
    x_here, z_here = tp_index // z_count, tp_index % z_count
    z_partner = jnp.where(
        z_here < TEAM,
        z_here + jnp.where(z_here < half_team, TEAM + half_team, half_team),
        z_here - jnp.where(z_here < TEAM + half_team, half_team, TEAM + half_team),
    )
    upper = z_here >= TEAM
    slot = jnp.arange(teams * ctx_local, dtype=jnp.int32)
    within = slot % (2 * ctx_local)
    source = z_count * ((x_here - slot // (2 * ctx_local)) % x_count)
    source = source + jnp.where(within < ctx_local, z_here, z_partner)
    position = ctx_local * source + within % ctx_local
    cached_mask = ((position >= TXT) | (position < text_len[0])).astype(f32)
    cached_mask = jnp.broadcast_to(cached_mask[:, None], (teams * ctx_local, LANES))

    current = in_flight[0]
    block = spread(current, shift_scale, z_count)
    block, flat = lax.optimization_barrier((block, context_kv[0]))
    flat = flat.reshape(2 * ctx_local, width)
    by_x = []
    for step in range(x_count):
        part = lax.dynamic_slice_in_dim(
            flat, (x_here + step) % x_count * 2 * team_width, 2 * team_width, 1
        )
        if step:
            route = [
                (z_count * x + z, z_count * ((x + step) % x_count) + z)
                for x in range(x_count) for z in range(z_count)
            ]
            part = lax.ppermute(part, "tp", route)
        by_x.append(part)
    by_x = jnp.stack(by_x)
    keep = jnp.where(upper, by_x[:, :, team_width:], by_x[:, :, :team_width])
    give = jnp.where(upper, by_x[:, :, :team_width], by_x[:, :, team_width:])

    for tick_number in range(TICKS):
        if tick_number == 0:
            normed = lax.all_to_all(block, "tp", 0, 0, axis_index_groups=along_z)
            normed = normed.reshape(-1, width)
            normed, give = lax.optimization_barrier((normed, give))
            got = lax.ppermute(
                give,
                "tp",
                [(z_count * x + z, z_count * x + partner[z]) for x in range(x_count) for z in range(z_count)],
            )
            normed = gathered(normed, along_x)
            normed, got = lax.optimization_barrier((normed, got))
        else:
            block = spread(current, shift_scale, len(hs))
            normed = lax.all_to_all(block, "tp", 0, 0, axis_index_groups=far)
            normed = gathered(normed.reshape(-1, width), blocks)
        team = project(normed, weight_qkv)
        team = lax.all_to_all(team, "tp", 0, 0, axis_index_groups=inside)
        parts = attend(team, keep, got, cached_mask, gains)
        parts = lax.all_to_all(parts, "tp", 0, 0, axis_index_groups=inside)
        hidden = jax.nn.gelu(
            lax.dot_general(
                normed, weight_mlp, (((1,), (1,)), ((), ())), preferred_element_type=f32
            ),
            approximate=True,
        ).astype(bf16)
        hidden = lax.optimization_barrier(hidden)
        forward = jnp.dot(hidden, weight_down, preferred_element_type=f32)
        forward = lax.optimization_barrier(forward)
        branch = finish(member[None], parts, weight_attn, forward, shift_scale)
        branch = summed_over(branch, blocks)
        branch = summed_over(branch.reshape(-1, LANES), far).reshape(rows, width)
        finished = (current.astype(f32) + branch).astype(bf16)
        current = shifted(finished, "pipe", 1)
    return current[None]


def solution(mesh):
    placed = (
        P("pipe", "tp", None),
        P("pipe", None, "tp", None),
        P("pipe", "tp", None),
        P("pipe", "tp", None),
        P("pipe", "tp", None),
        P("pipe", None, None),
        P("pipe", None, None),
        P("pipe", None, "tp", None),
        P(),
    )
    return jax.shard_map(
        local, mesh=mesh, in_specs=placed, out_specs=P("pipe", "tp", None), check_vma=False
    )
```

```python
import jax
import jax.numpy as jnp
from jax import lax
from jax.experimental import pallas as pl
from jax.experimental.pallas import tpu as pltpu
from jax.sharding import PartitionSpec as P

HEADS = 24
HEAD_DIM = 128
TICKS = 2
TXT = 512
TEAM = 8
TEAM_HEADS = 3
LANES = 128

eps_norm = 1e-06
f32 = jnp.float32
bf16 = jnp.bfloat16


def shifted(block, axis, distance):
    size = lax.axis_size(axis)
    return lax.ppermute(block, axis, [((i - distance) % size, i) for i in range(size)])


def spread_kernel(rows_ref, modulation_ref, out_ref, block_ref):
    x = rows_ref[...].astype(f32)
    centred = x - jnp.mean(x, axis=1, keepdims=True)
    variance = jnp.mean(centred * centred, axis=1, keepdims=True)
    normed = centred * lax.rsqrt(variance + eps_norm)
    normed = normed * (1.0 + modulation_ref[1]) + modulation_ref[0]
    rows, width = x.shape
    pieces = width // LANES
    for r in range(rows):
        for p in range(pieces):
            at = r * pieces + p
            block_ref[at : at + 1, :] = normed[r : r + 1, p * LANES : (p + 1) * LANES]
    block = block_ref[...].astype(bf16)
    for j in range(out_ref.shape[0]):
        out_ref[j] = block


def spread(rows, modulation, receivers):
    whole = pl.BlockSpec(memory_space=pltpu.VMEM)
    lines = rows.shape[0] * rows.shape[1] // LANES
    return pl.pallas_call(
        spread_kernel,
        out_shape=jax.ShapeDtypeStruct((receivers, lines, LANES), bf16),
        in_specs=[whole] * 2,
        out_specs=whole,
        scratch_shapes=[pltpu.VMEM((lines, LANES), f32)],
        compiler_params=pltpu.CompilerParams(vmem_limit_bytes=8 * 1024 * 1024),
    )(rows, modulation)


def finish_kernel(member_ref, parts_ref, weight_ref, forward_ref, modulation_ref, out_ref):
    shard, width = weight_ref.shape
    summed = parts_ref[0].astype(f32)
    for c in range(1, parts_ref.shape[0]):
        summed = summed + parts_ref[c].astype(f32)
    feature = member_ref[0] * shard + lax.broadcasted_iota(jnp.int32, (shard, LANES), 0)
    total = jnp.broadcast_to(summed[shard + TEAM_HEADS - 1][None], (shard, LANES))
    for h in range(TEAM_HEADS - 2, -1, -1):
        total = jnp.where(feature < (h + 1) * HEAD_DIM, summed[shard + h][None], total)
    attention = (summed[:shard] / total).astype(bf16)
    branch = lax.dot_general(
        attention, weight_ref[...], (((0,), (0,)), ((), ())), preferred_element_type=f32
    )
    out_ref[...] = ((branch + forward_ref[...]) * modulation_ref[2]).astype(bf16)


def finish(member, parts, weights, forward, modulation):
    whole = pl.BlockSpec(memory_space=pltpu.VMEM)
    return pl.pallas_call(
        finish_kernel,
        out_shape=jax.ShapeDtypeStruct(forward.shape, bf16),
        in_specs=[pl.BlockSpec(memory_space=pltpu.SMEM)] + [whole] * 4,
        out_specs=whole,
        compiler_params=pltpu.CompilerParams(vmem_limit_bytes=8 * 1024 * 1024),
    )(member, parts, weights, forward, modulation)


def project_kernel(normed_ref, weight_ref, out_ref):
    members = out_ref.shape[0]
    shard = weight_ref.shape[0] // 3
    contract = (((1,), (1,)), ((), ()))
    query = lax.dot_general(
        weight_ref[:shard], normed_ref[...], contract, preferred_element_type=f32
    ).astype(bf16)
    others = lax.dot_general(
        normed_ref[...], weight_ref[shard:], contract, preferred_element_type=f32
    ).astype(bf16)
    for c in range(members):
        out_ref[c, :shard, :] = query
        out_ref[c, shard:, : 2 * shard] = others[16 * c : 16 * c + 16]
        out_ref[c, shard:, 2 * shard :] = jnp.zeros((16, LANES - 2 * shard), bf16)


def project(normed, weights):
    whole = pl.BlockSpec(memory_space=pltpu.VMEM)
    return pl.pallas_call(
        project_kernel,
        out_shape=jax.ShapeDtypeStruct((TEAM, weights.shape[0] // 3 + 16, LANES), bf16),
        in_specs=[whole] * 2,
        out_specs=whole,
        compiler_params=pltpu.CompilerParams(vmem_limit_bytes=8 * 1024 * 1024),
    )(normed, weights)


def attend_kernel(team_ref, mask_ref, gain_q_ref, gain_k_ref, *refs):
    *cached_refs, out_ref, packed_ref = refs
    shard = team_ref.shape[1] - 16
    members = team_ref.shape[0]
    lane = lax.broadcasted_iota(jnp.int32, (16, LANES), 1)
    row = lax.broadcasted_iota(jnp.int32, (16, LANES), 0)
    fresh = [team_ref[c, shard:, :].astype(f32) for c in range(members)]
    features = jnp.concatenate([team_ref[c, :shard, :] for c in range(members)], axis=0)
    open_key = mask_ref[...] > 0.0
    blocks = [r[i].astype(f32) for r in cached_refs for i in range(r.shape[0])]
    half = blocks[0].shape[0] // 2
    cached_keys = jnp.concatenate([b[:half] for b in blocks], axis=0).astype(bf16)
    cached_values = jnp.concatenate([b[half:] for b in blocks], axis=0).astype(bf16)
    sums = jnp.zeros((16, LANES), f32)
    for h in range(TEAM_HEADS):
        query = features[h * HEAD_DIM : (h + 1) * HEAD_DIM].astype(f32)
        scale = lax.rsqrt(jnp.mean(query * query, axis=0, keepdims=True) + eps_norm)
        query = (query * scale * gain_q_ref[...] * HEAD_DIM ** (-0.5)).astype(bf16)
        key = jnp.zeros((16, LANES), f32)
        value = jnp.zeros((16, LANES), f32)
        for c in range(members):
            start = c * shard - h * HEAD_DIM
            if start <= -shard or start >= HEAD_DIM:
                continue
            here = (lane >= start) & (lane < start + shard)
            key = jnp.where(here, pltpu.roll(fresh[c], start % LANES, 1), key)
            value = jnp.where(here, pltpu.roll(fresh[c], (start - shard) % LANES, 1), value)
        scale = lax.rsqrt(jnp.mean(key * key, axis=1, keepdims=True) + eps_norm)
        key = (key * scale * gain_k_ref[...]).astype(bf16)
        cached_key = cached_keys[:, h * HEAD_DIM : (h + 1) * HEAD_DIM]
        cached_value = cached_values[:, h * HEAD_DIM : (h + 1) * HEAD_DIM]
        scores = jnp.dot(cached_key, query, preferred_element_type=f32)
        probs = jnp.exp(jnp.where(open_key, scores, -1e30))
        fresh_probs = jnp.exp(jnp.dot(key, query, preferred_element_type=f32))
        total = jnp.sum(probs, axis=0, keepdims=True) + jnp.sum(fresh_probs, axis=0, keepdims=True)
        sums = jnp.where(row == h, total, sums)
        contract = (((0,), (0,)), ((), ()))
        weighted = lax.dot_general(
            cached_value, probs.astype(bf16), contract, preferred_element_type=f32
        ) + lax.dot_general(
            value.astype(bf16), fresh_probs.astype(bf16), contract, preferred_element_type=f32
        )
        packed_ref[h * HEAD_DIM : (h + 1) * HEAD_DIM, :] = weighted.astype(bf16)
    for c in range(members):
        out_ref[c, :shard, :] = packed_ref[c * shard : (c + 1) * shard, :]
        out_ref[c, shard:, :] = sums.astype(bf16)


def attend(team, cached, mask, gains):
    whole = pl.BlockSpec(memory_space=pltpu.VMEM)
    return pl.pallas_call(
        attend_kernel,
        out_shape=jax.ShapeDtypeStruct(team.shape, bf16),
        in_specs=[whole] * (4 + len(cached)),
        out_specs=whole,
        scratch_shapes=[pltpu.VMEM((TEAM_HEADS * HEAD_DIM, LANES), bf16)],
        compiler_params=pltpu.CompilerParams(vmem_limit_bytes=8 * 1024 * 1024),
    )(team, mask, gains[0][:, None], gains[1][None, :], *cached)


def gathered(block, groups):
    size = len(groups[0])
    spread = jnp.broadcast_to(block[None], (size,) + block.shape)
    spread = lax.all_to_all(spread, "tp", 0, 0, axis_index_groups=groups)
    return spread.reshape((size * block.shape[0],) + block.shape[1:])


def summed_over(block, groups):
    size = len(groups[0])
    parts = block.astype(bf16).reshape((size, block.shape[0] // size) + block.shape[1:])
    parts = lax.all_to_all(parts, "tp", 0, 0, axis_index_groups=groups)
    return jnp.sum(parts.astype(f32), axis=0)


def local(
    in_flight, w_qkv, w_mlp, w_attn_out, w_mlp_out, modulation, qk_gain, context_kv, text_len
):
    tp_count = lax.axis_size("tp")
    tp_index = lax.axis_index("tp")
    rows = in_flight.shape[1]
    tokens = rows * tp_count
    width = w_attn_out.shape[2]
    shard = w_attn_out.shape[1]
    ctx_local = context_kv.shape[2]
    teams = tp_count // TEAM
    team_width = TEAM * shard
    member = tp_index % TEAM
    z_count, x_count = 2 * TEAM, tp_count // (2 * TEAM)
    xs, hs, two = range(x_count), range(z_count // 2), range(2)
    along_z = [[z_count * x + 2 * h + l for l in two for h in hs] for x in xs]
    along_x = [[z_count * x + z for x in xs] for z in range(z_count)]
    far = [[z_count * x + 2 * h + l for h in hs] for x in xs for l in two]
    blocks = [[z_count * x + 2 * h + l for x in xs for l in two] for h in hs]
    inside = [[TEAM * t + m for m in range(TEAM)] for t in range(teams)]
    shift_scale = modulation.reshape(3, 1, width)
    gains = qk_gain[0]
    weight_qkv = w_qkv[0].reshape(3 * shard, width)
    weight_mlp = w_mlp[0]
    weight_attn = w_attn_out[0]
    weight_down = w_mlp_out[0]

    half_team = TEAM // 2
    partner = [
        z + TEAM + half_team if z < half_team else z + half_team if z < TEAM
        else z - half_team if z < TEAM + half_team else z - TEAM - half_team
        for z in range(z_count)
    ]
    x_here, z_here = tp_index // z_count, tp_index % z_count
    z_partner = jnp.where(
        z_here < TEAM,
        z_here + jnp.where(z_here < half_team, TEAM + half_team, half_team),
        z_here - jnp.where(z_here < TEAM + half_team, half_team, TEAM + half_team),
    )
    upper = z_here >= TEAM
    slot = jnp.arange(teams * ctx_local, dtype=jnp.int32)
    own_z = slot < x_count * ctx_local
    source = z_count * ((x_here - slot // ctx_local % x_count) % x_count)
    source = source + jnp.where(own_z, z_here, z_partner)
    position = ctx_local * source + slot % ctx_local
    cached_mask = ((position >= TXT) | (position < text_len[0])).astype(f32)
    cached_mask = jnp.broadcast_to(cached_mask[:, None], (teams * ctx_local, LANES))

    current = in_flight[0]
    block = spread(current, shift_scale, z_count)
    block, flat = lax.optimization_barrier((block, context_kv[0]))
    flat = flat.reshape(2 * ctx_local, width)
    by_x = []
    for step in range(x_count):
        part = lax.dynamic_slice_in_dim(
            flat, (x_here + step) % x_count * 2 * team_width, 2 * team_width, 1
        )
        if step:
            route = [
                (z_count * x + z, z_count * ((x + step) % x_count) + z)
                for x in range(x_count) for z in range(z_count)
            ]
            part = lax.ppermute(part, "tp", route)
        by_x.append(part)
    by_x = jnp.stack(by_x)
    keep = jnp.where(upper, by_x[:, :, team_width:], by_x[:, :, :team_width])
    give = jnp.where(upper, by_x[:, :, :team_width], by_x[:, :, team_width:])

    for tick_number in range(TICKS):
        if tick_number == 0:
            normed = lax.all_to_all(block, "tp", 0, 0, axis_index_groups=along_z)
            normed = normed.reshape(-1, width)
            normed, give = lax.optimization_barrier((normed, give))
            route = [(z_count * x + z, z_count * x + partner[z]) for x in xs for z in range(z_count)]
            got = [
                lax.ppermute(part, "tp", route)
                for part in (give[: x_count // 2], give[x_count // 2 :])
            ]
            normed = gathered(normed, along_x)
            normed, got[0] = lax.optimization_barrier((normed, got[0]))
            cached = [keep] + got
        else:
            block = spread(current, shift_scale, len(hs))
            normed = lax.all_to_all(block, "tp", 0, 0, axis_index_groups=far)
            normed = gathered(normed.reshape(-1, width), blocks)
        team = project(normed, weight_qkv)
        team = lax.all_to_all(team, "tp", 0, 0, axis_index_groups=inside)
        parts = attend(team, cached, cached_mask, gains)
        parts = lax.all_to_all(parts, "tp", 0, 0, axis_index_groups=inside)
        hidden = jax.nn.gelu(
            lax.dot_general(
                normed, weight_mlp, (((1,), (1,)), ((), ())), preferred_element_type=f32
            ),
            approximate=True,
        ).astype(bf16)
        hidden = lax.optimization_barrier(hidden)
        forward = jnp.dot(hidden, weight_down, preferred_element_type=f32)
        forward = lax.optimization_barrier(forward)
        branch = finish(member[None], parts, weight_attn, forward, shift_scale)
        branch = summed_over(branch, blocks)
        branch = summed_over(branch.reshape(-1, LANES), far).reshape(rows, width)
        finished = (current.astype(f32) + branch).astype(bf16)
        current = shifted(finished, "pipe", 1)
    return current[None]


def solution(mesh):
    placed = (
        P("pipe", "tp", None),
        P("pipe", None, "tp", None),
        P("pipe", "tp", None),
        P("pipe", "tp", None),
        P("pipe", "tp", None),
        P("pipe", None, None),
        P("pipe", None, None),
        P("pipe", None, "tp", None),
        P(),
    )
    return jax.shard_map(
        local, mesh=mesh, in_specs=placed, out_specs=P("pipe", "tp", None), check_vma=False
    )
```

```python
import jax
import jax.numpy as jnp
from jax import lax
from jax.experimental import pallas as pl
from jax.experimental.pallas import tpu as pltpu
from jax.sharding import PartitionSpec as P

HEADS = 24
HEAD_DIM = 128
TICKS = 2
TXT = 512
TEAM = 8
TEAM_HEADS = 3
LANES = 128

eps_norm = 1e-06
f32 = jnp.float32
bf16 = jnp.bfloat16


def shifted(block, axis, distance):
    size = lax.axis_size(axis)
    return lax.ppermute(block, axis, [((i - distance) % size, i) for i in range(size)])


def spread_kernel(rows_ref, modulation_ref, out_ref, block_ref):
    x = rows_ref[...].astype(f32)
    centred = x - jnp.mean(x, axis=1, keepdims=True)
    variance = jnp.mean(centred * centred, axis=1, keepdims=True)
    normed = centred * lax.rsqrt(variance + eps_norm)
    normed = normed * (1.0 + modulation_ref[1]) + modulation_ref[0]
    rows, width = x.shape
    pieces = width // LANES
    for r in range(rows):
        for p in range(pieces):
            at = r * pieces + p
            block_ref[at : at + 1, :] = normed[r : r + 1, p * LANES : (p + 1) * LANES]
    block = block_ref[...].astype(bf16)
    for j in range(out_ref.shape[0]):
        out_ref[j] = block


def spread(rows, modulation, receivers):
    whole = pl.BlockSpec(memory_space=pltpu.VMEM)
    lines = rows.shape[0] * rows.shape[1] // LANES
    return pl.pallas_call(
        spread_kernel,
        out_shape=jax.ShapeDtypeStruct((receivers, lines, LANES), bf16),
        in_specs=[whole] * 2,
        out_specs=whole,
        scratch_shapes=[pltpu.VMEM((lines, LANES), f32)],
        compiler_params=pltpu.CompilerParams(vmem_limit_bytes=8 * 1024 * 1024),
    )(rows, modulation)


def finish_kernel(member_ref, parts_ref, weight_ref, forward_ref, modulation_ref, out_ref):
    shard, width = weight_ref.shape
    summed = parts_ref[0].astype(f32)
    for c in range(1, parts_ref.shape[0]):
        summed = summed + parts_ref[c].astype(f32)
    feature = member_ref[0] * shard + lax.broadcasted_iota(jnp.int32, (shard, LANES), 0)
    total = jnp.broadcast_to(summed[shard + TEAM_HEADS - 1][None], (shard, LANES))
    for h in range(TEAM_HEADS - 2, -1, -1):
        total = jnp.where(feature < (h + 1) * HEAD_DIM, summed[shard + h][None], total)
    attention = (summed[:shard] / total).astype(bf16)
    branch = lax.dot_general(
        attention, weight_ref[...], (((0,), (0,)), ((), ())), preferred_element_type=f32
    )
    out_ref[...] = ((branch + forward_ref[...]) * modulation_ref[2]).astype(bf16)


def finish(member, parts, weights, forward, modulation):
    whole = pl.BlockSpec(memory_space=pltpu.VMEM)
    return pl.pallas_call(
        finish_kernel,
        out_shape=jax.ShapeDtypeStruct(forward.shape, bf16),
        in_specs=[pl.BlockSpec(memory_space=pltpu.SMEM)] + [whole] * 4,
        out_specs=whole,
        compiler_params=pltpu.CompilerParams(vmem_limit_bytes=8 * 1024 * 1024),
    )(member, parts, weights, forward, modulation)


def project_kernel(normed_ref, weight_ref, out_ref):
    members = out_ref.shape[0]
    shard = weight_ref.shape[0] // 3
    contract = (((1,), (1,)), ((), ()))
    query = lax.dot_general(
        weight_ref[:shard], normed_ref[...], contract, preferred_element_type=f32
    ).astype(bf16)
    others = lax.dot_general(
        normed_ref[...], weight_ref[shard:], contract, preferred_element_type=f32
    ).astype(bf16)
    for c in range(members):
        out_ref[c, :shard, :] = query
        out_ref[c, shard:, : 2 * shard] = others[16 * c : 16 * c + 16]
        out_ref[c, shard:, 2 * shard :] = jnp.zeros((16, LANES - 2 * shard), bf16)


def project(normed, weights):
    whole = pl.BlockSpec(memory_space=pltpu.VMEM)
    return pl.pallas_call(
        project_kernel,
        out_shape=jax.ShapeDtypeStruct((TEAM, weights.shape[0] // 3 + 16, LANES), bf16),
        in_specs=[whole] * 2,
        out_specs=whole,
        compiler_params=pltpu.CompilerParams(vmem_limit_bytes=8 * 1024 * 1024),
    )(normed, weights)


def attend_kernel(team_ref, mask_ref, gain_q_ref, gain_k_ref, *refs):
    *cached_refs, out_ref, packed_ref = refs
    shard = team_ref.shape[1] - 16
    members = team_ref.shape[0]
    lane = lax.broadcasted_iota(jnp.int32, (16, LANES), 1)
    row = lax.broadcasted_iota(jnp.int32, (16, LANES), 0)
    fresh = [team_ref[c, shard:, :].astype(f32) for c in range(members)]
    features = jnp.concatenate([team_ref[c, :shard, :] for c in range(members)], axis=0)
    open_key = mask_ref[...] > 0.0
    blocks = [r[i].astype(f32) for r in cached_refs for i in range(r.shape[0])]
    half = blocks[0].shape[0] // 2
    cached_keys = jnp.concatenate([b[:half] for b in blocks], axis=0).astype(bf16)
    cached_values = jnp.concatenate([b[half:] for b in blocks], axis=0).astype(bf16)
    sums = jnp.zeros((16, LANES), f32)
    for h in range(TEAM_HEADS):
        query = features[h * HEAD_DIM : (h + 1) * HEAD_DIM].astype(f32)
        scale = lax.rsqrt(jnp.mean(query * query, axis=0, keepdims=True) + eps_norm)
        query = (query * scale * gain_q_ref[...] * HEAD_DIM ** (-0.5)).astype(bf16)
        key = jnp.zeros((16, LANES), f32)
        value = jnp.zeros((16, LANES), f32)
        for c in range(members):
            start = c * shard - h * HEAD_DIM
            if start <= -shard or start >= HEAD_DIM:
                continue
            here = (lane >= start) & (lane < start + shard)
            key = jnp.where(here, pltpu.roll(fresh[c], start % LANES, 1), key)
            value = jnp.where(here, pltpu.roll(fresh[c], (start - shard) % LANES, 1), value)
        scale = lax.rsqrt(jnp.mean(key * key, axis=1, keepdims=True) + eps_norm)
        key = (key * scale * gain_k_ref[...]).astype(bf16)
        cached_key = cached_keys[:, h * HEAD_DIM : (h + 1) * HEAD_DIM]
        cached_value = cached_values[:, h * HEAD_DIM : (h + 1) * HEAD_DIM]
        scores = jnp.dot(cached_key, query, preferred_element_type=f32)
        probs = jnp.exp(jnp.where(open_key, scores, -1e30))
        fresh_probs = jnp.exp(jnp.dot(key, query, preferred_element_type=f32))
        total = jnp.sum(probs, axis=0, keepdims=True) + jnp.sum(fresh_probs, axis=0, keepdims=True)
        sums = jnp.where(row == h, total, sums)
        contract = (((0,), (0,)), ((), ()))
        weighted = lax.dot_general(
            cached_value, probs.astype(bf16), contract, preferred_element_type=f32
        ) + lax.dot_general(
            value.astype(bf16), fresh_probs.astype(bf16), contract, preferred_element_type=f32
        )
        packed_ref[h * HEAD_DIM : (h + 1) * HEAD_DIM, :] = weighted.astype(bf16)
    for c in range(members):
        out_ref[c, :shard, :] = packed_ref[c * shard : (c + 1) * shard, :]
        out_ref[c, shard:, :] = sums.astype(bf16)


def attend(team, cached, mask, gains):
    whole = pl.BlockSpec(memory_space=pltpu.VMEM)
    return pl.pallas_call(
        attend_kernel,
        out_shape=jax.ShapeDtypeStruct(team.shape, bf16),
        in_specs=[whole] * (4 + len(cached)),
        out_specs=whole,
        scratch_shapes=[pltpu.VMEM((TEAM_HEADS * HEAD_DIM, LANES), bf16)],
        compiler_params=pltpu.CompilerParams(vmem_limit_bytes=8 * 1024 * 1024),
    )(team, mask, gains[0][:, None], gains[1][None, :], *cached)


def gathered(block, groups):
    size = len(groups[0])
    spread = jnp.broadcast_to(block[None], (size,) + block.shape)
    spread = lax.all_to_all(spread, "tp", 0, 0, axis_index_groups=groups)
    return spread.reshape((size * block.shape[0],) + block.shape[1:])


def summed_over(block, groups):
    size = len(groups[0])
    parts = block.astype(bf16).reshape((size, block.shape[0] // size) + block.shape[1:])
    parts = lax.all_to_all(parts, "tp", 0, 0, axis_index_groups=groups)
    return jnp.sum(parts.astype(f32), axis=0)


def local(
    in_flight, w_qkv, w_mlp, w_attn_out, w_mlp_out, modulation, qk_gain, context_kv, text_len
):
    tp_count = lax.axis_size("tp")
    tp_index = lax.axis_index("tp")
    rows = in_flight.shape[1]
    tokens = rows * tp_count
    width = w_attn_out.shape[2]
    shard = w_attn_out.shape[1]
    ctx_local = context_kv.shape[2]
    teams = tp_count // TEAM
    team_width = TEAM * shard
    member = tp_index % TEAM
    z_count, x_count = 2 * TEAM, tp_count // (2 * TEAM)
    xs, hs, two = range(x_count), range(z_count // 2), range(2)
    along_z = [[z_count * x + 2 * h + l for l in two for h in hs] for x in xs]
    along_x = [[z_count * x + z for x in xs] for z in range(z_count)]
    far = [[z_count * x + 2 * h + l for h in hs] for x in xs for l in two]
    blocks = [[z_count * x + 2 * h + l for x in xs for l in two] for h in hs]
    inside = [[TEAM * t + m for m in range(TEAM)] for t in range(teams)]
    shift_scale = modulation.reshape(3, 1, width)
    gains = qk_gain[0]
    weight_qkv = w_qkv[0].reshape(3 * shard, width)
    weight_mlp = w_mlp[0]
    weight_attn = w_attn_out[0]
    weight_down = w_mlp_out[0]

    half_team = TEAM // 2
    partner = [
        z + TEAM + half_team if z < half_team else z + half_team if z < TEAM
        else z - half_team if z < TEAM + half_team else z - TEAM - half_team
        for z in range(z_count)
    ]
    x_here, z_here = tp_index // z_count, tp_index % z_count
    z_partner = jnp.where(
        z_here < TEAM,
        z_here + jnp.where(z_here < half_team, TEAM + half_team, half_team),
        z_here - jnp.where(z_here < TEAM + half_team, half_team, TEAM + half_team),
    )
    upper = z_here >= TEAM
    slot = jnp.arange(teams * ctx_local, dtype=jnp.int32)
    own_z = slot < x_count * ctx_local
    source = z_count * ((x_here - slot // ctx_local % x_count) % x_count)
    source = source + jnp.where(own_z, z_here, z_partner)
    position = ctx_local * source + slot % ctx_local
    cached_mask = ((position >= TXT) | (position < text_len[0])).astype(f32)
    cached_mask = jnp.broadcast_to(cached_mask[:, None], (teams * ctx_local, LANES))

    current = in_flight[0]
    block = spread(current, shift_scale, z_count)
    block, flat = lax.optimization_barrier((block, context_kv[0]))
    flat = flat.reshape(2 * ctx_local, width)
    by_x = []
    for step in range(x_count):
        part = lax.dynamic_slice_in_dim(
            flat, (x_here + step) % x_count * 2 * team_width, 2 * team_width, 1
        )
        if step:
            route = [
                (z_count * x + z, z_count * ((x + step) % x_count) + z)
                for x in range(x_count) for z in range(z_count)
            ]
            part = lax.ppermute(part, "tp", route)
        by_x.append(part)
    by_x = jnp.stack(by_x)
    keep = jnp.where(upper, by_x[:, :, team_width:], by_x[:, :, :team_width])
    give = jnp.where(upper, by_x[:, :, :team_width], by_x[:, :, team_width:])

    for tick_number in range(TICKS):
        if tick_number == 0:
            normed = lax.all_to_all(block, "tp", 0, 0, axis_index_groups=along_z)
            normed = normed.reshape(-1, width)
            route = [(z_count * x + z, z_count * x + partner[z]) for x in xs for z in range(z_count)]
            got = [
                lax.ppermute(part, "tp", route)
                for part in (give[: x_count // 2], give[x_count // 2 :])
            ]
            normed = gathered(normed, along_x)
            normed, got[0] = lax.optimization_barrier((normed, got[0]))
            cached = [keep] + got
        else:
            block = spread(current, shift_scale, len(hs))
            normed = lax.all_to_all(block, "tp", 0, 0, axis_index_groups=far)
            normed = gathered(normed.reshape(-1, width), blocks)
        team = project(normed, weight_qkv)
        team = lax.all_to_all(team, "tp", 0, 0, axis_index_groups=inside)
        parts = attend(team, cached, cached_mask, gains)
        parts = lax.all_to_all(parts, "tp", 0, 0, axis_index_groups=inside)
        hidden = jax.nn.gelu(
            lax.dot_general(
                normed, weight_mlp, (((1,), (1,)), ((), ())), preferred_element_type=f32
            ),
            approximate=True,
        ).astype(bf16)
        hidden = lax.optimization_barrier(hidden)
        forward = jnp.dot(hidden, weight_down, preferred_element_type=f32)
        forward = lax.optimization_barrier(forward)
        branch = finish(member[None], parts, weight_attn, forward, shift_scale)
        branch = summed_over(branch, blocks)
        branch = summed_over(branch.reshape(-1, LANES), far).reshape(rows, width)
        finished = (current.astype(f32) + branch).astype(bf16)
        current = shifted(finished, "pipe", 1)
    return current[None]


def solution(mesh):
    placed = (
        P("pipe", "tp", None),
        P("pipe", None, "tp", None),
        P("pipe", "tp", None),
        P("pipe", "tp", None),
        P("pipe", "tp", None),
        P("pipe", None, None),
        P("pipe", None, None),
        P("pipe", None, "tp", None),
        P(),
    )
    return jax.shard_map(
        local, mesh=mesh, in_specs=placed, out_specs=P("pipe", "tp", None), check_vma=False
    )
```

```python
import jax
import jax.numpy as jnp
from jax import lax
from jax.experimental import pallas as pl
from jax.experimental.pallas import tpu as pltpu
from jax.sharding import PartitionSpec as P

HEADS = 24
HEAD_DIM = 128
TICKS = 2
TXT = 512
TEAM = 8
TEAM_HEADS = 3
LANES = 128

eps_norm = 1e-06
f32 = jnp.float32
bf16 = jnp.bfloat16


def shifted(block, axis, distance):
    size = lax.axis_size(axis)
    return lax.ppermute(block, axis, [((i - distance) % size, i) for i in range(size)])


def spread_kernel(rows_ref, modulation_ref, out_ref, block_ref):
    x = rows_ref[...].astype(f32)
    centred = x - jnp.mean(x, axis=1, keepdims=True)
    variance = jnp.mean(centred * centred, axis=1, keepdims=True)
    normed = centred * lax.rsqrt(variance + eps_norm)
    normed = normed * (1.0 + modulation_ref[1]) + modulation_ref[0]
    rows, width = x.shape
    pieces = width // LANES
    for r in range(rows):
        for p in range(pieces):
            at = r * pieces + p
            block_ref[at : at + 1, :] = normed[r : r + 1, p * LANES : (p + 1) * LANES]
    block = block_ref[...].astype(bf16)
    for j in range(out_ref.shape[0]):
        out_ref[j] = block


def spread(rows, modulation, receivers):
    whole = pl.BlockSpec(memory_space=pltpu.VMEM)
    lines = rows.shape[0] * rows.shape[1] // LANES
    return pl.pallas_call(
        spread_kernel,
        out_shape=jax.ShapeDtypeStruct((receivers, lines, LANES), bf16),
        in_specs=[whole] * 2,
        out_specs=whole,
        scratch_shapes=[pltpu.VMEM((lines, LANES), f32)],
        compiler_params=pltpu.CompilerParams(vmem_limit_bytes=8 * 1024 * 1024),
    )(rows, modulation)


def finish_kernel(member_ref, parts_ref, weight_ref, forward_ref, modulation_ref, out_ref):
    shard, width = weight_ref.shape
    summed = parts_ref[0].astype(f32)
    for c in range(1, parts_ref.shape[0]):
        summed = summed + parts_ref[c].astype(f32)
    feature = member_ref[0] * shard + lax.broadcasted_iota(jnp.int32, (shard, LANES), 0)
    total = jnp.broadcast_to(summed[shard + TEAM_HEADS - 1][None], (shard, LANES))
    for h in range(TEAM_HEADS - 2, -1, -1):
        total = jnp.where(feature < (h + 1) * HEAD_DIM, summed[shard + h][None], total)
    attention = (summed[:shard] / total).astype(bf16)
    branch = lax.dot_general(
        attention, weight_ref[...], (((0,), (0,)), ((), ())), preferred_element_type=f32
    )
    out_ref[...] = ((branch + forward_ref[...]) * modulation_ref[2]).astype(bf16)


def finish(member, parts, weights, forward, modulation, kernel=finish_kernel):
    whole = pl.BlockSpec(memory_space=pltpu.VMEM)
    return pl.pallas_call(
        kernel,
        out_shape=jax.ShapeDtypeStruct(forward.shape, bf16),
        in_specs=[pl.BlockSpec(memory_space=pltpu.SMEM)] + [whole] * 4,
        out_specs=whole,
        compiler_params=pltpu.CompilerParams(vmem_limit_bytes=8 * 1024 * 1024),
    )(member, parts, weights, forward, modulation)


def project_kernel(normed_ref, weight_ref, out_ref):
    members = out_ref.shape[0]
    shard = weight_ref.shape[0] // 3
    contract = (((1,), (1,)), ((), ()))
    query = lax.dot_general(
        weight_ref[:shard], normed_ref[...], contract, preferred_element_type=f32
    ).astype(bf16)
    others = lax.dot_general(
        normed_ref[...], weight_ref[shard:], contract, preferred_element_type=f32
    ).astype(bf16)
    each = others.shape[0] // members
    for c in range(members):
        out_ref[c, :shard, :] = query
        out_ref[c, shard:, : 2 * shard] = others[each * c : each * c + each]
        if 2 * shard < LANES:
            out_ref[c, shard:, 2 * shard :] = jnp.zeros((each, LANES - 2 * shard), bf16)


def project(normed, weights, members):
    whole = pl.BlockSpec(memory_space=pltpu.VMEM)
    return pl.pallas_call(
        project_kernel,
        out_shape=jax.ShapeDtypeStruct(
            (members, weights.shape[0] // 3 + normed.shape[0] // members, LANES), bf16
        ),
        in_specs=[whole] * 2,
        out_specs=whole,
        compiler_params=pltpu.CompilerParams(vmem_limit_bytes=8 * 1024 * 1024),
    )(normed, weights)


def attend_kernel(team_ref, mask_ref, gain_q_ref, gain_k_ref, *refs):
    *cached_refs, out_ref, packed_ref = refs
    shard = team_ref.shape[1] - 16
    members = team_ref.shape[0]
    lane = lax.broadcasted_iota(jnp.int32, (16, LANES), 1)
    row = lax.broadcasted_iota(jnp.int32, (16, LANES), 0)
    fresh = [team_ref[c, shard:, :].astype(f32) for c in range(members)]
    features = jnp.concatenate([team_ref[c, :shard, :] for c in range(members)], axis=0)
    open_key = mask_ref[...] > 0.0
    blocks = [r[i].astype(f32) for r in cached_refs for i in range(r.shape[0])]
    half = blocks[0].shape[0] // 2
    cached_keys = jnp.concatenate([b[:half] for b in blocks], axis=0).astype(bf16)
    cached_values = jnp.concatenate([b[half:] for b in blocks], axis=0).astype(bf16)
    sums = jnp.zeros((16, LANES), f32)
    for h in range(TEAM_HEADS):
        query = features[h * HEAD_DIM : (h + 1) * HEAD_DIM].astype(f32)
        scale = lax.rsqrt(jnp.mean(query * query, axis=0, keepdims=True) + eps_norm)
        query = (query * scale * gain_q_ref[...] * HEAD_DIM ** (-0.5)).astype(bf16)
        key = jnp.zeros((16, LANES), f32)
        value = jnp.zeros((16, LANES), f32)
        for c in range(members):
            start = c * shard - h * HEAD_DIM
            if start <= -shard or start >= HEAD_DIM:
                continue
            here = (lane >= start) & (lane < start + shard)
            key = jnp.where(here, pltpu.roll(fresh[c], start % LANES, 1), key)
            value = jnp.where(here, pltpu.roll(fresh[c], (start - shard) % LANES, 1), value)
        scale = lax.rsqrt(jnp.mean(key * key, axis=1, keepdims=True) + eps_norm)
        key = (key * scale * gain_k_ref[...]).astype(bf16)
        cached_key = cached_keys[:, h * HEAD_DIM : (h + 1) * HEAD_DIM]
        cached_value = cached_values[:, h * HEAD_DIM : (h + 1) * HEAD_DIM]
        scores = jnp.dot(cached_key, query, preferred_element_type=f32)
        probs = jnp.exp(jnp.where(open_key, scores, -1e30))
        fresh_probs = jnp.exp(jnp.dot(key, query, preferred_element_type=f32))
        total = jnp.sum(probs, axis=0, keepdims=True) + jnp.sum(fresh_probs, axis=0, keepdims=True)
        sums = jnp.where(row == h, total, sums)
        contract = (((0,), (0,)), ((), ()))
        weighted = lax.dot_general(
            cached_value, probs.astype(bf16), contract, preferred_element_type=f32
        ) + lax.dot_general(
            value.astype(bf16), fresh_probs.astype(bf16), contract, preferred_element_type=f32
        )
        packed_ref[h * HEAD_DIM : (h + 1) * HEAD_DIM, :] = weighted.astype(bf16)
    for c in range(members):
        out_ref[c, :shard, :] = packed_ref[c * shard : (c + 1) * shard, :]
        out_ref[c, shard:, :] = sums.astype(bf16)


def attend(team, cached, mask, gains):
    whole = pl.BlockSpec(memory_space=pltpu.VMEM)
    return pl.pallas_call(
        attend_kernel,
        out_shape=jax.ShapeDtypeStruct(team.shape, bf16),
        in_specs=[whole] * (4 + len(cached)),
        out_specs=whole,
        scratch_shapes=[pltpu.VMEM((TEAM_HEADS * HEAD_DIM, LANES), bf16)],
        compiler_params=pltpu.CompilerParams(vmem_limit_bytes=8 * 1024 * 1024),
    )(team, mask, gains[0][:, None], gains[1][None, :], *cached)


def attend_four_kernel(
    member_ref, team_ref, mask_ref, gain_q_ref, gain_k_ref, near_ref, other_ref, out_ref, features_ref
):
    members = team_ref.shape[0]
    own, more = 48, 16
    upper = member_ref[0] >= members
    lane = lax.broadcasted_iota(jnp.int32, (32, LANES), 1)
    own_at = [pl.multiple_of(jnp.where(upper, 64, 0) + own * j, 16) for j in range(members)]
    more_at = [pl.multiple_of(jnp.where(upper, 0, 192) + more * j, 16) for j in range(members)]
    keys = [jnp.zeros((32, LANES), f32) for _ in range(2)]
    values = [jnp.zeros((32, LANES), f32) for _ in range(2)]
    for j in range(members):
        features_ref[pl.ds(own_at[j], own), :] = team_ref[j, :own, :]
        features_ref[pl.ds(more_at[j], more), :] = team_ref[j, own : own + more, :]
        fresh = team_ref[j, own + more :, :].astype(f32)
        for at, length, place in ((own_at[j], own, 0), (more_at[j], more, own)):
            key = pltpu.roll(fresh, lax.rem(at - place + LANES, LANES), 1)
            value = pltpu.roll(fresh, lax.rem(at - place - 64 + 2 * LANES, LANES), 1)
            for h in range(2):
                here = lane + h * HEAD_DIM - at
                here = (here >= 0) & (here < length)
                keys[h] = jnp.where(here, key, keys[h])
                values[h] = jnp.where(here, value, values[h])
    features = features_ref[...].astype(f32)
    open_key = mask_ref[...] > 0.0
    blocks = [r[i].astype(f32) for r in (near_ref, other_ref) for i in range(r.shape[0])]
    half = blocks[0].shape[0] // 2
    cached_keys = jnp.concatenate([b[:half] for b in blocks], axis=0).astype(bf16)
    cached_values = jnp.concatenate([b[half:] for b in blocks], axis=0).astype(bf16)
    sums = jnp.zeros((16, LANES), f32)
    row = lax.broadcasted_iota(jnp.int32, (16, LANES), 0)
    token = lax.broadcasted_iota(jnp.int32, (HEAD_DIM, LANES), 1)
    contract = (((0,), (0,)), ((), ()))
    for h in range(2):
        query = features[h * HEAD_DIM : (h + 1) * HEAD_DIM]
        scale = lax.rsqrt(jnp.mean(query * query, axis=0, keepdims=True) + eps_norm)
        query = (query * scale * gain_q_ref[...] * HEAD_DIM ** (-0.5)).astype(bf16)
        scale = lax.rsqrt(jnp.mean(keys[h] * keys[h], axis=1, keepdims=True) + eps_norm)
        key = (keys[h] * scale * gain_k_ref[...]).astype(bf16)
        scores = jnp.dot(
            cached_keys[:, h * HEAD_DIM : (h + 1) * HEAD_DIM], query, preferred_element_type=f32
        )
        probs = jnp.exp(jnp.where(open_key, scores, -1e30))
        fresh_probs = jnp.exp(jnp.dot(key, query, preferred_element_type=f32))
        total = jnp.sum(probs, axis=0, keepdims=True) + jnp.sum(fresh_probs, axis=0, keepdims=True)
        sums = jnp.where(row == h, total, sums)
        weighted = lax.dot_general(
            cached_values[:, h * HEAD_DIM : (h + 1) * HEAD_DIM], probs.astype(bf16), contract,
            preferred_element_type=f32,
        ) + lax.dot_general(
            values[h].astype(bf16), fresh_probs.astype(bf16), contract, preferred_element_type=f32
        )
        shared = upper == (h == 0)
        mine = (token >= LANES // 2) == upper
        weighted = jnp.where(mine | jnp.logical_not(shared), weighted, 0.0)
        features_ref[h * HEAD_DIM : (h + 1) * HEAD_DIM, :] = weighted.astype(bf16)
    for j in range(members):
        out_ref[j, :own, :] = features_ref[pl.ds(own_at[j], own), :]
        out_ref[j, own : own + more, :] = features_ref[pl.ds(more_at[j], more), :]
        out_ref[j, own + more :, :] = sums.astype(bf16)


def attend_four(member, team, cached, mask, gains):
    whole = pl.BlockSpec(memory_space=pltpu.VMEM)
    return pl.pallas_call(
        attend_four_kernel,
        out_shape=jax.ShapeDtypeStruct((team.shape[0], 80, LANES), bf16),
        in_specs=[pl.BlockSpec(memory_space=pltpu.SMEM)] + [whole] * 6,
        out_specs=whole,
        scratch_shapes=[pltpu.VMEM((2 * HEAD_DIM, LANES), bf16)],
        compiler_params=pltpu.CompilerParams(vmem_limit_bytes=8 * 1024 * 1024),
    )(member, team, mask, gains[0][:, None], gains[1][None, :], *cached)


def finish_four_kernel(member_ref, parts_ref, weight_ref, forward_ref, modulation_ref, out_ref):
    own, more = 48, 16
    members = parts_ref.shape[0]
    upper = member_ref[0] >= members
    place = lax.rem(member_ref[0], members)
    summed = parts_ref[0].astype(f32)
    for c in range(1, members):
        summed = summed + parts_ref[c].astype(f32)
    row = lax.broadcasted_iota(jnp.int32, (own + more, LANES), 0)
    own_at = jnp.where(upper, 64, 0) + own * place
    more_at = jnp.where(upper, 0, 192) + more * place
    feature = jnp.where(row < own, own_at + row, more_at + row - own)
    first, second = summed[own + more][None], summed[own + more + 1][None]
    total = jnp.where(feature < HEAD_DIM, first, second)
    attention = (summed[: own + more] / total).astype(bf16)
    branch = lax.dot_general(
        attention, weight_ref[...], (((0,), (0,)), ((), ())), preferred_element_type=f32
    )
    out_ref[...] = ((branch + forward_ref[...]) * modulation_ref[2]).astype(bf16)


def gathered(block, groups):
    size = len(groups[0])
    spread = jnp.broadcast_to(block[None], (size,) + block.shape)
    spread = lax.all_to_all(spread, "tp", 0, 0, axis_index_groups=groups)
    return spread.reshape((size * block.shape[0],) + block.shape[1:])


def summed_over(block, groups):
    size = len(groups[0])
    parts = block.astype(bf16).reshape((size, block.shape[0] // size) + block.shape[1:])
    parts = lax.all_to_all(parts, "tp", 0, 0, axis_index_groups=groups)
    return jnp.sum(parts.astype(f32), axis=0)


def local(
    in_flight, w_qkv, w_mlp, w_attn_out, w_mlp_out, modulation, qk_gain, context_kv, text_len
):
    tp_count = lax.axis_size("tp")
    tp_index = lax.axis_index("tp")
    rows = in_flight.shape[1]
    tokens = rows * tp_count
    width = w_attn_out.shape[2]
    shard = w_attn_out.shape[1]
    ctx_local = context_kv.shape[2]
    teams = tp_count // TEAM
    team_width = TEAM * shard
    member = tp_index % TEAM
    half_team = TEAM // 2
    z_count, x_count = 2 * TEAM, tp_count // (2 * TEAM)
    xs, hs, two = range(x_count), range(z_count // 2), range(2)
    along_z = [[z_count * x + 2 * h + l for l in two for h in hs] for x in xs]
    along_x = [[z_count * x + z for x in xs] for z in range(z_count)]
    far = [[z_count * x + 2 * h + l for h in hs] for x in xs for l in two]
    blocks = [[z_count * x + 2 * h + l for x in xs for l in two] for h in hs]
    inside = [[TEAM * t + m for m in range(TEAM)] for t in range(teams)]
    fours = [[half_team * t + m for m in range(half_team)] for t in range(2 * teams)]
    shift_scale = modulation.reshape(3, 1, width)
    gains = qk_gain[0]
    weight_qkv = w_qkv[0].reshape(3 * shard, width)
    weight_mlp = w_mlp[0]
    weight_attn = w_attn_out[0]
    weight_down = w_mlp_out[0]

    partner = [
        z + TEAM + half_team if z < half_team else z + half_team if z < TEAM
        else z - half_team if z < TEAM + half_team else z - TEAM - half_team
        for z in range(z_count)
    ]
    x_here, z_here = tp_index // z_count, tp_index % z_count
    z_partner = jnp.where(
        z_here < TEAM,
        z_here + jnp.where(z_here < half_team, TEAM + half_team, half_team),
        z_here - jnp.where(z_here < TEAM + half_team, half_team, TEAM + half_team),
    )
    upper = z_here >= TEAM
    slot = jnp.arange(teams * ctx_local, dtype=jnp.int32)

    def open_keys(z, z_other):
        source = z_count * ((x_here - slot // ctx_local % x_count) % x_count)
        source = source + jnp.where(slot < x_count * ctx_local, z, z_other)
        position = ctx_local * source + slot % ctx_local
        return ((position >= TXT) | (position < text_len[0])).astype(f32)

    near_mask = open_keys(z_here, z_partner)
    other_mask = open_keys(z_here ^ half_team, z_partner ^ half_team)
    wide_mask = jnp.concatenate([near_mask, other_mask])
    near_mask = jnp.broadcast_to(near_mask[:, None], (near_mask.shape[0], LANES))
    wide_mask = jnp.broadcast_to(wide_mask[:, None], (wide_mask.shape[0], LANES))

    current = in_flight[0]
    block = spread(current, shift_scale, z_count)
    block, flat = lax.optimization_barrier((block, context_kv[0]))
    flat = flat.reshape(2 * ctx_local, width)
    by_x = []
    for step in range(x_count):
        part = lax.dynamic_slice_in_dim(
            flat, (x_here + step) % x_count * 2 * team_width, 2 * team_width, 1
        )
        if step:
            route = [
                (z_count * x + z, z_count * ((x + step) % x_count) + z)
                for x in range(x_count) for z in range(z_count)
            ]
            part = lax.ppermute(part, "tp", route)
        by_x.append(part)
    by_x = jnp.stack(by_x)
    keep = jnp.where(upper, by_x[:, :, team_width:], by_x[:, :, :team_width])
    give = jnp.where(upper, by_x[:, :, :team_width], by_x[:, :, team_width:])

    for tick_number in range(TICKS):
        if tick_number == 0:
            normed = lax.all_to_all(block, "tp", 0, 0, axis_index_groups=along_z)
            normed = normed.reshape(-1, width)
            route = [(z_count * x + z, z_count * x + partner[z]) for x in xs for z in range(z_count)]
            got = [
                lax.ppermute(part, "tp", route)
                for part in (give[: x_count // 2], give[x_count // 2 :])
            ]
            normed = gathered(normed, along_x)
            normed, got[0] = lax.optimization_barrier((normed, got[0]))
            cached = [keep] + got
        else:
            block = spread(current, shift_scale, len(hs))
            normed = lax.all_to_all(block, "tp", 0, 0, axis_index_groups=far)
            normed = gathered(normed.reshape(-1, width), blocks)
        if tick_number == 0:
            team = project(normed, weight_qkv, TEAM)
            team = lax.all_to_all(team, "tp", 0, 0, axis_index_groups=inside)
            parts = attend(team, cached, near_mask, gains)
            parts = lax.all_to_all(parts, "tp", 0, 0, axis_index_groups=inside)
        else:
            team = project(normed, wide_qkv, half_team)
            team = lax.all_to_all(team, "tp", 0, 0, axis_index_groups=fours)
            parts = attend_four(member[None], team, wide_cached, wide_mask, gains)
            parts = lax.all_to_all(parts, "tp", 0, 0, axis_index_groups=fours)
        hidden = jax.nn.gelu(
            lax.dot_general(
                normed, weight_mlp, (((1,), (1,)), ((), ())), preferred_element_type=f32
            ),
            approximate=True,
        ).astype(bf16)
        hidden = lax.optimization_barrier(hidden)
        forward = jnp.dot(hidden, weight_down, preferred_element_type=f32)
        forward = lax.optimization_barrier(forward)
        if tick_number == 0:
            branch = finish(member[None], parts, weight_attn, forward, shift_scale)
        else:
            branch = finish(
                member[None], parts, wide_attn, forward, shift_scale, finish_four_kernel
            )
        branch = summed_over(branch, blocks)
        branch = summed_over(branch.reshape(-1, LANES), far).reshape(rows, width)
        if tick_number == 0:
            rows_here = jnp.concatenate([w_qkv[0], w_attn_out], axis=0)
            more = 0
            for offset, moves in (
                (jnp.where(member % 2 == 0, 32, 0), ((4, 2), (5, 3), (2, 4), (3, 5))),
                (16, ((4, 1), (3, 6))),
                (jnp.where(member == 4, 0, 32), ((4, 0), (3, 7))),
            ):
                part = lax.dynamic_slice_in_dim(rows_here, offset, 16, 1)
                more = more + lax.ppermute(
                    part, "tp", [(TEAM * t + a, TEAM * t + b) for t in range(teams) for a, b in moves]
                )
            lower = member < half_team
            all_cached = jnp.concatenate(cached, axis=0)
            two_heads = 2 * HEAD_DIM
            near = jnp.where(lower, all_cached[..., :two_heads], all_cached[..., HEAD_DIM:])
            far_heads = jnp.where(lower, all_cached[..., HEAD_DIM:], all_cached[..., :two_heads])
            other = lax.ppermute(far_heads, "tp", [(i, i ^ half_team) for i in range(tp_count)])
            branch, more, other = lax.optimization_barrier((branch, more, other))
            wide = jnp.concatenate([rows_here, more], axis=1)
            wide_qkv, wide_attn = wide[:3].reshape(-1, width), wide[3]
            wide_cached = [near, other]
        finished = (current.astype(f32) + branch).astype(bf16)
        current = shifted(finished, "pipe", 1)
    return current[None]


def solution(mesh):
    placed = (
        P("pipe", "tp", None),
        P("pipe", None, "tp", None),
        P("pipe", "tp", None),
        P("pipe", "tp", None),
        P("pipe", "tp", None),
        P("pipe", None, None),
        P("pipe", None, None),
        P("pipe", None, "tp", None),
        P(),
    )
    return jax.shard_map(
        local, mesh=mesh, in_specs=placed, out_specs=P("pipe", "tp", None), check_vma=False
    )
```

```python
import jax
import jax.numpy as jnp
from jax import lax
from jax.experimental import pallas as pl
from jax.experimental.pallas import tpu as pltpu
from jax.sharding import PartitionSpec as P

HEADS = 24
HEAD_DIM = 128
TICKS = 2
TXT = 512
TEAM = 8
TEAM_HEADS = 3
LANES = 128

eps_norm = 1e-06
f32 = jnp.float32
bf16 = jnp.bfloat16


def shifted(block, axis, distance):
    size = lax.axis_size(axis)
    return lax.ppermute(block, axis, [((i - distance) % size, i) for i in range(size)])


def spread_kernel(rows_ref, modulation_ref, out_ref, block_ref):
    x = rows_ref[...].astype(f32)
    centred = x - jnp.mean(x, axis=1, keepdims=True)
    variance = jnp.mean(centred * centred, axis=1, keepdims=True)
    normed = centred * lax.rsqrt(variance + eps_norm)
    normed = normed * (1.0 + modulation_ref[1]) + modulation_ref[0]
    rows, width = x.shape
    pieces = width // LANES
    for r in range(rows):
        for p in range(pieces):
            at = r * pieces + p
            block_ref[at : at + 1, :] = normed[r : r + 1, p * LANES : (p + 1) * LANES]
    block = block_ref[...].astype(bf16)
    for j in range(out_ref.shape[0]):
        out_ref[j] = block


def spread(rows, modulation, receivers):
    whole = pl.BlockSpec(memory_space=pltpu.VMEM)
    lines = rows.shape[0] * rows.shape[1] // LANES
    return pl.pallas_call(
        spread_kernel,
        out_shape=jax.ShapeDtypeStruct((receivers, lines, LANES), bf16),
        in_specs=[whole] * 2,
        out_specs=whole,
        scratch_shapes=[pltpu.VMEM((lines, LANES), f32)],
        compiler_params=pltpu.CompilerParams(vmem_limit_bytes=8 * 1024 * 1024),
    )(rows, modulation)


def finish_kernel(member_ref, parts_ref, weight_ref, forward_ref, modulation_ref, out_ref):
    shard, width = weight_ref.shape
    summed = parts_ref[0].astype(f32)
    for c in range(1, parts_ref.shape[0]):
        summed = summed + parts_ref[c].astype(f32)
    feature = member_ref[0] * shard + lax.broadcasted_iota(jnp.int32, (shard, LANES), 0)
    total = jnp.broadcast_to(summed[shard + TEAM_HEADS - 1][None], (shard, LANES))
    for h in range(TEAM_HEADS - 2, -1, -1):
        total = jnp.where(feature < (h + 1) * HEAD_DIM, summed[shard + h][None], total)
    attention = (summed[:shard] / total).astype(bf16)
    branch = lax.dot_general(
        attention, weight_ref[...], (((0,), (0,)), ((), ())), preferred_element_type=f32
    )
    out_ref[...] = ((branch + forward_ref[...]) * modulation_ref[2]).astype(bf16)


def finish(member, parts, weights, forward, modulation):
    whole = pl.BlockSpec(memory_space=pltpu.VMEM)
    return pl.pallas_call(
        finish_kernel,
        out_shape=jax.ShapeDtypeStruct(forward.shape, bf16),
        in_specs=[pl.BlockSpec(memory_space=pltpu.SMEM)] + [whole] * 4,
        out_specs=whole,
        compiler_params=pltpu.CompilerParams(vmem_limit_bytes=8 * 1024 * 1024),
    )(member, parts, weights, forward, modulation)


def project_kernel(normed_ref, weight_ref, out_ref):
    members = out_ref.shape[0]
    shard = weight_ref.shape[0] // 3
    contract = (((1,), (1,)), ((), ()))
    query = lax.dot_general(
        weight_ref[:shard], normed_ref[...], contract, preferred_element_type=f32
    ).astype(bf16)
    others = lax.dot_general(
        normed_ref[...], weight_ref[shard:], contract, preferred_element_type=f32
    ).astype(bf16)
    for c in range(members):
        out_ref[c, :shard, :] = query
        out_ref[c, shard:, : 2 * shard] = others[16 * c : 16 * c + 16]
        out_ref[c, shard:, 2 * shard :] = jnp.zeros((16, LANES - 2 * shard), bf16)


def project(normed, weights):
    whole = pl.BlockSpec(memory_space=pltpu.VMEM)
    return pl.pallas_call(
        project_kernel,
        out_shape=jax.ShapeDtypeStruct((TEAM, weights.shape[0] // 3 + 16, LANES), bf16),
        in_specs=[whole] * 2,
        out_specs=whole,
        compiler_params=pltpu.CompilerParams(vmem_limit_bytes=8 * 1024 * 1024),
    )(normed, weights)


def attend_kernel(team_ref, mask_ref, gain_q_ref, gain_k_ref, *refs):
    *cached_refs, out_ref, packed_ref = refs
    shard = team_ref.shape[1] - 16
    members = team_ref.shape[0]
    lane = lax.broadcasted_iota(jnp.int32, (16, LANES), 1)
    row = lax.broadcasted_iota(jnp.int32, (16, LANES), 0)
    fresh = [team_ref[c, shard:, :].astype(f32) for c in range(members)]
    features = jnp.concatenate([team_ref[c, :shard, :] for c in range(members)], axis=0)
    open_key = mask_ref[...] > 0.0
    blocks = [r[i].astype(f32) for r in cached_refs for i in range(r.shape[0])]
    half = blocks[0].shape[0] // 2
    cached_keys = jnp.concatenate([b[:half] for b in blocks], axis=0).astype(bf16)
    cached_values = jnp.concatenate([b[half:] for b in blocks], axis=0).astype(bf16)
    sums = jnp.zeros((16, LANES), f32)
    for h in range(TEAM_HEADS):
        query = features[h * HEAD_DIM : (h + 1) * HEAD_DIM].astype(f32)
        scale = lax.rsqrt(jnp.mean(query * query, axis=0, keepdims=True) + eps_norm)
        query = (query * scale * gain_q_ref[...] * HEAD_DIM ** (-0.5)).astype(bf16)
        key = jnp.zeros((16, LANES), f32)
        value = jnp.zeros((16, LANES), f32)
        for c in range(members):
            start = c * shard - h * HEAD_DIM
            if start <= -shard or start >= HEAD_DIM:
                continue
            here = (lane >= start) & (lane < start + shard)
            key = jnp.where(here, pltpu.roll(fresh[c], start % LANES, 1), key)
            value = jnp.where(here, pltpu.roll(fresh[c], (start - shard) % LANES, 1), value)
        scale = lax.rsqrt(jnp.mean(key * key, axis=1, keepdims=True) + eps_norm)
        key = (key * scale * gain_k_ref[...]).astype(bf16)
        cached_key = cached_keys[:, h * HEAD_DIM : (h + 1) * HEAD_DIM]
        cached_value = cached_values[:, h * HEAD_DIM : (h + 1) * HEAD_DIM]
        scores = jnp.dot(cached_key, query, preferred_element_type=f32)
        probs = jnp.exp(jnp.where(open_key, scores, -1e30))
        fresh_probs = jnp.exp(jnp.dot(key, query, preferred_element_type=f32))
        total = jnp.sum(probs, axis=0, keepdims=True) + jnp.sum(fresh_probs, axis=0, keepdims=True)
        sums = jnp.where(row == h, total, sums)
        contract = (((0,), (0,)), ((), ()))
        weighted = lax.dot_general(
            cached_value, probs.astype(bf16), contract, preferred_element_type=f32
        ) + lax.dot_general(
            value.astype(bf16), fresh_probs.astype(bf16), contract, preferred_element_type=f32
        )
        packed_ref[h * HEAD_DIM : (h + 1) * HEAD_DIM, :] = weighted.astype(bf16)
    for c in range(members):
        out_ref[c, :shard, :] = packed_ref[c * shard : (c + 1) * shard, :]
        out_ref[c, shard:, :] = sums.astype(bf16)


def attend(team, cached, mask, gains):
    whole = pl.BlockSpec(memory_space=pltpu.VMEM)
    return pl.pallas_call(
        attend_kernel,
        out_shape=jax.ShapeDtypeStruct(team.shape, bf16),
        in_specs=[whole] * (4 + len(cached)),
        out_specs=whole,
        scratch_shapes=[pltpu.VMEM((TEAM_HEADS * HEAD_DIM, LANES), bf16)],
        compiler_params=pltpu.CompilerParams(vmem_limit_bytes=8 * 1024 * 1024),
    )(team, mask, gains[0][:, None], gains[1][None, :], *cached)


def gathered(block, groups):
    size = len(groups[0])
    spread = jnp.broadcast_to(block[None], (size,) + block.shape)
    spread = lax.all_to_all(spread, "tp", 0, 0, axis_index_groups=groups)
    return spread.reshape((size * block.shape[0],) + block.shape[1:])


def summed_over(block, groups):
    size = len(groups[0])
    parts = block.astype(bf16).reshape((size, block.shape[0] // size) + block.shape[1:])
    parts = lax.all_to_all(parts, "tp", 0, 0, axis_index_groups=groups)
    return jnp.sum(parts.astype(f32), axis=0)


def local(
    in_flight, w_qkv, w_mlp, w_attn_out, w_mlp_out, modulation, qk_gain, context_kv, text_len
):
    tp_count = lax.axis_size("tp")
    tp_index = lax.axis_index("tp")
    rows = in_flight.shape[1]
    tokens = rows * tp_count
    width = w_attn_out.shape[2]
    shard = w_attn_out.shape[1]
    ctx_local = context_kv.shape[2]
    teams = tp_count // TEAM
    team_width = TEAM * shard
    member = tp_index % TEAM
    z_count, x_count = 2 * TEAM, tp_count // (2 * TEAM)
    xs, hs, two = range(x_count), range(z_count // 2), range(2)
    along_z = [[z_count * x + 2 * h + l for l in two for h in hs] for x in xs]
    along_x = [[z_count * x + z for x in xs] for z in range(z_count)]
    far = [[z_count * x + 2 * h + l for h in hs] for x in xs for l in two]
    blocks = [[z_count * x + 2 * h + l for x in xs for l in two] for h in hs]
    inside = [[TEAM * t + m for m in range(TEAM)] for t in range(teams)]
    shift_scale = modulation.reshape(3, 1, width)
    gains = qk_gain[0]
    weight_qkv = w_qkv[0].reshape(3 * shard, width)
    weight_mlp = w_mlp[0]
    weight_attn = w_attn_out[0]
    weight_down = w_mlp_out[0]

    half_team = TEAM // 2
    partner = [
        z + TEAM + half_team if z < half_team else z + half_team if z < TEAM
        else z - half_team if z < TEAM + half_team else z - TEAM - half_team
        for z in range(z_count)
    ]
    x_here, z_here = tp_index // z_count, tp_index % z_count
    z_partner = jnp.where(
        z_here < TEAM,
        z_here + jnp.where(z_here < half_team, TEAM + half_team, half_team),
        z_here - jnp.where(z_here < TEAM + half_team, half_team, TEAM + half_team),
    )
    upper = z_here >= TEAM
    slot = jnp.arange(teams * ctx_local, dtype=jnp.int32)
    own_z = slot < x_count * ctx_local
    source = z_count * ((x_here - slot // ctx_local % x_count) % x_count)
    source = source + jnp.where(own_z, z_here, z_partner)
    position = ctx_local * source + slot % ctx_local
    cached_mask = ((position >= TXT) | (position < text_len[0])).astype(f32)
    cached_mask = jnp.broadcast_to(cached_mask[:, None], (teams * ctx_local, LANES))

    current = in_flight[0]
    block = spread(current, shift_scale, z_count)
    block, flat = lax.optimization_barrier((block, context_kv[0]))
    flat = flat.reshape(2 * ctx_local, width)
    by_x = []
    for step in range(x_count):
        part = lax.dynamic_slice_in_dim(
            flat, (x_here + step) % x_count * 2 * team_width, 2 * team_width, 1
        )
        if step:
            route = [
                (z_count * x + z, z_count * ((x + step) % x_count) + z)
                for x in range(x_count) for z in range(z_count)
            ]
            part = lax.ppermute(part, "tp", route)
        by_x.append(part)
    lower_teams = [part[:, :team_width] for part in by_x]
    upper_teams = [part[:, team_width:] for part in by_x]
    keep = [jnp.where(upper, u, l) for l, u in zip(lower_teams, upper_teams)]
    give = [jnp.where(upper, l, u) for l, u in zip(lower_teams, upper_teams)]

    for tick_number in range(TICKS):
        if tick_number == 0:
            normed = lax.all_to_all(block, "tp", 0, 0, axis_index_groups=along_z)
            normed = normed.reshape(-1, width)
            route = [(z_count * x + z, z_count * x + partner[z]) for x in xs for z in range(z_count)]
            got = [
                lax.ppermute(jnp.stack(part), "tp", route)
                for part in (give[:1], give[1:2], give[2:])
            ]
            normed, got[0] = lax.optimization_barrier((normed, got[0]))
            normed = gathered(normed, along_x)
            normed, got[1] = lax.optimization_barrier((normed, got[1]))
            cached = [jnp.stack(keep)] + got
        else:
            block = spread(current, shift_scale, len(hs))
            normed = lax.all_to_all(block, "tp", 0, 0, axis_index_groups=far)
            normed = gathered(normed.reshape(-1, width), blocks)
        team = project(normed, weight_qkv)
        team = lax.all_to_all(team, "tp", 0, 0, axis_index_groups=inside)
        parts = attend(team, cached, cached_mask, gains)
        parts = lax.all_to_all(parts, "tp", 0, 0, axis_index_groups=inside)
        hidden = jax.nn.gelu(
            lax.dot_general(
                normed, weight_mlp, (((1,), (1,)), ((), ())), preferred_element_type=f32
            ),
            approximate=True,
        ).astype(bf16)
        hidden = lax.optimization_barrier(hidden)
        forward = jnp.dot(hidden, weight_down, preferred_element_type=f32)
        forward = lax.optimization_barrier(forward)
        branch = finish(member[None], parts, weight_attn, forward, shift_scale)
        branch = summed_over(branch, blocks)
        branch = summed_over(branch.reshape(-1, LANES), far).reshape(rows, width)
        finished = (current.astype(f32) + branch).astype(bf16)
        current = shifted(finished, "pipe", 1)
    return current[None]


def solution(mesh):
    placed = (
        P("pipe", "tp", None),
        P("pipe", None, "tp", None),
        P("pipe", "tp", None),
        P("pipe", "tp", None),
        P("pipe", "tp", None),
        P("pipe", None, None),
        P("pipe", None, None),
        P("pipe", None, "tp", None),
        P(),
    )
    return jax.shard_map(
        local, mesh=mesh, in_specs=placed, out_specs=P("pipe", "tp", None), check_vma=False
    )
```

```python
import jax
import jax.numpy as jnp
from jax import lax
from jax.experimental import pallas as pl
from jax.experimental.pallas import tpu as pltpu
from jax.sharding import PartitionSpec as P

HEADS = 24
HEAD_DIM = 128
TICKS = 2
TXT = 512
TEAM = 8
TEAM_HEADS = 3
LANES = 128

eps_norm = 1e-06
f32 = jnp.float32
bf16 = jnp.bfloat16


def shifted(block, axis, distance):
    size = lax.axis_size(axis)
    return lax.ppermute(block, axis, [((i - distance) % size, i) for i in range(size)])


def spread_kernel(rows_ref, modulation_ref, out_ref, block_ref):
    x = rows_ref[...].astype(f32)
    centred = x - jnp.mean(x, axis=1, keepdims=True)
    variance = jnp.mean(centred * centred, axis=1, keepdims=True)
    normed = centred * lax.rsqrt(variance + eps_norm)
    normed = normed * (1.0 + modulation_ref[1]) + modulation_ref[0]
    rows, width = x.shape
    pieces = width // LANES
    for r in range(rows):
        for p in range(pieces):
            at = r * pieces + p
            block_ref[at : at + 1, :] = normed[r : r + 1, p * LANES : (p + 1) * LANES]
    block = block_ref[...].astype(bf16)
    for j in range(out_ref.shape[0]):
        out_ref[j] = block


def spread(rows, modulation, receivers):
    whole = pl.BlockSpec(memory_space=pltpu.VMEM)
    lines = rows.shape[0] * rows.shape[1] // LANES
    return pl.pallas_call(
        spread_kernel,
        out_shape=jax.ShapeDtypeStruct((receivers, lines, LANES), bf16),
        in_specs=[whole] * 2,
        out_specs=whole,
        scratch_shapes=[pltpu.VMEM((lines, LANES), f32)],
        compiler_params=pltpu.CompilerParams(vmem_limit_bytes=8 * 1024 * 1024),
    )(rows, modulation)


def finish_kernel(member_ref, parts_ref, weight_ref, forward_ref, modulation_ref, out_ref):
    shard, width = weight_ref.shape
    summed = parts_ref[0].astype(f32)
    for c in range(1, parts_ref.shape[0]):
        summed = summed + parts_ref[c].astype(f32)
    feature = member_ref[0] * shard + lax.broadcasted_iota(jnp.int32, (shard, LANES), 0)
    total = jnp.broadcast_to(summed[shard + TEAM_HEADS - 1][None], (shard, LANES))
    for h in range(TEAM_HEADS - 2, -1, -1):
        total = jnp.where(feature < (h + 1) * HEAD_DIM, summed[shard + h][None], total)
    attention = (summed[:shard] / total).astype(bf16)
    branch = lax.dot_general(
        attention, weight_ref[...], (((0,), (0,)), ((), ())), preferred_element_type=f32
    )
    out_ref[...] = ((branch + forward_ref[...]) * modulation_ref[2]).astype(bf16)


def finish(member, parts, weights, forward, modulation):
    whole = pl.BlockSpec(memory_space=pltpu.VMEM)
    return pl.pallas_call(
        finish_kernel,
        out_shape=jax.ShapeDtypeStruct(forward.shape, bf16),
        in_specs=[pl.BlockSpec(memory_space=pltpu.SMEM)] + [whole] * 4,
        out_specs=whole,
        compiler_params=pltpu.CompilerParams(vmem_limit_bytes=8 * 1024 * 1024),
    )(member, parts, weights, forward, modulation)


def project_kernel(normed_ref, weight_ref, out_ref):
    members = out_ref.shape[0]
    shard = weight_ref.shape[0] // 3
    contract = (((1,), (1,)), ((), ()))
    query = lax.dot_general(
        weight_ref[:shard], normed_ref[...], contract, preferred_element_type=f32
    ).astype(bf16)
    others = lax.dot_general(
        normed_ref[...], weight_ref[shard:], contract, preferred_element_type=f32
    ).astype(bf16)
    for c in range(members):
        out_ref[c, :shard, :] = query
        out_ref[c, shard:, : 2 * shard] = others[16 * c : 16 * c + 16]
        out_ref[c, shard:, 2 * shard :] = jnp.zeros((16, LANES - 2 * shard), bf16)


def project(normed, weights):
    whole = pl.BlockSpec(memory_space=pltpu.VMEM)
    return pl.pallas_call(
        project_kernel,
        out_shape=jax.ShapeDtypeStruct((TEAM, weights.shape[0] // 3 + 16, LANES), bf16),
        in_specs=[whole] * 2,
        out_specs=whole,
        compiler_params=pltpu.CompilerParams(vmem_limit_bytes=8 * 1024 * 1024),
    )(normed, weights)


def attend_kernel(team_ref, mask_ref, gain_q_ref, gain_k_ref, *refs):
    *cached_refs, out_ref, packed_ref = refs
    shard = team_ref.shape[1] - 16
    members = team_ref.shape[0]
    lane = lax.broadcasted_iota(jnp.int32, (16, LANES), 1)
    row = lax.broadcasted_iota(jnp.int32, (16, LANES), 0)
    fresh = [team_ref[c, shard:, :].astype(f32) for c in range(members)]
    features = jnp.concatenate([team_ref[c, :shard, :] for c in range(members)], axis=0)
    open_key = mask_ref[...] > 0.0
    blocks = [r[i].astype(f32) for r in cached_refs for i in range(r.shape[0])]
    half = blocks[0].shape[0] // 2
    cached_keys = jnp.concatenate([b[:half] for b in blocks], axis=0).astype(bf16)
    cached_values = jnp.concatenate([b[half:] for b in blocks], axis=0).astype(bf16)
    sums = jnp.zeros((16, LANES), f32)
    for h in range(TEAM_HEADS):
        query = features[h * HEAD_DIM : (h + 1) * HEAD_DIM].astype(f32)
        scale = lax.rsqrt(jnp.mean(query * query, axis=0, keepdims=True) + eps_norm)
        query = (query * scale * gain_q_ref[...] * HEAD_DIM ** (-0.5)).astype(bf16)
        key = jnp.zeros((16, LANES), f32)
        value = jnp.zeros((16, LANES), f32)
        for c in range(members):
            start = c * shard - h * HEAD_DIM
            if start <= -shard or start >= HEAD_DIM:
                continue
            here = (lane >= start) & (lane < start + shard)
            key = jnp.where(here, pltpu.roll(fresh[c], start % LANES, 1), key)
            value = jnp.where(here, pltpu.roll(fresh[c], (start - shard) % LANES, 1), value)
        scale = lax.rsqrt(jnp.mean(key * key, axis=1, keepdims=True) + eps_norm)
        key = (key * scale * gain_k_ref[...]).astype(bf16)
        cached_key = cached_keys[:, h * HEAD_DIM : (h + 1) * HEAD_DIM]
        cached_value = cached_values[:, h * HEAD_DIM : (h + 1) * HEAD_DIM]
        scores = jnp.dot(cached_key, query, preferred_element_type=f32)
        probs = jnp.exp(jnp.where(open_key, scores, -1e30))
        fresh_probs = jnp.exp(jnp.dot(key, query, preferred_element_type=f32))
        total = jnp.sum(probs, axis=0, keepdims=True) + jnp.sum(fresh_probs, axis=0, keepdims=True)
        sums = jnp.where(row == h, total, sums)
        contract = (((0,), (0,)), ((), ()))
        weighted = lax.dot_general(
            cached_value, probs.astype(bf16), contract, preferred_element_type=f32
        ) + lax.dot_general(
            value.astype(bf16), fresh_probs.astype(bf16), contract, preferred_element_type=f32
        )
        packed_ref[h * HEAD_DIM : (h + 1) * HEAD_DIM, :] = weighted.astype(bf16)
    for c in range(members):
        out_ref[c, :shard, :] = packed_ref[c * shard : (c + 1) * shard, :]
        out_ref[c, shard:, :] = sums.astype(bf16)


def attend(team, cached, mask, gains):
    whole = pl.BlockSpec(memory_space=pltpu.VMEM)
    return pl.pallas_call(
        attend_kernel,
        out_shape=jax.ShapeDtypeStruct(team.shape, bf16),
        in_specs=[whole] * (4 + len(cached)),
        out_specs=whole,
        scratch_shapes=[pltpu.VMEM((TEAM_HEADS * HEAD_DIM, LANES), bf16)],
        compiler_params=pltpu.CompilerParams(vmem_limit_bytes=8 * 1024 * 1024),
    )(team, mask, gains[0][:, None], gains[1][None, :], *cached)


def gathered(block, groups):
    size = len(groups[0])
    spread = jnp.broadcast_to(block[None], (size,) + block.shape)
    spread = lax.all_to_all(spread, "tp", 0, 0, axis_index_groups=groups)
    return spread.reshape((size * block.shape[0],) + block.shape[1:])


def summed_over(block, groups):
    size = len(groups[0])
    parts = block.astype(bf16).reshape((size, block.shape[0] // size) + block.shape[1:])
    parts = lax.all_to_all(parts, "tp", 0, 0, axis_index_groups=groups)
    return jnp.sum(parts.astype(f32), axis=0)


def local(
    in_flight, w_qkv, w_mlp, w_attn_out, w_mlp_out, modulation, qk_gain, context_kv, text_len
):
    tp_count = lax.axis_size("tp")
    tp_index = lax.axis_index("tp")
    rows = in_flight.shape[1]
    tokens = rows * tp_count
    width = w_attn_out.shape[2]
    shard = w_attn_out.shape[1]
    ctx_local = context_kv.shape[2]
    teams = tp_count // TEAM
    team_width = TEAM * shard
    member = tp_index % TEAM
    z_count, x_count = 2 * TEAM, tp_count // (2 * TEAM)
    xs, hs, two = range(x_count), range(z_count // 2), range(2)
    far = [[z_count * x + 2 * h + l for h in hs] for x in xs for l in two]
    blocks = [[z_count * x + 2 * h + l for x in xs for l in two] for h in hs]
    inside = [[TEAM * t + m for m in range(TEAM)] for t in range(teams)]
    shift_scale = modulation.reshape(3, 1, width)
    gains = qk_gain[0]
    weight_qkv = w_qkv[0].reshape(3 * shard, width)
    weight_mlp = w_mlp[0]
    weight_attn = w_attn_out[0]
    weight_down = w_mlp_out[0]

    half_team = TEAM // 2
    offset = [TEAM + half_team if m < half_team else half_team for m in range(TEAM)]
    across = [
        [z_count * x + m + half * offset[m] for x in xs for half in two] for m in range(TEAM)
    ]
    x_here, z_here = tp_index // z_count, tp_index % z_count
    z_partner = jnp.where(
        z_here < TEAM,
        z_here + jnp.where(z_here < half_team, TEAM + half_team, half_team),
        z_here - jnp.where(z_here < TEAM + half_team, half_team, TEAM + half_team),
    )
    slot = jnp.arange(teams * ctx_local, dtype=jnp.int32)
    block = slot // ctx_local
    z_block = jnp.where(block % 2 == 0, jnp.minimum(z_here, z_partner), jnp.maximum(z_here, z_partner))
    source = z_count * (block // 2) + z_block
    position = ctx_local * source + slot % ctx_local
    cached_mask = ((position >= TXT) | (position < text_len[0])).astype(f32)
    cached_mask = jnp.broadcast_to(cached_mask[:, None], (teams * ctx_local, LANES))

    current = in_flight[0]
    block = spread(current, shift_scale, len(hs))
    block, flat = lax.optimization_barrier((block, context_kv[0]))
    by_team = flat.reshape(2 * ctx_local, teams, team_width).transpose(1, 0, 2)

    for tick_number in range(TICKS):
        if tick_number:
            block = spread(current, shift_scale, len(hs))
        normed = lax.all_to_all(block, "tp", 0, 0, axis_index_groups=far).reshape(-1, width)
        if tick_number == 0:
            normed, by_team = lax.optimization_barrier((normed, by_team))
            cached = [lax.all_to_all(by_team, "tp", 0, 0, axis_index_groups=across)]
            normed, cached = lax.optimization_barrier((normed, cached))
        normed = gathered(normed, blocks)
        team = project(normed, weight_qkv)
        team = lax.all_to_all(team, "tp", 0, 0, axis_index_groups=inside)
        parts = attend(team, cached, cached_mask, gains)
        parts = lax.all_to_all(parts, "tp", 0, 0, axis_index_groups=inside)
        hidden = jax.nn.gelu(
            lax.dot_general(
                normed, weight_mlp, (((1,), (1,)), ((), ())), preferred_element_type=f32
            ),
            approximate=True,
        ).astype(bf16)
        hidden = lax.optimization_barrier(hidden)
        forward = jnp.dot(hidden, weight_down, preferred_element_type=f32)
        forward = lax.optimization_barrier(forward)
        branch = finish(member[None], parts, weight_attn, forward, shift_scale)
        branch = summed_over(branch, blocks)
        branch = summed_over(branch.reshape(-1, LANES), far).reshape(rows, width)
        finished = (current.astype(f32) + branch).astype(bf16)
        current = shifted(finished, "pipe", 1)
    return current[None]


def solution(mesh):
    placed = (
        P("pipe", "tp", None),
        P("pipe", None, "tp", None),
        P("pipe", "tp", None),
        P("pipe", "tp", None),
        P("pipe", "tp", None),
        P("pipe", None, None),
        P("pipe", None, None),
        P("pipe", None, "tp", None),
        P(),
    )
    return jax.shard_map(
        local, mesh=mesh, in_specs=placed, out_specs=P("pipe", "tp", None), check_vma=False
    )
```

```python
import jax
import jax.numpy as jnp
from jax import lax
from jax.experimental import pallas as pl
from jax.experimental.pallas import tpu as pltpu
from jax.sharding import PartitionSpec as P

HEADS = 24
HEAD_DIM = 128
TICKS = 2
TXT = 512
TEAM = 8
TEAM_HEADS = 3
LANES = 128

eps_norm = 1e-06
f32 = jnp.float32
bf16 = jnp.bfloat16


def shifted(block, axis, distance):
    size = lax.axis_size(axis)
    return lax.ppermute(block, axis, [((i - distance) % size, i) for i in range(size)])


def spread_kernel(rows_ref, modulation_ref, out_ref, block_ref):
    x = rows_ref[...].astype(f32)
    centred = x - jnp.mean(x, axis=1, keepdims=True)
    variance = jnp.mean(centred * centred, axis=1, keepdims=True)
    normed = centred * lax.rsqrt(variance + eps_norm)
    normed = normed * (1.0 + modulation_ref[1]) + modulation_ref[0]
    rows, width = x.shape
    pieces = width // LANES
    for r in range(rows):
        for p in range(pieces):
            at = r * pieces + p
            block_ref[at : at + 1, :] = normed[r : r + 1, p * LANES : (p + 1) * LANES]
    block = block_ref[...].astype(bf16)
    for j in range(out_ref.shape[0]):
        for k in range(out_ref.shape[1] // block.shape[0]):
            out_ref[j, k * block.shape[0] : (k + 1) * block.shape[0], :] = block


def spread(rows, modulation, receivers, copies=1):
    whole = pl.BlockSpec(memory_space=pltpu.VMEM)
    given = whole if copies == 1 else pl.BlockSpec()
    lines = rows.shape[0] * rows.shape[1] // LANES
    return pl.pallas_call(
        spread_kernel,
        out_shape=jax.ShapeDtypeStruct((receivers, copies * lines, LANES), bf16),
        in_specs=[given] * 2,
        out_specs=whole,
        scratch_shapes=[pltpu.VMEM((lines, LANES), f32)],
        compiler_params=pltpu.CompilerParams(vmem_limit_bytes=8 * 1024 * 1024),
    )(rows, modulation)


def finish_kernel(member_ref, parts_ref, weight_ref, forward_ref, modulation_ref, out_ref):
    shard, width = weight_ref.shape
    summed = parts_ref[0].astype(f32)
    for c in range(1, parts_ref.shape[0]):
        summed = summed + parts_ref[c].astype(f32)
    feature = member_ref[0] * shard + lax.broadcasted_iota(jnp.int32, (shard, LANES), 0)
    total = jnp.broadcast_to(summed[shard + TEAM_HEADS - 1][None], (shard, LANES))
    for h in range(TEAM_HEADS - 2, -1, -1):
        total = jnp.where(feature < (h + 1) * HEAD_DIM, summed[shard + h][None], total)
    attention = (summed[:shard] / total).astype(bf16)
    branch = lax.dot_general(
        attention, weight_ref[...], (((0,), (0,)), ((), ())), preferred_element_type=f32
    )
    out_ref[...] = ((branch + forward_ref[...]) * modulation_ref[2]).astype(bf16)


def finish(member, parts, weights, forward, modulation):
    whole = pl.BlockSpec(memory_space=pltpu.VMEM)
    return pl.pallas_call(
        finish_kernel,
        out_shape=jax.ShapeDtypeStruct(forward.shape, bf16),
        in_specs=[pl.BlockSpec(memory_space=pltpu.SMEM)] + [whole] * 4,
        out_specs=whole,
        compiler_params=pltpu.CompilerParams(vmem_limit_bytes=8 * 1024 * 1024),
    )(member, parts, weights, forward, modulation)


def project_kernel(normed_ref, weight_ref, out_ref):
    members = out_ref.shape[0]
    shard = weight_ref.shape[0] // 3
    contract = (((1,), (1,)), ((), ()))
    query = lax.dot_general(
        weight_ref[:shard], normed_ref[...], contract, preferred_element_type=f32
    ).astype(bf16)
    others = lax.dot_general(
        normed_ref[...], weight_ref[shard:], contract, preferred_element_type=f32
    ).astype(bf16)
    for c in range(members):
        out_ref[c, :shard, :] = query
        out_ref[c, shard:, : 2 * shard] = others[16 * c : 16 * c + 16]
        out_ref[c, shard:, 2 * shard :] = jnp.zeros((16, LANES - 2 * shard), bf16)


def project(normed, weights):
    whole = pl.BlockSpec(memory_space=pltpu.VMEM)
    return pl.pallas_call(
        project_kernel,
        out_shape=jax.ShapeDtypeStruct((TEAM, weights.shape[0] // 3 + 16, LANES), bf16),
        in_specs=[whole] * 2,
        out_specs=whole,
        compiler_params=pltpu.CompilerParams(vmem_limit_bytes=8 * 1024 * 1024),
    )(normed, weights)


def attend_kernel(team_ref, mask_ref, gain_q_ref, gain_k_ref, *refs):
    *cached_refs, out_ref, packed_ref = refs
    shard = team_ref.shape[1] - 16
    members = team_ref.shape[0]
    lane = lax.broadcasted_iota(jnp.int32, (16, LANES), 1)
    row = lax.broadcasted_iota(jnp.int32, (16, LANES), 0)
    fresh = [team_ref[c, shard:, :].astype(f32) for c in range(members)]
    features = jnp.concatenate([team_ref[c, :shard, :] for c in range(members)], axis=0)
    open_key = mask_ref[...] > 0.0
    blocks = [r[i].astype(f32) for r in cached_refs for i in range(r.shape[0])]
    half = blocks[0].shape[0] // 2
    cached_keys = jnp.concatenate([b[:half] for b in blocks], axis=0).astype(bf16)
    cached_values = jnp.concatenate([b[half:] for b in blocks], axis=0).astype(bf16)
    sums = jnp.zeros((16, LANES), f32)
    for h in range(TEAM_HEADS):
        query = features[h * HEAD_DIM : (h + 1) * HEAD_DIM].astype(f32)
        scale = lax.rsqrt(jnp.mean(query * query, axis=0, keepdims=True) + eps_norm)
        query = (query * scale * gain_q_ref[...] * HEAD_DIM ** (-0.5)).astype(bf16)
        key = jnp.zeros((16, LANES), f32)
        value = jnp.zeros((16, LANES), f32)
        for c in range(members):
            start = c * shard - h * HEAD_DIM
            if start <= -shard or start >= HEAD_DIM:
                continue
            here = (lane >= start) & (lane < start + shard)
            key = jnp.where(here, pltpu.roll(fresh[c], start % LANES, 1), key)
            value = jnp.where(here, pltpu.roll(fresh[c], (start - shard) % LANES, 1), value)
        scale = lax.rsqrt(jnp.mean(key * key, axis=1, keepdims=True) + eps_norm)
        key = (key * scale * gain_k_ref[...]).astype(bf16)
        cached_key = cached_keys[:, h * HEAD_DIM : (h + 1) * HEAD_DIM]
        cached_value = cached_values[:, h * HEAD_DIM : (h + 1) * HEAD_DIM]
        scores = jnp.dot(cached_key, query, preferred_element_type=f32)
        probs = jnp.exp(jnp.where(open_key, scores, -1e30))
        fresh_probs = jnp.exp(jnp.dot(key, query, preferred_element_type=f32))
        total = jnp.sum(probs, axis=0, keepdims=True) + jnp.sum(fresh_probs, axis=0, keepdims=True)
        sums = jnp.where(row == h, total, sums)
        contract = (((0,), (0,)), ((), ()))
        weighted = lax.dot_general(
            cached_value, probs.astype(bf16), contract, preferred_element_type=f32
        ) + lax.dot_general(
            value.astype(bf16), fresh_probs.astype(bf16), contract, preferred_element_type=f32
        )
        packed_ref[h * HEAD_DIM : (h + 1) * HEAD_DIM, :] = weighted.astype(bf16)
    for c in range(members):
        out_ref[c, :shard, :] = packed_ref[c * shard : (c + 1) * shard, :]
        out_ref[c, shard:, :] = sums.astype(bf16)


def attend(team, cached, mask, gains):
    whole = pl.BlockSpec(memory_space=pltpu.VMEM)
    return pl.pallas_call(
        attend_kernel,
        out_shape=jax.ShapeDtypeStruct(team.shape, bf16),
        in_specs=[whole] * (4 + len(cached)),
        out_specs=whole,
        scratch_shapes=[pltpu.VMEM((TEAM_HEADS * HEAD_DIM, LANES), bf16)],
        compiler_params=pltpu.CompilerParams(vmem_limit_bytes=8 * 1024 * 1024),
    )(team, mask, gains[0][:, None], gains[1][None, :], *cached)


def gathered(block, groups):
    size = len(groups[0])
    spread = jnp.broadcast_to(block[None], (size,) + block.shape)
    spread = lax.all_to_all(spread, "tp", 0, 0, axis_index_groups=groups)
    return spread.reshape((size * block.shape[0],) + block.shape[1:])


def summed_over(block, groups):
    size = len(groups[0])
    parts = block.astype(bf16).reshape((size, block.shape[0] // size) + block.shape[1:])
    parts = lax.all_to_all(parts, "tp", 0, 0, axis_index_groups=groups)
    return jnp.sum(parts.astype(f32), axis=0)


def local(
    in_flight, w_qkv, w_mlp, w_attn_out, w_mlp_out, modulation, qk_gain, context_kv, text_len
):
    tp_count = lax.axis_size("tp")
    tp_index = lax.axis_index("tp")
    rows = in_flight.shape[1]
    tokens = rows * tp_count
    width = w_attn_out.shape[2]
    shard = w_attn_out.shape[1]
    ctx_local = context_kv.shape[2]
    teams = tp_count // TEAM
    team_width = TEAM * shard
    member = tp_index % TEAM
    z_count, x_count = 2 * TEAM, tp_count // (2 * TEAM)
    xs, hs, two = range(x_count), range(z_count // 2), range(2)
    far = [[z_count * x + 2 * h + l for h in hs] for x in xs for l in two]
    blocks = [[z_count * x + 2 * h + l for x in xs for l in two] for h in hs]
    inside = [[TEAM * t + m for m in range(TEAM)] for t in range(teams)]
    shift_scale = modulation.reshape(3, 1, width)
    gains = qk_gain[0]
    weight_qkv = w_qkv[0].reshape(3 * shard, width)
    weight_mlp = w_mlp[0]
    weight_attn = w_attn_out[0]
    weight_down = w_mlp_out[0]

    half_team = TEAM // 2
    partner = [
        z + TEAM + half_team if z < half_team else z + half_team if z < TEAM
        else z - half_team if z < TEAM + half_team else z - TEAM - half_team
        for z in range(z_count)
    ]
    x_here, z_here = tp_index // z_count, tp_index % z_count
    z_partner = jnp.where(
        z_here < TEAM,
        z_here + jnp.where(z_here < half_team, TEAM + half_team, half_team),
        z_here - jnp.where(z_here < TEAM + half_team, half_team, TEAM + half_team),
    )
    upper = z_here >= TEAM
    slot = jnp.arange(teams * ctx_local, dtype=jnp.int32)
    own_z = slot < x_count * ctx_local
    source = z_count * ((x_here - slot // ctx_local % x_count) % x_count)
    source = source + jnp.where(own_z, z_here, z_partner)
    position = ctx_local * source + slot % ctx_local
    cached_mask = ((position >= TXT) | (position < text_len[0])).astype(f32)
    cached_mask = jnp.broadcast_to(cached_mask[:, None], (teams * ctx_local, LANES))

    current = in_flight[0]
    block = spread(current, shift_scale, len(hs), 2)
    block, flat = lax.optimization_barrier((block, context_kv[0]))
    flat = flat.reshape(2 * ctx_local, width)
    by_x = []
    for step in range(x_count):
        part = lax.dynamic_slice_in_dim(
            flat, (x_here + step) % x_count * 2 * team_width, 2 * team_width, 1
        )
        if step:
            route = [
                (z_count * x + z, z_count * ((x + step) % x_count) + z)
                for x in range(x_count) for z in range(z_count)
            ]
            part = lax.ppermute(part, "tp", route)
        by_x.append(part)
    by_x = jnp.stack(by_x)
    keep = jnp.where(upper, by_x[:, :, team_width:], by_x[:, :, :team_width])
    give = jnp.where(upper, by_x[:, :, :team_width], by_x[:, :, team_width:])

    for tick_number in range(TICKS):
        if tick_number == 0:
            normed = lax.all_to_all(block, "tp", 0, 0, axis_index_groups=far)
            normed = normed[:, : block.shape[1] // 2].reshape(-1, width)
            route = [(z_count * x + z, z_count * x + partner[z]) for x in xs for z in range(z_count)]
            got = [
                lax.ppermute(part, "tp", route)
                for part in (give[: x_count // 2], give[x_count // 2 :])
            ]
            normed = gathered(normed, blocks)
            normed, got[0] = lax.optimization_barrier((normed, got[0]))
            cached = [keep] + got
        else:
            block = spread(current, shift_scale, len(hs))
            normed = lax.all_to_all(block, "tp", 0, 0, axis_index_groups=far)
            normed = gathered(normed.reshape(-1, width), blocks)
        team = project(normed, weight_qkv)
        team = lax.all_to_all(team, "tp", 0, 0, axis_index_groups=inside)
        parts = attend(team, cached, cached_mask, gains)
        parts = lax.all_to_all(parts, "tp", 0, 0, axis_index_groups=inside)
        hidden = jax.nn.gelu(
            lax.dot_general(
                normed, weight_mlp, (((1,), (1,)), ((), ())), preferred_element_type=f32
            ),
            approximate=True,
        ).astype(bf16)
        hidden = lax.optimization_barrier(hidden)
        forward = jnp.dot(hidden, weight_down, preferred_element_type=f32)
        forward = lax.optimization_barrier(forward)
        branch = finish(member[None], parts, weight_attn, forward, shift_scale)
        branch = summed_over(branch, blocks)
        branch = summed_over(branch.reshape(-1, LANES), far).reshape(rows, width)
        finished = (current.astype(f32) + branch).astype(bf16)
        current = shifted(finished, "pipe", 1)
    return current[None]


def solution(mesh):
    placed = (
        P("pipe", "tp", None),
        P("pipe", None, "tp", None),
        P("pipe", "tp", None),
        P("pipe", "tp", None),
        P("pipe", "tp", None),
        P("pipe", None, None),
        P("pipe", None, None),
        P("pipe", None, "tp", None),
        P(),
    )
    return jax.shard_map(
        local, mesh=mesh, in_specs=placed, out_specs=P("pipe", "tp", None), check_vma=False
    )
```

```python
import jax
import jax.numpy as jnp
from jax import lax
from jax.experimental import pallas as pl
from jax.experimental.pallas import tpu as pltpu
from jax.sharding import PartitionSpec as P

HEADS = 24
HEAD_DIM = 128
TICKS = 2
TXT = 512
TEAM = 8
TEAM_HEADS = 3
LANES = 128

eps_norm = 1e-06
f32 = jnp.float32
bf16 = jnp.bfloat16


def shifted(block, axis, distance):
    size = lax.axis_size(axis)
    return lax.ppermute(block, axis, [((i - distance) % size, i) for i in range(size)])


def spread_kernel(rows_ref, modulation_ref, out_ref, block_ref):
    x = rows_ref[...].astype(f32)
    centred = x - jnp.mean(x, axis=1, keepdims=True)
    variance = jnp.mean(centred * centred, axis=1, keepdims=True)
    normed = centred * lax.rsqrt(variance + eps_norm)
    normed = normed * (1.0 + modulation_ref[1]) + modulation_ref[0]
    rows, width = x.shape
    pieces = width // LANES
    for r in range(rows):
        for p in range(pieces):
            at = r * pieces + p
            block_ref[at : at + 1, :] = normed[r : r + 1, p * LANES : (p + 1) * LANES]
    block = block_ref[...].astype(bf16)
    for j in range(out_ref.shape[0]):
        out_ref[j] = block


def spread(rows, modulation, receivers):
    whole = pl.BlockSpec(memory_space=pltpu.VMEM)
    lines = rows.shape[0] * rows.shape[1] // LANES
    return pl.pallas_call(
        spread_kernel,
        out_shape=jax.ShapeDtypeStruct((receivers, lines, LANES), bf16),
        in_specs=[whole] * 2,
        out_specs=whole,
        scratch_shapes=[pltpu.VMEM((lines, LANES), f32)],
        compiler_params=pltpu.CompilerParams(vmem_limit_bytes=8 * 1024 * 1024),
    )(rows, modulation)


def finish_kernel(member_ref, parts_ref, weight_ref, forward_ref, modulation_ref, out_ref):
    shard, width = weight_ref.shape
    summed = parts_ref[0].astype(f32)
    for c in range(1, parts_ref.shape[0]):
        summed = summed + parts_ref[c].astype(f32)
    feature = member_ref[0] * shard + lax.broadcasted_iota(jnp.int32, (shard, LANES), 0)
    total = jnp.broadcast_to(summed[shard + TEAM_HEADS - 1][None], (shard, LANES))
    for h in range(TEAM_HEADS - 2, -1, -1):
        total = jnp.where(feature < (h + 1) * HEAD_DIM, summed[shard + h][None], total)
    attention = (summed[:shard] / total).astype(bf16)
    branch = lax.dot_general(
        attention, weight_ref[...], (((0,), (0,)), ((), ())), preferred_element_type=f32
    )
    out_ref[...] = ((branch + forward_ref[...]) * modulation_ref[2]).astype(bf16)


def finish(member, parts, weights, forward, modulation):
    whole = pl.BlockSpec(memory_space=pltpu.VMEM)
    return pl.pallas_call(
        finish_kernel,
        out_shape=jax.ShapeDtypeStruct(forward.shape, bf16),
        in_specs=[pl.BlockSpec(memory_space=pltpu.SMEM)] + [whole] * 4,
        out_specs=whole,
        compiler_params=pltpu.CompilerParams(vmem_limit_bytes=8 * 1024 * 1024),
    )(member, parts, weights, forward, modulation)


def project_kernel(normed_ref, weight_ref, out_ref):
    members = out_ref.shape[0]
    shard = weight_ref.shape[0] // 3
    contract = (((1,), (1,)), ((), ()))
    query = lax.dot_general(
        weight_ref[:shard], normed_ref[...], contract, preferred_element_type=f32
    ).astype(bf16)
    others = lax.dot_general(
        normed_ref[...], weight_ref[shard:], contract, preferred_element_type=f32
    ).astype(bf16)
    for c in range(members):
        out_ref[c, :shard, :] = query
        out_ref[c, shard:, : 2 * shard] = others[16 * c : 16 * c + 16]
        out_ref[c, shard:, 2 * shard :] = jnp.zeros((16, LANES - 2 * shard), bf16)


def project(normed, weights):
    whole = pl.BlockSpec(memory_space=pltpu.VMEM)
    return pl.pallas_call(
        project_kernel,
        out_shape=jax.ShapeDtypeStruct((TEAM, weights.shape[0] // 3 + 16, LANES), bf16),
        in_specs=[whole] * 2,
        out_specs=whole,
        compiler_params=pltpu.CompilerParams(vmem_limit_bytes=8 * 1024 * 1024),
    )(normed, weights)


def attend_kernel(team_ref, mask_ref, gain_q_ref, gain_k_ref, *refs):
    *cached_refs, out_ref, packed_ref = refs
    shard = team_ref.shape[1] - 16
    members = team_ref.shape[0]
    lane = lax.broadcasted_iota(jnp.int32, (16, LANES), 1)
    row = lax.broadcasted_iota(jnp.int32, (16, LANES), 0)
    fresh = [team_ref[c, shard:, :].astype(f32) for c in range(members)]
    features = jnp.concatenate([team_ref[c, :shard, :] for c in range(members)], axis=0)
    open_key = mask_ref[...] > 0.0
    blocks = [r[i].astype(f32) for r in cached_refs for i in range(r.shape[0])]
    half = blocks[0].shape[0] // 2
    cached_keys = jnp.concatenate([b[:half] for b in blocks], axis=0).astype(bf16)
    cached_values = jnp.concatenate([b[half:] for b in blocks], axis=0).astype(bf16)
    sums = jnp.zeros((16, LANES), f32)
    for h in range(TEAM_HEADS):
        query = features[h * HEAD_DIM : (h + 1) * HEAD_DIM].astype(f32)
        scale = lax.rsqrt(jnp.mean(query * query, axis=0, keepdims=True) + eps_norm)
        query = (query * scale * gain_q_ref[...] * HEAD_DIM ** (-0.5)).astype(bf16)
        key = jnp.zeros((16, LANES), f32)
        value = jnp.zeros((16, LANES), f32)
        for c in range(members):
            start = c * shard - h * HEAD_DIM
            if start <= -shard or start >= HEAD_DIM:
                continue
            here = (lane >= start) & (lane < start + shard)
            key = jnp.where(here, pltpu.roll(fresh[c], start % LANES, 1), key)
            value = jnp.where(here, pltpu.roll(fresh[c], (start - shard) % LANES, 1), value)
        scale = lax.rsqrt(jnp.mean(key * key, axis=1, keepdims=True) + eps_norm)
        key = (key * scale * gain_k_ref[...]).astype(bf16)
        cached_key = cached_keys[:, h * HEAD_DIM : (h + 1) * HEAD_DIM]
        cached_value = cached_values[:, h * HEAD_DIM : (h + 1) * HEAD_DIM]
        scores = jnp.dot(cached_key, query, preferred_element_type=f32)
        probs = jnp.exp(jnp.where(open_key, scores, -1e30))
        fresh_probs = jnp.exp(jnp.dot(key, query, preferred_element_type=f32))
        total = jnp.sum(probs, axis=0, keepdims=True) + jnp.sum(fresh_probs, axis=0, keepdims=True)
        sums = jnp.where(row == h, total, sums)
        contract = (((0,), (0,)), ((), ()))
        weighted = lax.dot_general(
            cached_value, probs.astype(bf16), contract, preferred_element_type=f32
        ) + lax.dot_general(
            value.astype(bf16), fresh_probs.astype(bf16), contract, preferred_element_type=f32
        )
        packed_ref[h * HEAD_DIM : (h + 1) * HEAD_DIM, :] = weighted.astype(bf16)
    for c in range(members):
        out_ref[c, :shard, :] = packed_ref[c * shard : (c + 1) * shard, :]
        out_ref[c, shard:, :] = sums.astype(bf16)


def attend(team, cached, mask, gains):
    whole = pl.BlockSpec(memory_space=pltpu.VMEM)
    return pl.pallas_call(
        attend_kernel,
        out_shape=jax.ShapeDtypeStruct(team.shape, bf16),
        in_specs=[whole] * (4 + len(cached)),
        out_specs=whole,
        scratch_shapes=[pltpu.VMEM((TEAM_HEADS * HEAD_DIM, LANES), bf16)],
        compiler_params=pltpu.CompilerParams(vmem_limit_bytes=8 * 1024 * 1024),
    )(team, mask, gains[0][:, None], gains[1][None, :], *cached)


def gathered(block, groups):
    size = len(groups[0])
    spread = jnp.broadcast_to(block[None], (size,) + block.shape)
    spread = lax.all_to_all(spread, "tp", 0, 0, axis_index_groups=groups)
    return spread.reshape((size * block.shape[0],) + block.shape[1:])


def summed_over(block, groups):
    size = len(groups[0])
    parts = block.astype(bf16).reshape((size, block.shape[0] // size) + block.shape[1:])
    parts = lax.all_to_all(parts, "tp", 0, 0, axis_index_groups=groups)
    return jnp.sum(parts.astype(f32), axis=0)


def local(
    in_flight, w_qkv, w_mlp, w_attn_out, w_mlp_out, modulation, qk_gain, context_kv, text_len
):
    tp_count = lax.axis_size("tp")
    tp_index = lax.axis_index("tp")
    rows = in_flight.shape[1]
    tokens = rows * tp_count
    width = w_attn_out.shape[2]
    shard = w_attn_out.shape[1]
    ctx_local = context_kv.shape[2]
    teams = tp_count // TEAM
    team_width = TEAM * shard
    member = tp_index % TEAM
    z_count, x_count = 2 * TEAM, tp_count // (2 * TEAM)
    xs, hs, two = range(x_count), range(z_count // 2), range(2)
    along_z = [[z_count * x + 2 * h + l for l in two for h in hs] for x in xs]
    along_x = [[z_count * x + z for x in xs] for z in range(z_count)]
    far = [[z_count * x + 2 * h + l for h in hs] for x in xs for l in two]
    blocks = [[z_count * x + 2 * h + l for x in xs for l in two] for h in hs]
    inside = [[TEAM * t + m for m in range(TEAM)] for t in range(teams)]
    shift_scale = modulation.reshape(3, 1, width)
    gains = qk_gain[0]
    weight_qkv = w_qkv[0].reshape(3 * shard, width)
    weight_mlp = w_mlp[0]
    weight_attn = w_attn_out[0]
    weight_down = w_mlp_out[0]

    half_team = TEAM // 2
    partner = [
        z + TEAM + half_team if z < half_team else z + half_team if z < TEAM
        else z - half_team if z < TEAM + half_team else z - TEAM - half_team
        for z in range(z_count)
    ]
    x_here, z_here = tp_index // z_count, tp_index % z_count
    z_partner = jnp.where(
        z_here < TEAM,
        z_here + jnp.where(z_here < half_team, TEAM + half_team, half_team),
        z_here - jnp.where(z_here < TEAM + half_team, half_team, TEAM + half_team),
    )
    upper = z_here >= TEAM
    slot = jnp.arange(teams * ctx_local, dtype=jnp.int32)
    own_z = slot < x_count * ctx_local
    source = z_count * ((x_here - slot // ctx_local % x_count) % x_count)
    source = source + jnp.where(own_z, z_here, z_partner)
    position = ctx_local * source + slot % ctx_local
    cached_mask = ((position >= TXT) | (position < text_len[0])).astype(f32)
    cached_mask = jnp.broadcast_to(cached_mask[:, None], (teams * ctx_local, LANES))

    current = in_flight[0]
    block = spread(current, shift_scale, z_count)
    block, flat = lax.optimization_barrier((block, context_kv[0]))
    flat = flat.reshape(2 * ctx_local, width)
    by_x = []
    for step in range(x_count):
        part = lax.dynamic_slice_in_dim(
            flat, (x_here + step) % x_count * 2 * team_width, 2 * team_width, 1
        )
        if step:
            route = [
                (z_count * x + z, z_count * ((x + step) % x_count) + z)
                for x in range(x_count) for z in range(z_count)
            ]
            part = lax.ppermute(part, "tp", route)
        by_x.append(part)
    by_x = jnp.stack(by_x)
    keep = jnp.where(upper, by_x[:, :, team_width:], by_x[:, :, :team_width])
    give = jnp.where(upper, by_x[:, :, :team_width], by_x[:, :, team_width:])

    for tick_number in range(TICKS):
        if tick_number == 0:
            normed = lax.all_to_all(block, "tp", 0, 0, axis_index_groups=along_z)
            normed = normed.reshape(-1, width)
            route = [(z_count * x + z, z_count * x + partner[z]) for x in xs for z in range(z_count)]
            got = [
                lax.ppermute(part, "tp", route)
                for part in (give[: x_count // 2], give[x_count // 2 :])
            ]
            normed = gathered(normed, along_x)
            normed, got[0] = lax.optimization_barrier((normed, got[0]))
            cached = [keep] + got
        else:
            block = spread(current, shift_scale, len(hs))
            normed = lax.all_to_all(block, "tp", 0, 0, axis_index_groups=far)
            normed = gathered(normed.reshape(-1, width), blocks)
        team = project(normed, weight_qkv)
        team = lax.all_to_all(team, "tp", 0, 0, axis_index_groups=inside)
        parts = attend(team, cached, cached_mask, gains)
        parts = lax.all_to_all(parts, "tp", 0, 0, axis_index_groups=inside)
        hidden = jax.nn.gelu(
            lax.dot_general(
                normed, weight_mlp, (((1,), (1,)), ((), ())), preferred_element_type=f32
            ),
            approximate=True,
        ).astype(bf16)
        hidden = lax.optimization_barrier(hidden)
        forward = jnp.dot(hidden, weight_down, preferred_element_type=f32)
        forward = lax.optimization_barrier(forward)
        branch = finish(member[None], parts, weight_attn, forward, shift_scale)
        branch = summed_over(branch, along_x)
        branch = summed_over(branch.reshape(-1, LANES), along_z).reshape(rows, width)
        finished = (current.astype(f32) + branch).astype(bf16)
        current = shifted(finished, "pipe", 1)
    return current[None]


def solution(mesh):
    placed = (
        P("pipe", "tp", None),
        P("pipe", None, "tp", None),
        P("pipe", "tp", None),
        P("pipe", "tp", None),
        P("pipe", "tp", None),
        P("pipe", None, None),
        P("pipe", None, None),
        P("pipe", None, "tp", None),
        P(),
    )
    return jax.shard_map(
        local, mesh=mesh, in_specs=placed, out_specs=P("pipe", "tp", None), check_vma=False
    )
```

```python
import jax
import jax.numpy as jnp
from jax import lax
from jax.experimental import pallas as pl
from jax.experimental.pallas import tpu as pltpu
from jax.sharding import PartitionSpec as P

HEADS = 24
HEAD_DIM = 128
TICKS = 2
TXT = 512
TEAM = 8
TEAM_HEADS = 3
LANES = 128

eps_norm = 1e-06
f32 = jnp.float32
bf16 = jnp.bfloat16


def shifted(block, axis, distance):
    size = lax.axis_size(axis)
    return lax.ppermute(block, axis, [((i - distance) % size, i) for i in range(size)])


def spread_kernel(rows_ref, modulation_ref, out_ref, block_ref):
    x = rows_ref[...].astype(f32)
    centred = x - jnp.mean(x, axis=1, keepdims=True)
    variance = jnp.mean(centred * centred, axis=1, keepdims=True)
    normed = centred * lax.rsqrt(variance + eps_norm)
    normed = normed * (1.0 + modulation_ref[1]) + modulation_ref[0]
    rows, width = x.shape
    pieces = width // LANES
    for r in range(rows):
        for p in range(pieces):
            at = r * pieces + p
            block_ref[at : at + 1, :] = normed[r : r + 1, p * LANES : (p + 1) * LANES]
    block = block_ref[...].astype(bf16)
    for j in range(out_ref.shape[0]):
        out_ref[j] = block


def spread(rows, modulation, receivers):
    whole = pl.BlockSpec(memory_space=pltpu.VMEM)
    lines = rows.shape[0] * rows.shape[1] // LANES
    return pl.pallas_call(
        spread_kernel,
        out_shape=jax.ShapeDtypeStruct((receivers, lines, LANES), bf16),
        in_specs=[whole] * 2,
        out_specs=whole,
        scratch_shapes=[pltpu.VMEM((lines, LANES), f32)],
        compiler_params=pltpu.CompilerParams(vmem_limit_bytes=8 * 1024 * 1024),
    )(rows, modulation)


def finish_kernel(member_ref, parts_ref, weight_ref, forward_ref, modulation_ref, out_ref):
    shard, width = weight_ref.shape
    summed = parts_ref[0].astype(f32)
    for c in range(1, parts_ref.shape[0]):
        summed = summed + parts_ref[c].astype(f32)
    feature = member_ref[0] * shard + lax.broadcasted_iota(jnp.int32, (shard, LANES), 0)
    total = jnp.broadcast_to(summed[shard + TEAM_HEADS - 1][None], (shard, LANES))
    for h in range(TEAM_HEADS - 2, -1, -1):
        total = jnp.where(feature < (h + 1) * HEAD_DIM, summed[shard + h][None], total)
    attention = (summed[:shard] / total).astype(bf16)
    branch = lax.dot_general(
        attention, weight_ref[...], (((0,), (0,)), ((), ())), preferred_element_type=f32
    )
    out_ref[...] = ((branch + forward_ref[...]) * modulation_ref[2]).astype(bf16)


def finish(member, parts, weights, forward, modulation):
    whole = pl.BlockSpec(memory_space=pltpu.VMEM)
    return pl.pallas_call(
        finish_kernel,
        out_shape=jax.ShapeDtypeStruct(forward.shape, bf16),
        in_specs=[pl.BlockSpec(memory_space=pltpu.SMEM)] + [whole] * 4,
        out_specs=whole,
        compiler_params=pltpu.CompilerParams(vmem_limit_bytes=8 * 1024 * 1024),
    )(member, parts, weights, forward, modulation)


def project_kernel(normed_ref, weight_ref, out_ref):
    members = out_ref.shape[0]
    shard = weight_ref.shape[0] // 3
    contract = (((1,), (1,)), ((), ()))
    query = lax.dot_general(
        weight_ref[:shard], normed_ref[...], contract, preferred_element_type=f32
    ).astype(bf16)
    others = lax.dot_general(
        normed_ref[...], weight_ref[shard:], contract, preferred_element_type=f32
    ).astype(bf16)
    for c in range(members):
        out_ref[c, :shard, :] = query
        out_ref[c, shard:, : 2 * shard] = others[16 * c : 16 * c + 16]
        out_ref[c, shard:, 2 * shard :] = jnp.zeros((16, LANES - 2 * shard), bf16)


def project(normed, weights):
    whole = pl.BlockSpec(memory_space=pltpu.VMEM)
    return pl.pallas_call(
        project_kernel,
        out_shape=jax.ShapeDtypeStruct((TEAM, weights.shape[0] // 3 + 16, LANES), bf16),
        in_specs=[whole] * 2,
        out_specs=whole,
        compiler_params=pltpu.CompilerParams(vmem_limit_bytes=8 * 1024 * 1024),
    )(normed, weights)


def attend_kernel(team_ref, mask_ref, gain_q_ref, gain_k_ref, *refs):
    *cached_refs, out_ref, packed_ref = refs
    shard = team_ref.shape[1] - 16
    members = team_ref.shape[0]
    lane = lax.broadcasted_iota(jnp.int32, (16, LANES), 1)
    row = lax.broadcasted_iota(jnp.int32, (16, LANES), 0)
    fresh = [team_ref[c, shard:, :].astype(f32) for c in range(members)]
    features = jnp.concatenate([team_ref[c, :shard, :] for c in range(members)], axis=0)
    open_key = mask_ref[...] > 0.0
    blocks = [r[i].astype(f32) for r in cached_refs for i in range(r.shape[0])]
    half = blocks[0].shape[0] // 2
    cached_keys = jnp.concatenate([b[:half] for b in blocks], axis=0).astype(bf16)
    cached_values = jnp.concatenate([b[half:] for b in blocks], axis=0).astype(bf16)
    sums = jnp.zeros((16, LANES), f32)
    for h in range(TEAM_HEADS):
        query = features[h * HEAD_DIM : (h + 1) * HEAD_DIM].astype(f32)
        scale = lax.rsqrt(jnp.mean(query * query, axis=0, keepdims=True) + eps_norm)
        query = (query * scale * gain_q_ref[...] * HEAD_DIM ** (-0.5)).astype(bf16)
        key = jnp.zeros((16, LANES), f32)
        value = jnp.zeros((16, LANES), f32)
        for c in range(members):
            start = c * shard - h * HEAD_DIM
            if start <= -shard or start >= HEAD_DIM:
                continue
            here = (lane >= start) & (lane < start + shard)
            key = jnp.where(here, pltpu.roll(fresh[c], start % LANES, 1), key)
            value = jnp.where(here, pltpu.roll(fresh[c], (start - shard) % LANES, 1), value)
        scale = lax.rsqrt(jnp.mean(key * key, axis=1, keepdims=True) + eps_norm)
        key = (key * scale * gain_k_ref[...]).astype(bf16)
        cached_key = cached_keys[:, h * HEAD_DIM : (h + 1) * HEAD_DIM]
        cached_value = cached_values[:, h * HEAD_DIM : (h + 1) * HEAD_DIM]
        scores = jnp.dot(cached_key, query, preferred_element_type=f32)
        probs = jnp.exp(jnp.where(open_key, scores, -1e30))
        fresh_probs = jnp.exp(jnp.dot(key, query, preferred_element_type=f32))
        total = jnp.sum(probs, axis=0, keepdims=True) + jnp.sum(fresh_probs, axis=0, keepdims=True)
        sums = jnp.where(row == h, total, sums)
        contract = (((0,), (0,)), ((), ()))
        weighted = lax.dot_general(
            cached_value, probs.astype(bf16), contract, preferred_element_type=f32
        ) + lax.dot_general(
            value.astype(bf16), fresh_probs.astype(bf16), contract, preferred_element_type=f32
        )
        packed_ref[h * HEAD_DIM : (h + 1) * HEAD_DIM, :] = weighted.astype(bf16)
    for c in range(members):
        out_ref[c, :shard, :] = packed_ref[c * shard : (c + 1) * shard, :]
        out_ref[c, shard:, :] = sums.astype(bf16)


def attend(team, cached, mask, gains):
    whole = pl.BlockSpec(memory_space=pltpu.VMEM)
    return pl.pallas_call(
        attend_kernel,
        out_shape=jax.ShapeDtypeStruct(team.shape, bf16),
        in_specs=[whole] * (4 + len(cached)),
        out_specs=whole,
        scratch_shapes=[pltpu.VMEM((TEAM_HEADS * HEAD_DIM, LANES), bf16)],
        compiler_params=pltpu.CompilerParams(vmem_limit_bytes=8 * 1024 * 1024),
    )(team, mask, gains[0][:, None], gains[1][None, :], *cached)


def gathered(block, groups):
    size = len(groups[0])
    spread = jnp.broadcast_to(block[None], (size,) + block.shape)
    spread = lax.all_to_all(spread, "tp", 0, 0, axis_index_groups=groups)
    return spread.reshape((size * block.shape[0],) + block.shape[1:])


def summed_over(block, groups):
    size = len(groups[0])
    parts = block.astype(bf16).reshape((size, block.shape[0] // size) + block.shape[1:])
    parts = lax.all_to_all(parts, "tp", 0, 0, axis_index_groups=groups)
    return jnp.sum(parts.astype(f32), axis=0)


def local(
    in_flight, w_qkv, w_mlp, w_attn_out, w_mlp_out, modulation, qk_gain, context_kv, text_len
):
    tp_count = lax.axis_size("tp")
    tp_index = lax.axis_index("tp")
    rows = in_flight.shape[1]
    tokens = rows * tp_count
    width = w_attn_out.shape[2]
    shard = w_attn_out.shape[1]
    ctx_local = context_kv.shape[2]
    teams = tp_count // TEAM
    team_width = TEAM * shard
    member = tp_index % TEAM
    z_count, x_count = 2 * TEAM, tp_count // (2 * TEAM)
    xs, hs, two = range(x_count), range(z_count // 2), range(2)
    along_z = [[z_count * x + 2 * h + l for l in two for h in hs] for x in xs]
    along_x = [[z_count * x + z for x in xs] for z in range(z_count)]
    far = [[z_count * x + 2 * h + l for h in hs] for x in xs for l in two]
    blocks = [
        [z_count * x + 2 * h for x in xs] + [z_count * x + 2 * h + 1 for x in reversed(xs)]
        for h in hs
    ]
    inside = [[TEAM * t + m for m in range(TEAM)] for t in range(teams)]
    shift_scale = modulation.reshape(3, 1, width)
    gains = qk_gain[0]
    weight_qkv = w_qkv[0].reshape(3 * shard, width)
    weight_mlp = w_mlp[0]
    weight_attn = w_attn_out[0]
    weight_down = w_mlp_out[0]

    half_team = TEAM // 2
    partner = [
        z + TEAM + half_team if z < half_team else z + half_team if z < TEAM
        else z - half_team if z < TEAM + half_team else z - TEAM - half_team
        for z in range(z_count)
    ]
    x_here, z_here = tp_index // z_count, tp_index % z_count
    z_partner = jnp.where(
        z_here < TEAM,
        z_here + jnp.where(z_here < half_team, TEAM + half_team, half_team),
        z_here - jnp.where(z_here < TEAM + half_team, half_team, TEAM + half_team),
    )
    upper = z_here >= TEAM
    slot = jnp.arange(teams * ctx_local, dtype=jnp.int32)
    own_z = slot < x_count * ctx_local
    source = z_count * ((x_here - slot // ctx_local % x_count) % x_count)
    source = source + jnp.where(own_z, z_here, z_partner)
    position = ctx_local * source + slot % ctx_local
    cached_mask = ((position >= TXT) | (position < text_len[0])).astype(f32)
    cached_mask = jnp.broadcast_to(cached_mask[:, None], (teams * ctx_local, LANES))

    current = in_flight[0]
    block = spread(current, shift_scale, z_count)
    block, flat = lax.optimization_barrier((block, context_kv[0]))
    flat = flat.reshape(2 * ctx_local, width)
    by_x = []
    for step in range(x_count):
        part = lax.dynamic_slice_in_dim(
            flat, (x_here + step) % x_count * 2 * team_width, 2 * team_width, 1
        )
        if step:
            route = [
                (z_count * x + z, z_count * ((x + step) % x_count) + z)
                for x in range(x_count) for z in range(z_count)
            ]
            part = lax.ppermute(part, "tp", route)
        by_x.append(part)
    by_x = jnp.stack(by_x)
    keep = jnp.where(upper, by_x[:, :, team_width:], by_x[:, :, :team_width])
    give = jnp.where(upper, by_x[:, :, :team_width], by_x[:, :, team_width:])

    for tick_number in range(TICKS):
        if tick_number == 0:
            normed = lax.all_to_all(block, "tp", 0, 0, axis_index_groups=along_z)
            normed = normed.reshape(-1, width)
            route = [(z_count * x + z, z_count * x + partner[z]) for x in xs for z in range(z_count)]
            got = [
                lax.ppermute(part, "tp", route)
                for part in (give[: x_count // 2], give[x_count // 2 :])
            ]
            normed = gathered(normed, along_x)
            normed, got[0] = lax.optimization_barrier((normed, got[0]))
            cached = [keep] + got
        else:
            block = spread(current, shift_scale, len(hs))
            normed = lax.all_to_all(block, "tp", 0, 0, axis_index_groups=far)
            normed = gathered(normed.reshape(-1, width), blocks)
        team = project(normed, weight_qkv)
        team = lax.all_to_all(team, "tp", 0, 0, axis_index_groups=inside)
        parts = attend(team, cached, cached_mask, gains)
        parts = lax.all_to_all(parts, "tp", 0, 0, axis_index_groups=inside)
        hidden = jax.nn.gelu(
            lax.dot_general(
                normed, weight_mlp, (((1,), (1,)), ((), ())), preferred_element_type=f32
            ),
            approximate=True,
        ).astype(bf16)
        hidden = lax.optimization_barrier(hidden)
        forward = jnp.dot(hidden, weight_down, preferred_element_type=f32)
        forward = lax.optimization_barrier(forward)
        branch = finish(member[None], parts, weight_attn, forward, shift_scale)
        near_groups, far_groups = (blocks, far) if tick_number else (along_x, along_z)
        branch = summed_over(branch, near_groups)
        branch = summed_over(branch.reshape(-1, LANES), far_groups).reshape(rows, width)
        finished = (current.astype(f32) + branch).astype(bf16)
        current = shifted(finished, "pipe", 1)
    return current[None]


def solution(mesh):
    placed = (
        P("pipe", "tp", None),
        P("pipe", None, "tp", None),
        P("pipe", "tp", None),
        P("pipe", "tp", None),
        P("pipe", "tp", None),
        P("pipe", None, None),
        P("pipe", None, None),
        P("pipe", None, "tp", None),
        P(),
    )
    return jax.shard_map(
        local, mesh=mesh, in_specs=placed, out_specs=P("pipe", "tp", None), check_vma=False
    )
```

```python
import jax
import jax.numpy as jnp
from jax import lax
from jax.experimental import pallas as pl
from jax.experimental.pallas import tpu as pltpu
from jax.sharding import PartitionSpec as P

HEADS = 24
HEAD_DIM = 128
TICKS = 2
TXT = 512
TEAM = 8
TEAM_HEADS = 3
LANES = 128

eps_norm = 1e-06
f32 = jnp.float32
bf16 = jnp.bfloat16


def shifted(block, axis, distance):
    size = lax.axis_size(axis)
    return lax.ppermute(block, axis, [((i - distance) % size, i) for i in range(size)])


def spread_kernel(rows_ref, modulation_ref, out_ref, block_ref):
    x = rows_ref[...].astype(f32)
    centred = x - jnp.mean(x, axis=1, keepdims=True)
    variance = jnp.mean(centred * centred, axis=1, keepdims=True)
    normed = centred * lax.rsqrt(variance + eps_norm)
    normed = normed * (1.0 + modulation_ref[1]) + modulation_ref[0]
    rows, width = x.shape
    pieces = width // LANES
    for r in range(rows):
        for p in range(pieces):
            at = r * pieces + p
            block_ref[at : at + 1, :] = normed[r : r + 1, p * LANES : (p + 1) * LANES]
    block = block_ref[...].astype(bf16)
    for j in range(out_ref.shape[0]):
        out_ref[j] = block


def spread(rows, modulation, receivers):
    whole = pl.BlockSpec(memory_space=pltpu.VMEM)
    lines = rows.shape[0] * rows.shape[1] // LANES
    return pl.pallas_call(
        spread_kernel,
        out_shape=jax.ShapeDtypeStruct((receivers, lines, LANES), bf16),
        in_specs=[whole] * 2,
        out_specs=whole,
        scratch_shapes=[pltpu.VMEM((lines, LANES), f32)],
        compiler_params=pltpu.CompilerParams(vmem_limit_bytes=8 * 1024 * 1024),
    )(rows, modulation)


def finish_kernel(member_ref, parts_ref, weight_ref, forward_ref, modulation_ref, out_ref):
    shard, width = weight_ref.shape
    summed = parts_ref[0].astype(f32)
    for c in range(1, parts_ref.shape[0]):
        summed = summed + parts_ref[c].astype(f32)
    feature = member_ref[0] * shard + lax.broadcasted_iota(jnp.int32, (shard, LANES), 0)
    total = jnp.broadcast_to(summed[shard + TEAM_HEADS - 1][None], (shard, LANES))
    for h in range(TEAM_HEADS - 2, -1, -1):
        total = jnp.where(feature < (h + 1) * HEAD_DIM, summed[shard + h][None], total)
    attention = (summed[:shard] / total).astype(bf16)
    branch = lax.dot_general(
        attention, weight_ref[...], (((0,), (0,)), ((), ())), preferred_element_type=f32
    )
    out_ref[...] = ((branch + forward_ref[...]) * modulation_ref[2]).astype(bf16)


def finish(member, parts, weights, forward, modulation):
    whole = pl.BlockSpec(memory_space=pltpu.VMEM)
    return pl.pallas_call(
        finish_kernel,
        out_shape=jax.ShapeDtypeStruct(forward.shape, bf16),
        in_specs=[pl.BlockSpec(memory_space=pltpu.SMEM)] + [whole] * 4,
        out_specs=whole,
        compiler_params=pltpu.CompilerParams(vmem_limit_bytes=8 * 1024 * 1024),
    )(member, parts, weights, forward, modulation)


def project_kernel(normed_ref, weight_ref, out_ref):
    members = out_ref.shape[0]
    shard = weight_ref.shape[0] // 3
    contract = (((1,), (1,)), ((), ()))
    query = lax.dot_general(
        weight_ref[:shard], normed_ref[...], contract, preferred_element_type=f32
    ).astype(bf16)
    others = lax.dot_general(
        normed_ref[...], weight_ref[shard:], contract, preferred_element_type=f32
    ).astype(bf16)
    for c in range(members):
        out_ref[c, :shard, :] = query
        out_ref[c, shard:, : 2 * shard] = others[16 * c : 16 * c + 16]
        out_ref[c, shard:, 2 * shard :] = jnp.zeros((16, LANES - 2 * shard), bf16)


def project(normed, weights):
    whole = pl.BlockSpec(memory_space=pltpu.VMEM)
    return pl.pallas_call(
        project_kernel,
        out_shape=jax.ShapeDtypeStruct((TEAM, weights.shape[0] // 3 + 16, LANES), bf16),
        in_specs=[whole] * 2,
        out_specs=whole,
        compiler_params=pltpu.CompilerParams(vmem_limit_bytes=8 * 1024 * 1024),
    )(normed, weights)


def attend_kernel(team_ref, mask_ref, gain_q_ref, gain_k_ref, *refs):
    *cached_refs, out_ref, packed_ref = refs
    shard = team_ref.shape[1] - 16
    members = team_ref.shape[0]
    lane = lax.broadcasted_iota(jnp.int32, (16, LANES), 1)
    row = lax.broadcasted_iota(jnp.int32, (16, LANES), 0)
    fresh = [team_ref[c, shard:, :].astype(f32) for c in range(members)]
    features = jnp.concatenate([team_ref[c, :shard, :] for c in range(members)], axis=0)
    open_key = mask_ref[...] > 0.0
    blocks = [r[i].astype(f32) for r in cached_refs for i in range(r.shape[0])]
    half = blocks[0].shape[0] // 2
    cached_keys = jnp.concatenate([b[:half] for b in blocks], axis=0).astype(bf16)
    cached_values = jnp.concatenate([b[half:] for b in blocks], axis=0).astype(bf16)
    sums = jnp.zeros((16, LANES), f32)
    for h in range(TEAM_HEADS):
        query = features[h * HEAD_DIM : (h + 1) * HEAD_DIM].astype(f32)
        scale = lax.rsqrt(jnp.mean(query * query, axis=0, keepdims=True) + eps_norm)
        query = (query * scale * gain_q_ref[...] * HEAD_DIM ** (-0.5)).astype(bf16)
        key = jnp.zeros((16, LANES), f32)
        value = jnp.zeros((16, LANES), f32)
        for c in range(members):
            start = c * shard - h * HEAD_DIM
            if start <= -shard or start >= HEAD_DIM:
                continue
            here = (lane >= start) & (lane < start + shard)
            key = jnp.where(here, pltpu.roll(fresh[c], start % LANES, 1), key)
            value = jnp.where(here, pltpu.roll(fresh[c], (start - shard) % LANES, 1), value)
        scale = lax.rsqrt(jnp.mean(key * key, axis=1, keepdims=True) + eps_norm)
        key = (key * scale * gain_k_ref[...]).astype(bf16)
        cached_key = cached_keys[:, h * HEAD_DIM : (h + 1) * HEAD_DIM]
        cached_value = cached_values[:, h * HEAD_DIM : (h + 1) * HEAD_DIM]
        scores = jnp.dot(cached_key, query, preferred_element_type=f32)
        probs = jnp.exp(jnp.where(open_key, scores, -1e30))
        fresh_probs = jnp.exp(jnp.dot(key, query, preferred_element_type=f32))
        total = jnp.sum(probs, axis=0, keepdims=True) + jnp.sum(fresh_probs, axis=0, keepdims=True)
        sums = jnp.where(row == h, total, sums)
        contract = (((0,), (0,)), ((), ()))
        weighted = lax.dot_general(
            cached_value, probs.astype(bf16), contract, preferred_element_type=f32
        ) + lax.dot_general(
            value.astype(bf16), fresh_probs.astype(bf16), contract, preferred_element_type=f32
        )
        packed_ref[h * HEAD_DIM : (h + 1) * HEAD_DIM, :] = weighted.astype(bf16)
    for c in range(members):
        out_ref[c, :shard, :] = packed_ref[c * shard : (c + 1) * shard, :]
        out_ref[c, shard:, :] = sums.astype(bf16)


def attend(team, cached, mask, gains):
    whole = pl.BlockSpec(memory_space=pltpu.VMEM)
    return pl.pallas_call(
        attend_kernel,
        out_shape=jax.ShapeDtypeStruct(team.shape, bf16),
        in_specs=[whole] * (4 + len(cached)),
        out_specs=whole,
        scratch_shapes=[pltpu.VMEM((TEAM_HEADS * HEAD_DIM, LANES), bf16)],
        compiler_params=pltpu.CompilerParams(vmem_limit_bytes=8 * 1024 * 1024),
    )(team, mask, gains[0][:, None], gains[1][None, :], *cached)


def gathered(block, groups):
    size = len(groups[0])
    spread = jnp.broadcast_to(block[None], (size,) + block.shape)
    spread = lax.all_to_all(spread, "tp", 0, 0, axis_index_groups=groups)
    return spread.reshape((size * block.shape[0],) + block.shape[1:])


def summed_over(block, groups):
    size = len(groups[0])
    parts = block.astype(bf16).reshape((size, block.shape[0] // size) + block.shape[1:])
    parts = lax.all_to_all(parts, "tp", 0, 0, axis_index_groups=groups)
    return jnp.sum(parts.astype(f32), axis=0)


def local(
    in_flight, w_qkv, w_mlp, w_attn_out, w_mlp_out, modulation, qk_gain, context_kv, text_len
):
    tp_count = lax.axis_size("tp")
    tp_index = lax.axis_index("tp")
    rows = in_flight.shape[1]
    tokens = rows * tp_count
    width = w_attn_out.shape[2]
    shard = w_attn_out.shape[1]
    ctx_local = context_kv.shape[2]
    teams = tp_count // TEAM
    team_width = TEAM * shard
    member = tp_index % TEAM
    z_count, x_count = 2 * TEAM, tp_count // (2 * TEAM)
    xs, hs, two = range(x_count), range(z_count // 2), range(2)
    along_z = [[z_count * x + 2 * h + l for l in two for h in hs] for x in xs]
    along_x = [[z_count * x + z for x in xs] for z in range(z_count)]
    far = [[z_count * x + 2 * h + l for h in hs] for x in xs for l in two]
    blocks = [[z_count * x + 2 * h + l for x in xs for l in two] for h in hs]
    inside = [[TEAM * t + m for m in range(TEAM)] for t in range(teams)]
    shift_scale = modulation.reshape(3, 1, width)
    gains = qk_gain[0]
    weight_qkv = w_qkv[0].reshape(3 * shard, width)
    weight_mlp = w_mlp[0]
    weight_attn = w_attn_out[0]
    weight_down = w_mlp_out[0]

    half_team = TEAM // 2
    partner = [
        z + TEAM + half_team if z < half_team else z + half_team if z < TEAM
        else z - half_team if z < TEAM + half_team else z - TEAM - half_team
        for z in range(z_count)
    ]
    x_here, z_here = tp_index // z_count, tp_index % z_count
    z_partner = jnp.where(
        z_here < TEAM,
        z_here + jnp.where(z_here < half_team, TEAM + half_team, half_team),
        z_here - jnp.where(z_here < TEAM + half_team, half_team, TEAM + half_team),
    )
    upper = z_here >= TEAM
    slot = jnp.arange(teams * ctx_local, dtype=jnp.int32)
    own_z = slot < x_count * ctx_local
    source = z_count * ((x_here - slot // ctx_local % x_count) % x_count)
    source = source + jnp.where(own_z, z_here, z_partner)
    position = ctx_local * source + slot % ctx_local
    cached_mask = ((position >= TXT) | (position < text_len[0])).astype(f32)
    cached_mask = jnp.broadcast_to(cached_mask[:, None], (teams * ctx_local, LANES))

    current = in_flight[0]
    block = spread(current, shift_scale, z_count)
    block, flat = lax.optimization_barrier((block, context_kv[0]))
    flat = flat.reshape(2 * ctx_local, width)
    by_x = []
    for step in range(x_count):
        part = lax.dynamic_slice_in_dim(
            flat, (x_here + step) % x_count * 2 * team_width, 2 * team_width, 1
        )
        if step:
            route = [
                (z_count * x + z, z_count * ((x + step) % x_count) + z)
                for x in range(x_count) for z in range(z_count)
            ]
            part = lax.ppermute(part, "tp", route)
        by_x.append(part)
    by_x = jnp.stack(by_x)
    keep = jnp.where(upper, by_x[:, :, team_width:], by_x[:, :, :team_width])
    give = jnp.where(upper, by_x[:, :, :team_width], by_x[:, :, team_width:])

    for tick_number in range(TICKS):
        if tick_number == 0:
            normed = lax.all_to_all(block, "tp", 0, 0, axis_index_groups=along_z)
            normed = normed.reshape(-1, width)
            route = [(z_count * x + z, z_count * x + partner[z]) for x in xs for z in range(z_count)]
            got = [
                lax.ppermute(part, "tp", route)
                for part in (give[: x_count - 1], give[x_count - 1 :])
            ]
            normed = gathered(normed, along_x)
            normed, got[0] = lax.optimization_barrier((normed, got[0]))
            cached = [keep] + got
        else:
            block = spread(current, shift_scale, len(hs))
            normed = lax.all_to_all(block, "tp", 0, 0, axis_index_groups=far)
            normed = gathered(normed.reshape(-1, width), blocks)
        team = project(normed, weight_qkv)
        team = lax.all_to_all(team, "tp", 0, 0, axis_index_groups=inside)
        parts = attend(team, cached, cached_mask, gains)
        parts = lax.all_to_all(parts, "tp", 0, 0, axis_index_groups=inside)
        hidden = jax.nn.gelu(
            lax.dot_general(
                normed, weight_mlp, (((1,), (1,)), ((), ())), preferred_element_type=f32
            ),
            approximate=True,
        ).astype(bf16)
        hidden = lax.optimization_barrier(hidden)
        forward = jnp.dot(hidden, weight_down, preferred_element_type=f32)
        forward = lax.optimization_barrier(forward)
        branch = finish(member[None], parts, weight_attn, forward, shift_scale)
        branch = summed_over(branch, along_x)
        branch = summed_over(branch.reshape(-1, LANES), along_z).reshape(rows, width)
        finished = (current.astype(f32) + branch).astype(bf16)
        current = shifted(finished, "pipe", 1)
    return current[None]


def solution(mesh):
    placed = (
        P("pipe", "tp", None),
        P("pipe", None, "tp", None),
        P("pipe", "tp", None),
        P("pipe", "tp", None),
        P("pipe", "tp", None),
        P("pipe", None, None),
        P("pipe", None, None),
        P("pipe", None, "tp", None),
        P(),
    )
    return jax.shard_map(
        local, mesh=mesh, in_specs=placed, out_specs=P("pipe", "tp", None), check_vma=False
    )
```

```python
import jax
import jax.numpy as jnp
from jax import lax
from jax.experimental import pallas as pl
from jax.experimental.pallas import tpu as pltpu
from jax.sharding import PartitionSpec as P

HEADS = 24
HEAD_DIM = 128
TICKS = 2
TXT = 512
TEAM = 8
TEAM_HEADS = 3
LANES = 128

eps_norm = 1e-06
f32 = jnp.float32
bf16 = jnp.bfloat16


def shifted(block, axis, distance):
    size = lax.axis_size(axis)
    return lax.ppermute(block, axis, [((i - distance) % size, i) for i in range(size)])


def spread_kernel(rows_ref, modulation_ref, out_ref, block_ref):
    x = rows_ref[...].astype(f32)
    centred = x - jnp.mean(x, axis=1, keepdims=True)
    variance = jnp.mean(centred * centred, axis=1, keepdims=True)
    normed = centred * lax.rsqrt(variance + eps_norm)
    normed = normed * (1.0 + modulation_ref[1]) + modulation_ref[0]
    rows, width = x.shape
    pieces = width // LANES
    for r in range(rows):
        for p in range(pieces):
            at = r * pieces + p
            block_ref[at : at + 1, :] = normed[r : r + 1, p * LANES : (p + 1) * LANES]
    block = block_ref[...].astype(bf16)
    for j in range(out_ref.shape[0]):
        out_ref[j] = block


def spread(rows, modulation, receivers):
    whole = pl.BlockSpec(memory_space=pltpu.VMEM)
    lines = rows.shape[0] * rows.shape[1] // LANES
    return pl.pallas_call(
        spread_kernel,
        out_shape=jax.ShapeDtypeStruct((receivers, lines, LANES), bf16),
        in_specs=[whole] * 2,
        out_specs=whole,
        scratch_shapes=[pltpu.VMEM((lines, LANES), f32)],
        compiler_params=pltpu.CompilerParams(vmem_limit_bytes=8 * 1024 * 1024),
    )(rows, modulation)


def finish_kernel(member_ref, parts_ref, weight_ref, forward_ref, modulation_ref, out_ref):
    shard, width = weight_ref.shape
    summed = parts_ref[0].astype(f32)
    for c in range(1, parts_ref.shape[0]):
        summed = summed + parts_ref[c].astype(f32)
    feature = member_ref[0] * shard + lax.broadcasted_iota(jnp.int32, (shard, LANES), 0)
    total = jnp.broadcast_to(summed[shard + TEAM_HEADS - 1][None], (shard, LANES))
    for h in range(TEAM_HEADS - 2, -1, -1):
        total = jnp.where(feature < (h + 1) * HEAD_DIM, summed[shard + h][None], total)
    attention = (summed[:shard] / total).astype(bf16)
    branch = lax.dot_general(
        attention, weight_ref[...], (((0,), (0,)), ((), ())), preferred_element_type=f32
    )
    out_ref[...] = ((branch + forward_ref[...]) * modulation_ref[2]).astype(bf16)


def finish(member, parts, weights, forward, modulation):
    whole = pl.BlockSpec(memory_space=pltpu.VMEM)
    return pl.pallas_call(
        finish_kernel,
        out_shape=jax.ShapeDtypeStruct(forward.shape, bf16),
        in_specs=[pl.BlockSpec(memory_space=pltpu.SMEM)] + [whole] * 4,
        out_specs=whole,
        compiler_params=pltpu.CompilerParams(vmem_limit_bytes=8 * 1024 * 1024),
    )(member, parts, weights, forward, modulation)


def project_kernel(normed_ref, weight_ref, out_ref):
    members = out_ref.shape[0]
    shard = weight_ref.shape[0] // 3
    contract = (((1,), (1,)), ((), ()))
    query = lax.dot_general(
        weight_ref[:shard], normed_ref[...], contract, preferred_element_type=f32
    ).astype(bf16)
    others = lax.dot_general(
        normed_ref[...], weight_ref[shard:], contract, preferred_element_type=f32
    ).astype(bf16)
    for c in range(members):
        out_ref[c, :shard, :] = query
        out_ref[c, shard:, : 2 * shard] = others[16 * c : 16 * c + 16]
        out_ref[c, shard:, 2 * shard :] = jnp.zeros((16, LANES - 2 * shard), bf16)


def project(normed, weights):
    whole = pl.BlockSpec(memory_space=pltpu.VMEM)
    return pl.pallas_call(
        project_kernel,
        out_shape=jax.ShapeDtypeStruct((TEAM, weights.shape[0] // 3 + 16, LANES), bf16),
        in_specs=[whole] * 2,
        out_specs=whole,
        compiler_params=pltpu.CompilerParams(vmem_limit_bytes=8 * 1024 * 1024),
    )(normed, weights)


def attend_kernel(team_ref, mask_ref, gain_q_ref, gain_k_ref, *refs):
    *cached_refs, out_ref, packed_ref = refs
    shard = team_ref.shape[1] - 16
    members = team_ref.shape[0]
    lane = lax.broadcasted_iota(jnp.int32, (16, LANES), 1)
    row = lax.broadcasted_iota(jnp.int32, (16, LANES), 0)
    fresh = [team_ref[c, shard:, :].astype(f32) for c in range(members)]
    features = jnp.concatenate([team_ref[c, :shard, :] for c in range(members)], axis=0)
    open_key = mask_ref[...] > 0.0
    count = sum(r.shape[0] for r in cached_refs)
    half = cached_refs[0].shape[1] // 2
    cached = jnp.concatenate(
        [r[...].reshape(2 * half * r.shape[0], r.shape[2]) for r in cached_refs], axis=0
    )
    sums = jnp.zeros((16, LANES), f32)
    for h in range(TEAM_HEADS):
        query = features[h * HEAD_DIM : (h + 1) * HEAD_DIM].astype(f32)
        scale = lax.rsqrt(jnp.mean(query * query, axis=0, keepdims=True) + eps_norm)
        query = (query * scale * gain_q_ref[...] * HEAD_DIM ** (-0.5)).astype(bf16)
        key = jnp.zeros((16, LANES), f32)
        value = jnp.zeros((16, LANES), f32)
        for c in range(members):
            start = c * shard - h * HEAD_DIM
            if start <= -shard or start >= HEAD_DIM:
                continue
            here = (lane >= start) & (lane < start + shard)
            key = jnp.where(here, pltpu.roll(fresh[c], start % LANES, 1), key)
            value = jnp.where(here, pltpu.roll(fresh[c], (start - shard) % LANES, 1), value)
        scale = lax.rsqrt(jnp.mean(key * key, axis=1, keepdims=True) + eps_norm)
        key = (key * scale * gain_k_ref[...]).astype(bf16)
        both = cached[:, h * HEAD_DIM : (h + 1) * HEAD_DIM]
        scores = jnp.dot(both, query, preferred_element_type=f32)
        scores = scores.reshape(count, 2 * half, LANES)[:, :half].reshape(count * half, LANES)
        probs = jnp.exp(jnp.where(open_key, scores, -1e30))
        at_values = probs.reshape(count, half, LANES)
        at_values = jnp.concatenate([jnp.zeros_like(at_values), at_values], axis=1)
        at_values = at_values.reshape(2 * half * count, LANES)
        fresh_probs = jnp.exp(jnp.dot(key, query, preferred_element_type=f32))
        total = jnp.sum(probs, axis=0, keepdims=True) + jnp.sum(fresh_probs, axis=0, keepdims=True)
        sums = jnp.where(row == h, total, sums)
        contract = (((0,), (0,)), ((), ()))
        weighted = lax.dot_general(
            both, at_values.astype(bf16), contract, preferred_element_type=f32
        ) + lax.dot_general(
            value.astype(bf16), fresh_probs.astype(bf16), contract, preferred_element_type=f32
        )
        packed_ref[h * HEAD_DIM : (h + 1) * HEAD_DIM, :] = weighted.astype(bf16)
    for c in range(members):
        out_ref[c, :shard, :] = packed_ref[c * shard : (c + 1) * shard, :]
        out_ref[c, shard:, :] = sums.astype(bf16)


def attend(team, cached, mask, gains):
    whole = pl.BlockSpec(memory_space=pltpu.VMEM)
    return pl.pallas_call(
        attend_kernel,
        out_shape=jax.ShapeDtypeStruct(team.shape, bf16),
        in_specs=[whole] * (4 + len(cached)),
        out_specs=whole,
        scratch_shapes=[pltpu.VMEM((TEAM_HEADS * HEAD_DIM, LANES), bf16)],
        compiler_params=pltpu.CompilerParams(vmem_limit_bytes=8 * 1024 * 1024),
    )(team, mask, gains[0][:, None], gains[1][None, :], *cached)


def gathered(block, groups):
    size = len(groups[0])
    spread = jnp.broadcast_to(block[None], (size,) + block.shape)
    spread = lax.all_to_all(spread, "tp", 0, 0, axis_index_groups=groups)
    return spread.reshape((size * block.shape[0],) + block.shape[1:])


def summed_over(block, groups):
    size = len(groups[0])
    parts = block.astype(bf16).reshape((size, block.shape[0] // size) + block.shape[1:])
    parts = lax.all_to_all(parts, "tp", 0, 0, axis_index_groups=groups)
    return jnp.sum(parts.astype(f32), axis=0)


def local(
    in_flight, w_qkv, w_mlp, w_attn_out, w_mlp_out, modulation, qk_gain, context_kv, text_len
):
    tp_count = lax.axis_size("tp")
    tp_index = lax.axis_index("tp")
    rows = in_flight.shape[1]
    tokens = rows * tp_count
    width = w_attn_out.shape[2]
    shard = w_attn_out.shape[1]
    ctx_local = context_kv.shape[2]
    teams = tp_count // TEAM
    team_width = TEAM * shard
    member = tp_index % TEAM
    z_count, x_count = 2 * TEAM, tp_count // (2 * TEAM)
    xs, hs, two = range(x_count), range(z_count // 2), range(2)
    along_z = [[z_count * x + 2 * h + l for l in two for h in hs] for x in xs]
    along_x = [[z_count * x + z for x in xs] for z in range(z_count)]
    far = [[z_count * x + 2 * h + l for h in hs] for x in xs for l in two]
    blocks = [[z_count * x + 2 * h + l for x in xs for l in two] for h in hs]
    inside = [[TEAM * t + m for m in range(TEAM)] for t in range(teams)]
    shift_scale = modulation.reshape(3, 1, width)
    gains = qk_gain[0]
    weight_qkv = w_qkv[0].reshape(3 * shard, width)
    weight_mlp = w_mlp[0]
    weight_attn = w_attn_out[0]
    weight_down = w_mlp_out[0]

    half_team = TEAM // 2
    partner = [
        z + TEAM + half_team if z < half_team else z + half_team if z < TEAM
        else z - half_team if z < TEAM + half_team else z - TEAM - half_team
        for z in range(z_count)
    ]
    x_here, z_here = tp_index // z_count, tp_index % z_count
    z_partner = jnp.where(
        z_here < TEAM,
        z_here + jnp.where(z_here < half_team, TEAM + half_team, half_team),
        z_here - jnp.where(z_here < TEAM + half_team, half_team, TEAM + half_team),
    )
    upper = z_here >= TEAM
    slot = jnp.arange(teams * ctx_local, dtype=jnp.int32)
    own_z = slot < x_count * ctx_local
    source = z_count * ((x_here - slot // ctx_local % x_count) % x_count)
    source = source + jnp.where(own_z, z_here, z_partner)
    position = ctx_local * source + slot % ctx_local
    cached_mask = ((position >= TXT) | (position < text_len[0])).astype(f32)
    cached_mask = jnp.broadcast_to(cached_mask[:, None], (teams * ctx_local, LANES))

    current = in_flight[0]
    block = spread(current, shift_scale, z_count)
    block, flat = lax.optimization_barrier((block, context_kv[0]))
    flat = flat.reshape(2 * ctx_local, width)
    by_x = []
    for step in range(x_count):
        part = lax.dynamic_slice_in_dim(
            flat, (x_here + step) % x_count * 2 * team_width, 2 * team_width, 1
        )
        if step:
            route = [
                (z_count * x + z, z_count * ((x + step) % x_count) + z)
                for x in range(x_count) for z in range(z_count)
            ]
            part = lax.ppermute(part, "tp", route)
        by_x.append(part)
    by_x = jnp.stack(by_x)
    keep = jnp.where(upper, by_x[:, :, team_width:], by_x[:, :, :team_width])
    give = jnp.where(upper, by_x[:, :, :team_width], by_x[:, :, team_width:])

    for tick_number in range(TICKS):
        if tick_number == 0:
            normed = lax.all_to_all(block, "tp", 0, 0, axis_index_groups=along_z)
            normed = normed.reshape(-1, width)
            route = [(z_count * x + z, z_count * x + partner[z]) for x in xs for z in range(z_count)]
            got = [
                lax.ppermute(part, "tp", route)
                for part in (give[: x_count // 2], give[x_count // 2 :])
            ]
            normed = gathered(normed, along_x)
            normed, got[0] = lax.optimization_barrier((normed, got[0]))
            cached = [keep] + got
        else:
            block = spread(current, shift_scale, len(hs))
            normed = lax.all_to_all(block, "tp", 0, 0, axis_index_groups=far)
            normed = gathered(normed.reshape(-1, width), blocks)
        team = project(normed, weight_qkv)
        team = lax.all_to_all(team, "tp", 0, 0, axis_index_groups=inside)
        parts = attend(team, cached, cached_mask, gains)
        parts = lax.all_to_all(parts, "tp", 0, 0, axis_index_groups=inside)
        hidden = jax.nn.gelu(
            lax.dot_general(
                normed, weight_mlp, (((1,), (1,)), ((), ())), preferred_element_type=f32
            ),
            approximate=True,
        ).astype(bf16)
        hidden = lax.optimization_barrier(hidden)
        forward = jnp.dot(hidden, weight_down, preferred_element_type=f32)
        forward = lax.optimization_barrier(forward)
        branch = finish(member[None], parts, weight_attn, forward, shift_scale)
        branch = summed_over(branch, along_x)
        branch = summed_over(branch.reshape(-1, LANES), along_z).reshape(rows, width)
        finished = (current.astype(f32) + branch).astype(bf16)
        current = shifted(finished, "pipe", 1)
    return current[None]


def solution(mesh):
    placed = (
        P("pipe", "tp", None),
        P("pipe", None, "tp", None),
        P("pipe", "tp", None),
        P("pipe", "tp", None),
        P("pipe", "tp", None),
        P("pipe", None, None),
        P("pipe", None, None),
        P("pipe", None, "tp", None),
        P(),
    )
    return jax.shard_map(
        local, mesh=mesh, in_specs=placed, out_specs=P("pipe", "tp", None), check_vma=False
    )
```
